32 devices in a mesh: seq: 8 (over z, x), batch: 4 (over y, core).
Axes of the slice: x: 2, y: 2, z: 4, core: 2. Of those that a mesh axis runs over, the one named last changes fastest.
Arguments:
- tokens: bfloat16 [4, 2048, 1024], P('batch', 'seq'), may hold values from -6 to 6
- qkv_weight: bfloat16 [2, 1024, 3072], P(None, ('seq', 'batch')), may hold values from -0.1875 to 0.1875
- conv_weight: bfloat16 [2, 4, 3072], P(None, None, ('seq', 'batch')), may hold values from -3 to 3
- beta_weight: bfloat16 [2, 1024, 8], P(None, ('seq', 'batch')), may hold values from -0.1875 to 0.1875
- beta_bias: bfloat16 [2, 8], replicated, may hold values from -6 to -2
- head_gain: bfloat16 [2, 128], replicated, may hold values from 0.5 to 1.5
- out_weight: bfloat16 [2, 1024, 1024], P(None, ('seq', 'batch')), may hold values from -0.1875 to 0.1875
- mixer_gain: bfloat16 [2, 1024], P(None, ('seq', 'batch')), may hold values from 0.5 to 1.5
- mlp_gain: bfloat16 [2, 1024], P(None, ('seq', 'batch')), may hold values from 0.5 to 1.5
- gate_weight: bfloat16 [2, 1024, 2816], P(None, ('seq', 'batch')), may hold values from -0.1875 to 0.1875
- up_weight: bfloat16 [2, 1024, 2816], P(None, ('seq', 'batch')), may hold values from -0.1875 to 0.1875
- down_weight: bfloat16 [2, 2816, 1024], P(None, ('seq', 'batch')), may hold values from -0.109375 to 0.109375
- lengths: int32 [4, 3], P('batch'), may hold values from 64 to 1920, as said below
- cotangent: bfloat16 [4, 2048, 1024], P('batch', 'seq'), may hold values from -6 to 6
Outputs:
- mixed: bfloat16 [4, 2048, 1024], P('batch', 'seq')
- d_tokens: float32 [4, 2048, 1024], P('batch', 'seq')
- d_qkv: float32 [2, 1024, 3072], P(None, ('seq', 'batch'))
- d_conv: float32 [2, 4, 3072], P(None, None, ('seq', 'batch'))
- d_beta_weight: float32 [2, 1024, 8], P(None, ('seq', 'batch'))
- d_beta_bias: float32 [2, 8], replicated
- d_head_gain: float32 [2, 128], replicated
- d_out: float32 [2, 1024, 1024], P(None, ('seq', 'batch'))
- d_mixer_gain: float32 [2, 1024], P(None, ('seq', 'batch'))
- d_mlp_gain: float32 [2, 1024], P(None, ('seq', 'batch'))
- d_gate: float32 [2, 1024, 2816], P(None, ('seq', 'batch'))
- d_up: float32 [2, 1024, 2816], P(None, ('seq', 'batch'))
- d_down: float32 [2, 2816, 1024], P(None, ('seq', 'batch'))
The draws below stay inside these ranges and needn't reach their ends.
Inputs may be any that keep to these rules, and one draw needn't show every extreme that they name: Every length is a multiple of 64; the lengths of a group sum to 2048; the second sequence of each group begins within the first 256 tokens and ends within the last 256.
All inputs are finite; a program needn't handle non-finite values.
Results may differ from the reference program's by a relative error of at most 0.035.
Values may be sent and summed in bfloat16 or wider, within the bound.
A program may use at most 320 MiB of HBM per device.

```python
import jax
import jax.numpy as jnp
from jax import lax

D = 1024
HEADS = 8
HEAD_DIM = 128
FF = 2816
CONV = 4
STRETCH = 64
LAYERS = 2
TOK_DEV = 256
GROUP_TOK = 2048
GROUPS = 4


def draw_lengths(key, part):
    key = jax.random.fold_in(key, 7)
    per_device = TOK_DEV // STRETCH
    head_key, tail_key = jax.random.split(key)
    leading = jax.random.randint(head_key, (GROUPS,), 1, per_device)
    trailing = jax.random.randint(tail_key, (GROUPS,), 1, per_device)
    first_row = jnp.arange(GROUPS) == 0
    leading = jnp.where(first_row, 1, leading)
    trailing = jnp.where(first_row, 1, trailing)
    middle = GROUP_TOK // STRETCH - leading - trailing
    return (jnp.stack([leading, middle, trailing], axis=1) * STRETCH).astype(jnp.int32)


def block_scale(key, extent, shards, least, largest):
    loudness = 1.0
    for position, shards_of in shards:
        draws = jax.random.uniform(jax.random.fold_in(jax.random.fold_in(key, 6), position), (shards_of,), jnp.float32, least / len(shards), largest / len(shards))
        loudness = loudness * jnp.repeat(jnp.exp(draws), extent[position] // shards_of).reshape((-1,) + (1,) * (len(extent) - 1 - position))
    return loudness


def bell_draw(key, shape, scale, reach, cuts=(), kind=jnp.bfloat16):
    loudness = block_scale(key, shape, cuts, -0.22, 0.18) if cuts else 1.0
    array = jax.random.normal(key, shape, jnp.float32) * scale * loudness
    return jnp.minimum(jnp.maximum(array, -reach), reach).astype(kind)


def setup_inputs(seed: int = 0) -> dict:
    splits = jax.random.split(jax.random.key(seed), 15)
    tokens = bell_draw(splits[0], (GROUPS, GROUP_TOK, D), 1.0, 6.0, ((0, 4), (1, 8)))
    qkv_weight = bell_draw(splits[1], (LAYERS, D, 3 * D), D ** -0.5, 0.1875, ((1, 32),))
    conv_weight = bell_draw(splits[2], (LAYERS, CONV, 3 * D), 0.5, 3.0, ((2, 32),))
    beta_weight = bell_draw(splits[3], (LAYERS, D, HEADS), D ** -0.5, 0.1875, ((1, 32),))
    beta_bias = jnp.clip(jax.random.uniform(splits[4], (LAYERS, HEADS), jnp.float32, -6.0, -2.0), -6.0, -2.0).astype(jnp.bfloat16)
    head_gain = jnp.clip(1.0 + 0.1 * jax.random.normal(splits[5], (LAYERS, HEAD_DIM), jnp.float32), 0.5, 1.5).astype(jnp.bfloat16)
    out_weight = bell_draw(splits[6], (LAYERS, D, D), D ** -0.5, 0.1875, ((1, 32),))
    mixer_gain = jnp.clip(1.0 + 0.1 * jax.random.normal(splits[7], (LAYERS, D), jnp.float32), 0.5, 1.5).astype(jnp.bfloat16)
    mlp_gain = jnp.clip(1.0 + 0.1 * jax.random.normal(splits[8], (LAYERS, D), jnp.float32), 0.5, 1.5).astype(jnp.bfloat16)
    gate_weight = bell_draw(splits[9], (LAYERS, D, FF), D ** -0.5, 0.1875, ((1, 32),))
    up_weight = bell_draw(splits[10], (LAYERS, D, FF), D ** -0.5, 0.1875, ((1, 32),))
    down_weight = bell_draw(splits[11], (LAYERS, FF, D), FF ** -0.5, 0.109375, ((1, 32),))
    lengths = draw_lengths(jax.random.fold_in(splits[14], 71), 0)
    cotangent = bell_draw(splits[13], (GROUPS, GROUP_TOK, D), 1.0, 6.0, ((0, 4), (1, 8)))
    return dict(tokens=tokens, qkv_weight=qkv_weight, conv_weight=conv_weight, beta_weight=beta_weight, beta_bias=beta_bias, head_gain=head_gain, out_weight=out_weight, mixer_gain=mixer_gain, mlp_gain=mlp_gain, gate_weight=gate_weight, up_weight=up_weight, down_weight=down_weight, lengths=lengths, cotangent=cotangent)


EPSILON = 1e-06
PRECISE = lax.Precision.HIGHEST

@jax.custom_vjp
def low(v):
    return lax.optimization_barrier(v.astype(jnp.bfloat16)).astype(jnp.float32)

@jax.custom_vjp
def low_back(v):
    return v

def low_keep(v):
    return (low(v), None)

def low_pass(kept, grad):
    return (grad,)

def back_keep(v):
    return (v, None)

def back_low(kept, grad):
    return (low(grad),)
low.defvjp(low_keep, low_pass)
low_back.defvjp(back_keep, back_low)

def matmul(left, right):
    return jnp.dot(left, right, precision=PRECISE)

def rms_scale(values, gain):
    return values * lax.rsqrt(lax.optimization_barrier(jnp.mean(values * values, axis=-1, keepdims=True)) + EPSILON) * gain

def unit_rows(values):
    return values * lax.rsqrt(lax.optimization_barrier(jnp.sum(values * values, axis=-1, keepdims=True)) + EPSILON)

def to_blocks(values, count):
    return jnp.swapaxes(values.reshape(count, STRETCH, HEADS, -1), 1, 2)

def from_blocks(values):
    count = values.shape[0]
    return jnp.swapaxes(values, 1, 2).reshape(count * STRETCH, HEADS, -1)

def stretch_prepare(keys_t, values_t, betas_t):
    width = keys_t.shape[2]
    size = keys_t.shape[3]
    scaled = keys_t * betas_t
    gram = jnp.einsum('nhid,nhjd->nhij', scaled, keys_t, precision=PRECISE)
    strict = jnp.tril(jnp.ones((width, width), jnp.float32), -1)
    system = jnp.eye(width, dtype=jnp.float32) + gram * strict
    right_side = jnp.concatenate([scaled, values_t * betas_t], axis=-1)
    solved = lax.linalg.triangular_solve(system, right_side, left_side=True, lower=True, unit_diagonal=True)
    return (solved[..., :size], solved[..., size:])

def stretch_outputs(state, queries_t, keys_t, w_mat, u_mat, keep):
    width = queries_t.shape[2]
    causal = jnp.tril(jnp.ones((width, width), jnp.float32))

    def advance(current, item):
        query_block, key_block, w_block, u_block, flag = item
        current = current * flag
        fresh = u_block - jnp.einsum('hce,hef->hcf', w_block, current, precision=PRECISE)
        scores = jnp.einsum('hcd,hed->hce', query_block, key_block, precision=PRECISE) * causal
        result = jnp.einsum('hcd,hdf->hcf', query_block, current, precision=PRECISE)
        result = result + jnp.einsum('hce,hef->hcf', scores, fresh, precision=PRECISE)
        current = current + jnp.einsum('hcd,hcf->hdf', key_block, fresh, precision=PRECISE)
        return (current, result)
    final_state, results = lax.scan(jax.checkpoint(advance), state, (queries_t, keys_t, w_mat, u_mat, keep))
    return results

def mixer_inputs(padded, conv_taps, logits, bias, positions_in):
    total = logits.shape[0]
    mixed_rows = jnp.zeros((total, padded.shape[1]), jnp.float32)
    for tap_index in range(CONV):
        offset = CONV - 1 - tap_index
        allowed = (positions_in >= offset).astype(jnp.float32)[:, None]
        mixed_rows = mixed_rows + conv_taps[tap_index] * padded[tap_index:tap_index + total] * allowed
    activated = jax.nn.silu(mixed_rows)
    width = HEADS * HEAD_DIM
    queries = unit_rows(activated[:, :width].reshape(total, HEADS, HEAD_DIM)) * HEAD_DIM ** (-0.5)
    keys_all = unit_rows(activated[:, width:2 * width].reshape(total, HEADS, HEAD_DIM))
    values_all = activated[:, 2 * width:].reshape(total, HEADS, HEAD_DIM)
    betas = jax.nn.sigmoid(logits + bias)
    return (queries, keys_all, values_all, betas)

def positions_of(seq_lengths, total):
    starts = jnp.cumsum(seq_lengths) - seq_lengths
    index = jnp.arange(total, dtype=jnp.int32)
    begin = lax.optimization_barrier(jnp.max(jnp.where(starts[None, :] <= index[:, None], starts[None, :], 0), axis=1))
    return (index - begin).astype(jnp.int32)

def delta_rule(queries, keys_all, values_all, betas, keep):
    count = queries.shape[0] // STRETCH
    queries_t = to_blocks(queries, count)
    keys_t = to_blocks(keys_all, count)
    values_t = to_blocks(values_all, count)
    betas_t = to_blocks(betas, count)
    w_mat, u_mat = stretch_prepare(keys_t, values_t, betas_t)
    start_state = jnp.zeros((HEADS, HEAD_DIM, HEAD_DIM), jnp.float32)
    return from_blocks(stretch_outputs(start_state, queries_t, keys_t, w_mat, u_mat, keep))

def block_forward(hidden_in, params, positions_in, keep):
    w_qkv, w_conv, w_beta, bias, head_scale, w_out, gain_mix, gain_mlp, w_gate, w_up, w_down = params
    total = hidden_in.shape[0]
    normed_in = low(rms_scale(hidden_in, gain_mix))
    projected = low_back(matmul(normed_in, w_qkv))
    logits = low_back(matmul(normed_in, w_beta))
    padded = jnp.pad(projected, ((CONV - 1, 0), (0, 0)))
    queries, keys_all, values_all, betas = mixer_inputs(padded, w_conv, logits, bias, positions_in)
    heads_out = delta_rule(queries, keys_all, values_all, betas, keep)
    normed_heads = low(rms_scale(heads_out, head_scale).reshape(total, D))
    after_mixer = hidden_in + low_back(matmul(normed_heads, w_out))
    normed_mlp = low(rms_scale(after_mixer, gain_mlp))
    gate = low_back(matmul(normed_mlp, w_gate))
    up_rows = low_back(matmul(normed_mlp, w_up))
    hidden_mid = low(jax.nn.silu(gate) * up_rows)
    return after_mixer + low_back(matmul(hidden_mid, w_down))

def reference(tokens, qkv_weight, conv_weight, beta_weight, beta_bias, head_gain, out_weight, mixer_gain, mlp_gain, gate_weight, up_weight, down_weight, lengths, cotangent):
    params = tuple((item.astype(jnp.float32) for item in (qkv_weight, conv_weight, beta_weight, beta_bias, head_gain, out_weight, mixer_gain, mlp_gain, gate_weight, up_weight, down_weight)))
    total = tokens.shape[1]

    def forward(inputs, weights):

        def one_group(item):
            stream, seq_lengths = item
            positions_in = positions_of(seq_lengths, total)
            keep = (positions_in[::STRETCH] != 0).astype(jnp.float32)
            for layer_index in range(LAYERS):
                stream = block_forward(stream, tuple((weight[layer_index] for weight in weights)), positions_in, keep)
            return stream
        return lax.map(one_group, (inputs, lengths))
    result, pullback = jax.vjp(forward, tokens.astype(jnp.float32), params)
    d_inputs, d_weights = pullback(cotangent.astype(jnp.float32))
    return (result.astype(jnp.bfloat16), d_inputs) + tuple(d_weights)
```

```python
import functools

import jax
import jax.numpy as jnp
from jax import lax
from jax.experimental import pallas as pl
from jax.experimental.pallas import tpu as pltpu
from jax.sharding import PartitionSpec as P

D = 1024
HEADS = 8
HEAD_DIM = 128
CONV = 4
STRETCH = 64
LAYERS = 2
EPSILON = 1e-06
BF = jnp.bfloat16
F32 = jnp.float32
BOTH = ("seq", "batch")
VMEM_BYTES = 56 * 1024 * 1024


def dot(a, b):
    return lax.dot_general(a.astype(BF), b.astype(BF), (((1,), (0,)), ((), ())), preferred_element_type=F32)


def dot_t(a, b):
    return lax.dot_general(a.astype(BF), b.astype(BF), (((1,), (1,)), ((), ())), preferred_element_type=F32)


def t_dot(a, b):
    return lax.dot_general(a.astype(BF), b.astype(BF), (((0,), (0,)), ((), ())), preferred_element_type=F32)


def rms_scale(values, gain):
    return values * lax.rsqrt(jnp.mean(values * values, axis=-1, keepdims=True) + EPSILON) * gain


def rms_back(values, gain, grad):
    r = lax.rsqrt(jnp.mean(values * values, axis=-1, keepdims=True) + EPSILON)
    unit = values * r
    scaled = grad * gain
    back = r * (scaled - unit * jnp.mean(scaled * unit, axis=-1, keepdims=True))
    return back, grad * unit


def masks(rows):
    i = lax.broadcasted_iota(jnp.int32, (rows, rows), 0)
    j = lax.broadcasted_iota(jnp.int32, (rows, rows), 1)
    same = (i // STRETCH) == (j // STRETCH)
    strict = same & (i > j)
    causal = same & (i >= j)
    return i, j, strict, causal


def conv_rows(rows, before, taps, pos):
    total = rows.shape[0]
    padded = jnp.concatenate([before, rows], axis=0)
    acc = taps[CONV - 1 : CONV] * rows
    for tap in range(CONV - 1):
        offset = CONV - 1 - tap
        shifted = padded[8 - offset : 8 - offset + total]
        acc = acc + taps[tap : tap + 1] * jnp.where(pos >= offset, shifted, 0.0)
    return acc, padded


def unit_rows(values):
    return values * lax.rsqrt(jnp.sum(values * values, axis=-1, keepdims=True) + EPSILON)


def columns(ref, start):
    return ref[:, pl.ds(pl.multiple_of(start, HEAD_DIM), HEAD_DIM)]


def head_column(ref, head):
    values = ref[...]
    lane = lax.broadcasted_iota(jnp.int32, values.shape, 1)
    return jnp.sum(jnp.where(lane == head, values, 0.0), axis=1, keepdims=True)


def inverse_less_one(lower, i, j):
    near = (i // 16) == (j // 16)
    base = jnp.where(near, lower, 0.0)
    r = -base
    power = base
    for _ in range(3):
        power = dot(power, power)
        r = r + power + dot(r, power)
    for width in (32, 64):
        step = ((i // width) == (j // width)) & ((i // (width // 2)) != (j // (width // 2)))
        m = jnp.where(step, lower, 0.0)
        y = m + dot(r, m)
        r = r - y - dot(y, r)
    return r


def local_kernel(keep_ref, pos_ref, beta_ref, proj_ref, before_ref, taps_ref, o_ref, eff_ref, tot_ref, inv_ref, st_ref):
    rows = proj_ref.shape[0]
    i, j, strict, causal = masks(rows)
    pos = pos_ref[...]
    per = tot_ref.shape[0]
    for g in range(per):
        head = pl.program_id(0) * per + g
        parts = []
        for third in range(3):
            start = third * D + head * HEAD_DIM
            acc, _ = conv_rows(columns(proj_ref, start), columns(before_ref, start).astype(F32)[8:], columns(taps_ref, start).astype(F32), pos)
            parts.append(acc * jax.nn.sigmoid(acc))
        q = (unit_rows(parts[0]) * HEAD_DIM ** (-0.5)).astype(BF)
        k32 = unit_rows(parts[1])
        k = k32.astype(BF)
        beta = head_column(beta_ref, head)
        lower = jnp.where(strict, beta * dot_t(k, k), 0.0)
        r = inverse_less_one(lower, i, j)
        inv = r.astype(BF)
        inv_ref[g] = inv
        x = jnp.concatenate([beta * k32, beta * parts[2]], axis=1)
        wu = x + dot(inv, x)
        w = wu[:, :HEAD_DIM].astype(BF)
        u = wu[:, HEAD_DIM:]
        scores = jnp.where(causal, dot_t(q, k), 0.0).astype(BF)
        ii = lax.broadcasted_iota(jnp.int32, (HEAD_DIM, 2 * HEAD_DIM), 0)
        jj = lax.broadcasted_iota(jnp.int32, (HEAD_DIM, 2 * HEAD_DIM), 1)
        state = jnp.where(ii + HEAD_DIM == jj, 1.0, 0.0)
        for c in range(rows // STRETCH):
            s = slice(c * STRETCH, (c + 1) * STRETCH)
            state = state * keep_ref[c]
            low = state.astype(BF)
            st_ref[g, c] = low
            both = dot(jnp.concatenate([w[s], q[s]], axis=0), low)
            fresh = -both[:STRETCH]
            fresh = jnp.concatenate([fresh[:, :HEAD_DIM] + u[s], fresh[:, HEAD_DIM:]], axis=1).astype(BF)
            out = both[STRETCH:] + dot(scores[s, s], fresh)
            state = state + t_dot(k[s], fresh)
            o_ref[s, g * HEAD_DIM : (g + 1) * HEAD_DIM] = out[:, :HEAD_DIM]
            eff_ref[s, g * HEAD_DIM : (g + 1) * HEAD_DIM] = out[:, HEAD_DIM:].astype(BF)
        tot_ref[g] = state


def full(shape):
    return pl.BlockSpec(shape, lambda h: (0,) * len(shape))


def local_call(keep, pos, beta, proj, before, taps):
    rows = proj.shape[0]
    count = rows // STRETCH
    per = 2
    wide = per * HEAD_DIM
    return pl.pallas_call(
        local_kernel,
        grid=(HEADS // per,),
        in_specs=[
            pl.BlockSpec(memory_space=pltpu.SMEM),
            full((rows, 1)),
            full((rows, HEADS)),
            full((rows, 3 * D)),
            full((16, 3 * D)),
            full((CONV, 3 * D)),
        ],
        out_specs=[
            pl.BlockSpec((rows, wide), lambda h: (0, h)),
            pl.BlockSpec((rows, wide), lambda h: (0, h)),
            pl.BlockSpec((per, HEAD_DIM, 2 * HEAD_DIM), lambda h: (h, 0, 0)),
            pl.BlockSpec((per, rows, rows), lambda h: (h, 0, 0)),
            pl.BlockSpec((per, count, HEAD_DIM, 2 * HEAD_DIM), lambda h: (h, 0, 0, 0)),
        ],
        out_shape=[
            jax.ShapeDtypeStruct((rows, D), F32),
            jax.ShapeDtypeStruct((rows, D), BF),
            jax.ShapeDtypeStruct((HEADS, HEAD_DIM, 2 * HEAD_DIM), F32),
            jax.ShapeDtypeStruct((HEADS, rows, rows), BF),
            jax.ShapeDtypeStruct((HEADS, count, HEAD_DIM, 2 * HEAD_DIM), BF),
        ],
        compiler_params=pltpu.CompilerParams(vmem_limit_bytes=VMEM_BYTES),
        cost_estimate=pl.CostEstimate(flops=8 * 16 * 2 * 256**3, bytes_accessed=10 * 2**20, transcendentals=0),
        name="delta_local",
    )(keep, pos, beta, proj, before, taps)


def back_kernel(
    keep_ref, pos_ref, beta_ref, proj_ref, before_ref, taps_ref, inv_ref, st_ref, sin_ref, ds_ref, do_ref,
    dproj_ref, tail_ref, dbefore_ref, dtaps_ref, dbeta_ref,
):
    rows = proj_ref.shape[0]
    count = rows // STRETCH
    i, j, strict, causal = masks(rows)
    pos = pos_ref[...]
    per = inv_ref.shape[0]

    @pl.when(pl.program_id(0) == 0)
    def _():
        dbeta_ref[...] = jnp.zeros_like(dbeta_ref)

    for g in range(per):
        head = pl.program_id(0) * per + g
        raw, act, padded = [], [], []
        for third in range(3):
            start = third * D + head * HEAD_DIM
            acc, pad = conv_rows(columns(proj_ref, start), columns(before_ref, start).astype(F32)[8:], columns(taps_ref, start).astype(F32), pos)
            raw.append(acc)
            act.append(acc * jax.nn.sigmoid(acc))
            padded.append(pad)
        rq = lax.rsqrt(jnp.sum(act[0] * act[0], axis=-1, keepdims=True) + EPSILON)
        rk = lax.rsqrt(jnp.sum(act[1] * act[1], axis=-1, keepdims=True) + EPSILON)
        q = (act[0] * rq * HEAD_DIM ** (-0.5)).astype(BF)
        k32 = act[1] * rk
        k = k32.astype(BF)
        beta = head_column(beta_ref, head)
        gram = jnp.where(strict, dot_t(k, k), 0.0)
        inv = inv_ref[g]
        x = jnp.concatenate([beta * k32, beta * act[2]], axis=1)
        wu = x + dot(inv, x)
        w = wu[:, :HEAD_DIM].astype(BF)
        u = wu[:, HEAD_DIM:]
        scores = jnp.where(causal, dot_t(q, k), 0.0).astype(BF)
        dout = do_ref[:, g * HEAD_DIM : (g + 1) * HEAD_DIM]
        sin = sin_ref[g].astype(BF)
        states, fresh = [], []
        for c in range(count):
            s = slice(c * STRETCH, (c + 1) * STRETCH)
            packed = st_ref[g, c]
            state = (packed[:, :HEAD_DIM].astype(F32) + dot(packed[:, HEAD_DIM:], sin)).astype(BF)
            states.append(state)
            fresh.append((u[s] - dot(w[s], state)).astype(BF))
        fresh_all = jnp.concatenate(fresh, axis=0)
        dscores = jnp.where(causal, dot_t(dout, fresh_all), 0.0).astype(BF)
        dfresh0 = t_dot(scores, dout)
        ds = ds_ref[g]
        dfresh = [None] * count
        dk_state = [None] * count
        dq_state = [None] * count
        dw = [None] * count
        for c in reversed(range(count)):
            s = slice(c * STRETCH, (c + 1) * STRETCH)
            low = ds.astype(BF)
            part = dfresh0[s] + dot(k[s], low)
            dfresh[c] = part
            part_low = part.astype(BF)
            dk_state[c] = dot_t(fresh[c], low)
            both = dot_t(jnp.concatenate([dout[s], part_low], axis=0), states[c])
            dq_state[c] = both[:STRETCH]
            dw[c] = -both[STRETCH:]
            ds = (ds + t_dot(q[s], dout[s]) - t_dot(w[s], part_low)) * keep_ref[c]
        dfresh_all = jnp.concatenate(dfresh, axis=0)
        dq = jnp.concatenate(dq_state, axis=0) + dot(dscores, k)
        dk = jnp.concatenate(dk_state, axis=0) + t_dot(dscores, q)
        dwu = jnp.concatenate([jnp.concatenate(dw, axis=0), dfresh_all], axis=1)
        dx = dwu + t_dot(inv, dwu)
        dlower = jnp.where(strict, -dot_t(dx, wu), 0.0)
        dbeta = jnp.sum(dlower * gram, axis=1, keepdims=True)
        dxk = dx[:, :HEAD_DIM]
        dxv = dx[:, HEAD_DIM:]
        dbeta = dbeta + jnp.sum(dxk * k32 + dxv * act[2], axis=1, keepdims=True)
        dgram = (dlower * beta).astype(BF)
        dk = dk + dot(dgram, k) + t_dot(dgram, k) + beta * dxk
        dv = beta * dxv
        lane = lax.broadcasted_iota(jnp.int32, (rows, HEADS), 1)
        dbeta_ref[...] += jnp.where(lane == head, dbeta * beta * (1.0 - beta), 0.0)
        dq = dq * HEAD_DIM ** (-0.5)
        grads = (
            rq * (dq - act[0] * (rq * rq * jnp.sum(act[0] * dq, axis=-1, keepdims=True))),
            rk * (dk - k32 * jnp.sum(k32 * dk, axis=-1, keepdims=True)),
            dv,
        )
        for third in range(3):
            start = third * D + head * HEAD_DIM
            spot = pl.ds(pl.multiple_of(start, HEAD_DIM), HEAD_DIM)
            sig = jax.nn.sigmoid(raw[third])
            dmix = grads[third] * (sig + act[third] * (1.0 - sig))
            taps = columns(taps_ref, start).astype(F32)
            dpad = jnp.concatenate([jnp.zeros((8, HEAD_DIM), F32), taps[CONV - 1 : CONV] * dmix], axis=0)
            dtap = [None] * CONV
            dtap[CONV - 1] = jnp.sum(dmix * padded[third][8:], axis=0, keepdims=True)
            for tap in range(CONV - 1):
                offset = CONV - 1 - tap
                kept = jnp.where(pos >= offset, dmix, 0.0)
                dtap[tap] = jnp.sum(kept * padded[third][8 - offset : 8 - offset + rows], axis=0, keepdims=True)
                scaled = taps[tap : tap + 1] * kept
                dpad = dpad + jnp.concatenate(
                    [jnp.zeros((8 - offset, HEAD_DIM), F32), scaled, jnp.zeros((offset, HEAD_DIM), F32)], axis=0
                )
            dproj_ref[:, spot] = dpad[8:].astype(BF)
            tail_ref[:, spot] = dpad[rows - 8 :]
            dbefore_ref[:, spot] = jnp.concatenate([jnp.zeros((8, HEAD_DIM), F32), dpad[:8]], axis=0).astype(BF)
            dtaps_ref[:, spot] = jnp.concatenate(dtap, axis=0)


def back_call(keep, pos, beta, proj, before, taps, inv, st, sin, ds, do):
    rows = proj.shape[0]
    count = rows // STRETCH
    per = 2
    wide = per * HEAD_DIM
    return pl.pallas_call(
        back_kernel,
        grid=(HEADS // per,),
        in_specs=[
            pl.BlockSpec(memory_space=pltpu.SMEM),
            full((rows, 1)),
            full((rows, HEADS)),
            full((rows, 3 * D)),
            full((16, 3 * D)),
            full((CONV, 3 * D)),
            pl.BlockSpec((per, rows, rows), lambda h: (h, 0, 0)),
            pl.BlockSpec((per, count, HEAD_DIM, 2 * HEAD_DIM), lambda h: (h, 0, 0, 0)),
            pl.BlockSpec((per, HEAD_DIM, HEAD_DIM), lambda h: (h, 0, 0)),
            pl.BlockSpec((per, HEAD_DIM, HEAD_DIM), lambda h: (h, 0, 0)),
            pl.BlockSpec((rows, wide), lambda h: (0, h)),
        ],
        out_specs=[full((rows, 3 * D)), full((16, 3 * D)), full((16, 3 * D)), full((CONV, 3 * D)), full((rows, HEADS))],
        out_shape=[
            jax.ShapeDtypeStruct((rows, 3 * D), BF),
            jax.ShapeDtypeStruct((16, 3 * D), F32),
            jax.ShapeDtypeStruct((16, 3 * D), BF),
            jax.ShapeDtypeStruct((CONV, 3 * D), F32),
            jax.ShapeDtypeStruct((rows, HEADS), F32),
        ],
        compiler_params=pltpu.CompilerParams(vmem_limit_bytes=VMEM_BYTES),
        cost_estimate=pl.CostEstimate(flops=8 * 20 * 2 * 256**3, bytes_accessed=10 * 2**20, transcendentals=0),
        name="delta_back",
    )(keep, pos, beta, proj, before, taps, inv, st, sin, ds, do)


def shift(values, steps):
    count = lax.axis_size("seq")
    first, last = max(0, -steps), min(count, count - steps)
    return lax.ppermute(values, "seq", [(n, n + steps) for n in range(first, last)])


def chain(tot_b, tot_a, steps):
    peers = lax.axis_size("seq")
    state = jnp.zeros(tot_b.shape, F32)
    low_a = tot_a.astype(BF)
    for turn in range(peers - 1):
        if turn == 0:
            new = tot_b
        else:
            new = tot_b + jnp.einsum("hde,hef->hdf", low_a, state.astype(BF), preferred_element_type=F32)
        state = shift(new.astype(BF), steps).astype(F32)
    return state


def swap_seq(values, bit):
    return lax.ppermute(values, "seq", [(n, n ^ bit) for n in range(8)])


def swap_batch(values, bit):
    return lax.ppermute(values, "batch", [(n, n ^ bit) for n in range(4)])


def swap_x(values):
    return swap_seq(values, 1)


def swap_y(values):
    return swap_batch(values, 2)


def swap_c(values):
    return swap_batch(values, 1)


def shift_z(values, steps):
    return lax.ppermute(values, "seq", [(n, (n + 2 * steps) % 8) for n in range(8)])


def place_xy():
    seq, batch = lax.axis_index("seq"), lax.axis_index("batch")
    return lax.rem(seq, 2), lax.div(batch, 2), lax.rem(batch, 2), lax.div(seq, 2)


def by_core(mine, other, axis):
    core = place_xy()[2]
    return jnp.where(
        core == 0, jnp.concatenate([mine, other], axis=axis), jnp.concatenate([other, mine], axis=axis)
    )


def pick(values, index, axis):
    return lax.dynamic_index_in_dim(values, index, axis, keepdims=False)


def z_kernel(widths, *refs):
    pieces, outs = refs[:4], refs[4:6]
    z = place_xy()[3]
    for k in range(4):
        spot = lax.rem(z + 4 - k, 4)
        outs[0][spot] = pieces[k][:, : widths[0]]
        outs[1][spot] = pieces[k][:, widths[0] :]


def z_place(pieces, widths):
    rows = pieces[0].shape[0]
    return pl.pallas_call(
        functools.partial(z_kernel, widths),
        out_shape=[jax.ShapeDtypeStruct((4, rows, width), BF) for width in widths],
        compiler_params=pltpu.CompilerParams(vmem_limit_bytes=VMEM_BYTES),
        cost_estimate=pl.CostEstimate(flops=0, bytes_accessed=16 * rows * sum(widths), transcendentals=0),
        name="z_place",
    )(*pieces)


def halves(width):
    first = (width // 256) * 128
    return (first, width - first)


def gather_chunk(chunk):
    widths = halves(chunk.shape[1])
    near = [chunk] + [shift_z(chunk, k) for k in range(1, 4)]
    first, second = z_place(near, widths)
    first_x, second_y = swap_x(first), swap_y(second)
    first_y, second_x = swap_y(first), swap_x(second)
    first_xy, second_xy = swap_y(first_x), swap_x(second_y)
    own = [first, first_y, first_x, first_xy, second, second_y, second_x, second_xy]
    return own + [swap_c(piece) for piece in own]


def blocks(width, most=512):
    return [(start, min(most, width - start)) for start in range(0, width, most)]


def grad_kernel(rows, left_ref, right_ref, got_ref, keep_a, send_a, keep_b, send_b, total, sems):
    x, y, core, _ = place_xy()
    width = got_ref.shape[1]
    widths = halves(width)
    left = left_ref[...]
    copies = []
    begin = 0
    for half in range(2):
        for start, size in blocks(widths[half]):
            start += begin
            spot = pl.multiple_of(core * width + start, 128)
            part = t_dot(left, right_ref[:, pl.ds(spot, size)]) + got_ref[:, start : start + size].astype(F32)
            total[:, :, :, start : start + size] = part.astype(BF).reshape(4, 4, rows, size)
        for far in range(2):
            if half == 0:
                keep, send = (x + far) % 2 * 2 + y, (x + far) % 2 * 2 + 1 - y
                pair = (keep_a, send_a)
            else:
                keep, send = x * 2 + (y + far) % 2, (1 - x) * 2 + (y + far) % 2
                pair = (keep_b, send_b)
            for n, (ref, spot) in enumerate(zip(pair, (keep, send))):
                copy = pltpu.make_async_copy(
                    total.at[:, spot, :, pl.ds(begin, widths[half])], ref.at[far], sems.at[half * 4 + far * 2 + n]
                )
                copy.start()
                copies.append(copy)
        begin += widths[half]
    for copy in copies:
        copy.wait()


def grad_call(left, right, got, rows):
    width = got.shape[1]
    widths = halves(width)
    whole = pl.BlockSpec(memory_space=pltpu.VMEM)
    return pl.pallas_call(
        functools.partial(grad_kernel, rows),
        in_specs=[whole] * 3,
        out_specs=[pl.BlockSpec(memory_space=pl.ANY)] * 4,
        out_shape=[jax.ShapeDtypeStruct((2, 4, rows, widths[n // 2]), BF) for n in range(4)],
        scratch_shapes=[pltpu.VMEM((4, 4, rows, width), BF), pltpu.SemaphoreType.DMA((8,))],
        compiler_params=pltpu.CompilerParams(vmem_limit_bytes=VMEM_BYTES),
        cost_estimate=pl.CostEstimate(
            flops=2 * 256 * got.size, bytes_accessed=4 * got.size + 2 * right.size, transcendentals=0
        ),
        name="grad_split",
    )(left, right, got)


def add(*values):
    total = values[0].astype(F32)
    for value in values[1:]:
        total = total + value.astype(F32)
    return total


def first_sum_kernel(keep_a, got_a, keep_b, got_b, far_a, far_b):
    far_a[...] = add(keep_a[1], got_a[1]).astype(BF)
    far_b[...] = add(keep_b[1], got_b[1]).astype(BF)


def second_sum_kernel(keep_a, got_a, keep_b, got_b, more_a, more_b, own, *sends):
    z = place_xy()[3]
    first = more_a.shape[2]
    for k in range(4):
        spot = lax.rem(z + k, 4)
        left = add(keep_a[0, spot], got_a[0, spot], more_a[spot])
        right = add(keep_b[0, spot], got_b[0, spot], more_b[spot])
        ref = sends[k - 1] if k else own
        ref[:, :first] = left.astype(ref.dtype)
        ref[:, first:] = right.astype(ref.dtype)


def third_sum_kernel(own, got_1, got_2, got_3, mine, other):
    core = place_xy()[2]
    half = mine.shape[0]
    total = add(own[...], got_1[...], got_2[...], got_3[...])
    low, high = total[:half], total[half:]
    mine[...] = jnp.where(core == 0, low, high)
    other[...] = jnp.where(core == 0, high, low)


def last_kernel(count, *refs):
    core = place_xy()[2]
    ins, outs = refs[: 4 * count], refs[4 * count :]
    for n in range(count):
        for layer in range(2):
            mine, other = ins[4 * n + 2 * layer], ins[4 * n + 2 * layer + 1]
            if n == 2:
                low = jnp.where(core == 0, mine[...], other[...])
                high = jnp.where(core == 0, other[...], mine[...])
                outs[2][layer] = low
                outs[3][layer] = high
            else:
                ref = outs[n + (1 if n > 2 else 0)]
                width = mine.shape[1]
                ref[layer, :, pl.ds(pl.multiple_of(core * width, 128), width)] = mine[...]
                ref[layer, :, pl.ds(pl.multiple_of((1 - core) * width, 128), width)] = other[...]


def simple_call(kernel, out_shape, args, name):
    moved = sum(a.size * a.dtype.itemsize for a in list(args) + list(out_shape))
    return pl.pallas_call(
        kernel,
        out_shape=out_shape,
        compiler_params=pltpu.CompilerParams(vmem_limit_bytes=VMEM_BYTES),
        cost_estimate=pl.CostEstimate(flops=0, bytes_accessed=moved, transcendentals=0),
        name=name,
    )(*args)


def scatter_chunk(left, right, rows):
    core = place_xy()[2]
    width = right.shape[1] // 2
    widths = halves(width)
    other = lax.dynamic_slice_in_dim(right, (1 - core) * width, width, 1)
    sent = lax.dot_general(left, other, (((0,), (0,)), ((), ())), preferred_element_type=F32).astype(BF)
    keep_a, send_a, keep_b, send_b = grad_call(left, right, swap_c(sent), rows)
    got_a, got_b = swap_y(send_a), swap_x(send_b)
    far_a, far_b = simple_call(
        first_sum_kernel,
        [jax.ShapeDtypeStruct((4, rows, w), BF) for w in widths],
        (keep_a, got_a, keep_b, got_b),
        "first_sum",
    )
    more_a, more_b = swap_x(far_a), swap_y(far_b)
    own, *sends = simple_call(
        second_sum_kernel,
        [jax.ShapeDtypeStruct((rows, width), F32 if n == 0 else BF) for n in range(4)],
        (keep_a, got_a, keep_b, got_b, more_a, more_b),
        "second_sum",
    )
    got = [shift_z(value, k + 1) for k, value in enumerate(sends)]
    mine, other = simple_call(
        third_sum_kernel, [jax.ShapeDtypeStruct((rows // 2, width), F32)] * 2, (own, *got), "third_sum"
    )
    return mine, swap_c(other)


def last_call(pairs):
    args = []
    shapes = []
    for n, pair in enumerate(pairs):
        for mine, other in pair:
            args += [mine, other]
        rows, width = pair[0][0].shape
        if n == 2:
            shapes += [jax.ShapeDtypeStruct((2, rows, width), F32)] * 2
        else:
            shapes.append(jax.ShapeDtypeStruct((2, rows, 2 * width), F32))
    return simple_call(functools.partial(last_kernel, len(pairs)), shapes, args, "last_layout")


def load_plan(meta):
    kind, rows, width = meta
    if kind == "plain":
        return 1, (rows, width), 1
    return 16, (4, 4, rows, width), 16


def start_load(meta, refs, vmem, sems):
    kind, rows, width = meta
    if kind == "plain":
        copy = pltpu.make_async_copy(refs[0], vmem, sems.at[0])
        copy.start()
        cuts = blocks(width, 1408 if width % 1408 == 0 else 768 if width % 768 == 0 else 512)
        return [(start, size, start, [copy] if start == 0 else []) for start, size in cuts]
    x, y, core, _ = place_xy()
    half_width = width // 2
    widths = halves(half_width)
    groups = []
    for other in range(2):
        side = core if other == 0 else 1 - core
        for half in range(2):
            begin = widths[0] if half else 0
            size = widths[half]
            copies = []
            for dx in range(2):
                for dy in range(2):
                    n = ((other * 2 + half) * 2 + dx) * 2 + dy
                    spot = (x + dx) % 2 * 2 + (y + dy) % 2
                    src = refs[n]
                    if src.shape[2] != size:
                        src = src.at[:, :, pl.ds(0, size)]
                    copy = pltpu.make_async_copy(
                        src, vmem.at[:, spot, :, pl.ds(other * half_width + begin, size)], sems.at[n]
                    )
                    copy.start()
                    copies.append(copy)
            groups.append((other * half_width + begin, size, side * half_width + begin, copies))
    return groups


def loaded(meta, vmem, start, size):
    if meta[0] == "plain":
        return vmem[:, start : start + size]
    return vmem[:, :, :, start : start + size].reshape(16 * meta[1], size)


def spot_of(start, size):
    if isinstance(start, int):
        return pl.ds(start, size)
    return pl.ds(pl.multiple_of(start, 128), size)


def times(meta, left, vmem, groups, store):
    for start, size, place, copies in groups:
        for copy in copies:
            copy.wait()
        store(spot_of(place, size), dot(left, loaded(meta, vmem, start, size)))


def times_t(meta, left_ref, vmem, groups):
    total = None
    for start, size, place, copies in groups:
        for copy in copies:
            copy.wait()
        part = dot_t(left_ref[:, spot_of(place, size)], loaded(meta, vmem, start, size))
        total = part if total is None else total + part
    return total


def weight_call(kernel, metas, weights, args, out_shape, scratch, name, flops):
    counts = [load_plan(m) for m in metas]

    def run(*refs):
        refs = list(refs)
        ins = [refs.pop(0) for _ in args]
        pieces = [[refs.pop(0) for _ in range(c[0])] for c in counts]
        outs = [refs.pop(0) for _ in out_shape]
        buffers = [(refs.pop(0), refs.pop(0)) for _ in counts]
        kernel(metas, ins, pieces, outs, buffers, refs)

    whole = pl.BlockSpec(memory_space=pltpu.VMEM)
    moved = sum(a.size * a.dtype.itemsize for a in list(args) + list(out_shape))
    scratches = []
    for c in counts:
        scratches += [pltpu.VMEM(c[1], BF), pltpu.SemaphoreType.DMA((c[2],))]
    for c in counts:
        size = 2
        for n in c[1]:
            size *= n
        moved += size
    return pl.pallas_call(
        run,
        in_specs=[whole] * len(args) + [pl.BlockSpec(memory_space=pl.ANY)] * sum(c[0] for c in counts),
        out_specs=[whole] * len(out_shape),
        out_shape=out_shape,
        scratch_shapes=scratches + list(scratch),
        compiler_params=pltpu.CompilerParams(vmem_limit_bytes=VMEM_BYTES),
        cost_estimate=pl.CostEstimate(flops=flops, bytes_accessed=moved, transcendentals=0),
        name=name,
    )(*args, *[p for w in weights for p in w])


def qkv_kernel(metas, ins, pieces, outs, buffers, scratch):
    x_ref, gain_ref, wb_ref, bias_ref = ins
    h_ref, proj_ref, beta_ref, edge_ref = outs
    groups = start_load(metas[0], pieces[0], *buffers[0])
    h = rms_scale(x_ref[...], gain_ref[...].astype(F32)).astype(BF)
    h_ref[...] = h
    beta_ref[...] = jax.nn.sigmoid(dot(h, wb_ref[...]) + bias_ref[...])

    def store(spot, value):
        proj_ref[:, spot] = value
        edge_ref[:, spot] = value[-16:].astype(BF)

    times(metas[0], h, buffers[0][0], groups, store)


def out_kernel(metas, ins, pieces, outs, buffers, scratch):
    o_ref, eff_ref, state_ref, head_ref, x_ref, gain_ref = ins
    full_ref, on_ref, x1_ref, h2_ref = outs
    groups = start_load(metas[0], pieces[0], *buffers[0])
    gain = head_ref[...].astype(F32)
    for head in range(HEADS):
        s = slice(head * HEAD_DIM, (head + 1) * HEAD_DIM)
        o = o_ref[:, s] + dot(eff_ref[:, s], state_ref[head])
        full_ref[:, s] = o
        on_ref[:, s] = rms_scale(o, gain).astype(BF)

    def store(spot, value):
        x1_ref[:, spot] = x_ref[:, spot] + value

    times(metas[0], on_ref[...], buffers[0][0], groups, store)
    h2_ref[...] = rms_scale(x1_ref[...], gain_ref[...].astype(F32)).astype(BF)


def mlp_kernel(metas, ins, pieces, outs, buffers, scratch):
    h2_ref, x1_ref = ins
    gu_ref, hid_ref, x2_ref = outs
    groups = start_load(metas[0], pieces[0], *buffers[0])
    later = start_load(metas[1], pieces[1], *buffers[1])

    def store(spot, value):
        gu_ref[:, spot] = value

    times(metas[0], h2_ref[...], buffers[0][0], groups, store)
    ff = hid_ref.shape[1]
    for start, size in blocks(ff):
        gate = gu_ref[:, start : start + size]
        hid_ref[:, start : start + size] = (
            gate * jax.nn.sigmoid(gate) * gu_ref[:, ff + start : ff + start + size]
        ).astype(BF)

    def store_two(spot, value):
        x2_ref[:, spot] = x1_ref[:, spot] + value

    times(metas[1], hid_ref[...], buffers[1][0], later, store_two)


def mlp_back_kernel(metas, ins, pieces, outs, buffers, scratch):
    g_ref, gu_ref, x1_ref, gain_ref, o_ref, eff_ref, head_ref = ins
    dgu_ref, dx1_ref, dy1_ref, dmlp_ref, do_ref, ds_ref, dgain_ref = outs
    dy2_ref, dhid_ref, don_ref = scratch
    down = start_load(metas[0], pieces[0], *buffers[0])
    gate_up = start_load(metas[1], pieces[1], *buffers[1])
    out = start_load(metas[2], pieces[2], *buffers[2])
    dy2_ref[...] = g_ref[...].astype(BF)
    dhid_ref[...] = times_t(metas[0], dy2_ref, buffers[0][0], down)
    ff = dhid_ref.shape[1]
    for start, size in blocks(ff):
        s = slice(start, start + size)
        f = slice(ff + start, ff + start + size)
        gate = gu_ref[:, s]
        sig = jax.nn.sigmoid(gate)
        dhid = dhid_ref[:, s]
        act = gate * sig
        dgu_ref[:, s] = (dhid * gu_ref[:, f] * (sig + act * (1.0 - sig))).astype(BF)
        dgu_ref[:, f] = (dhid * act).astype(BF)
    dh2 = times_t(metas[1], dgu_ref, buffers[1][0], gate_up)
    back, part = rms_back(x1_ref[...], gain_ref[...].astype(F32), dh2)
    dmlp_ref[...] = jnp.sum(part, axis=0, keepdims=True)
    dx1 = g_ref[...] + back
    dx1_ref[...] = dx1
    dy1_ref[...] = dx1.astype(BF)
    don_ref[...] = times_t(metas[2], dy1_ref, buffers[2][0], out)
    gain = head_ref[...].astype(F32)
    dgain = jnp.zeros((1, HEAD_DIM), F32)
    for head in range(HEADS):
        s = slice(head * HEAD_DIM, (head + 1) * HEAD_DIM)
        back, part = rms_back(o_ref[:, s], gain, don_ref[:, s])
        dgain = dgain + jnp.sum(part, axis=0, keepdims=True)
        low = back.astype(BF)
        do_ref[:, s] = low
        ds_ref[head] = t_dot(eff_ref[:, s], low)
    dgain_ref[...] = dgain


def qkv_back_kernel(metas, ins, pieces, outs, buffers, scratch):
    dproj_ref, tail_ref, back_ref, dlogit_ref, wb_ref, x_ref, gain_ref, dx1_ref, h_ref = ins
    fixed_ref, g_ref, dmix_ref, dbeta_ref, dbias_ref = outs
    groups = start_load(metas[0], pieces[0], *buffers[0])
    rows = dproj_ref.shape[0]
    fixed_ref[: rows - 16] = dproj_ref[: rows - 16]
    fixed_ref[rows - 16 :] = (tail_ref[...] + back_ref[...].astype(F32)).astype(BF)
    dlogit = dlogit_ref[...]
    dbias_ref[...] = jnp.sum(dlogit, axis=0, keepdims=True)
    low = dlogit.astype(BF)
    dbeta_ref[...] = t_dot(h_ref[...], low)
    dh = times_t(metas[0], fixed_ref, buffers[0][0], groups) + dot_t(low, wb_ref[...])
    back, part = rms_back(x_ref[...], gain_ref[...].astype(F32), dh)
    dmix_ref[...] = jnp.sum(part, axis=0, keepdims=True)
    g_ref[...] = dx1_ref[...] + back


def is_fast():
    return lax.axis_size("seq") == 8 and lax.axis_size("batch") == 4


def gather_weights(qkv, conv, beta, out, mix, mlp, gate, up, down):
    layers = qkv.shape[0]
    result = []
    if not is_fast():
        for n in range(layers):
            rows = [lax.all_gather(a[n], BOTH, axis=0, tiled=True) for a in (beta, mix, mlp, qkv, out, gate, up, down)]
            rows[5:7] = [jnp.concatenate(rows[5:7], axis=1)]
            names = ("beta", "mix", "mlp", "qkv", "out", "gate_up", "down")
            found = dict(zip(names[:3], rows[:3]))
            found["conv"] = lax.all_gather(conv[n], BOTH, axis=1, tiled=True)
            for name, value in zip(names[3:], rows[3:]):
                found[name] = (("plain",) + value.shape, [value])
            result.append(found)
        return result
    x, y, core, _ = place_xy()

    def split(values):
        width = values.shape[2] // 2
        return (
            lax.dynamic_slice_in_dim(values, core * width, width, 2),
            lax.dynamic_slice_in_dim(values, (1 - core) * width, width, 2),
        )

    gate_up = jnp.concatenate([gate, up], axis=2)
    mine, other = zip(*(split(v) for v in (qkv, out, gate_up, down)))
    wide = swap_c(jnp.concatenate(other[:3], axis=2))
    cuts = (other[0].shape[2], other[0].shape[2] + other[1].shape[2])
    got = (wide[..., : cuts[0]], wide[..., cuts[0] : cuts[1]], wide[..., cuts[1] :], swap_c(other[3]))
    chunks = [by_core(a, b, 1) for a, b in zip(mine, got)]
    flat = jnp.concatenate([v.reshape(-1) for v in (conv, beta, mix, mlp)])
    rows = chunks[0].shape[1]
    lanes = flat.shape[0] // rows
    extra = jnp.pad(flat.reshape(rows, lanes), ((0, 0), (0, 128 - lanes)))
    devices = lax.axis_size("seq") * lax.axis_size("batch")

    def unflip(values, axis, bit):
        return jnp.where(bit == 0, values, jnp.flip(values, axis))

    for n in range(layers):
        first = chunks[0][n]
        if n == 0:
            first = jnp.concatenate([first, extra], axis=1)
        pieces = gather_chunk(first)
        if n == 0:
            begin = pieces[4].shape[2] - 128
            tiny = jnp.stack([p[:, :, begin : begin + lanes] for p in pieces[4:8] + pieces[12:16]])
            tiny = tiny.reshape((2, 2, 2, 4, rows, lanes))
            tiny = unflip(unflip(unflip(tiny, 0, core), 1, x), 2, y)
            flats = jnp.transpose(tiny, (3, 1, 2, 0, 4, 5)).reshape(devices, -1)
            small = []
            start = 0
            for v in (conv, beta, mix, mlp):
                small.append(flats[:, start : start + v.size].reshape((devices,) + v.shape))
                start += v.size
            conv_all = jnp.moveaxis(small[0], 0, 2).reshape(layers, CONV, -1)
            beta_all, mix_all, mlp_all = (jnp.moveaxis(v, 0, 1).reshape((layers, -1) + v.shape[3:]) for v in small[1:])
        found = dict(conv=conv_all[n], beta=beta_all[n], mix=mix_all[n], mlp=mlp_all[n])
        found["qkv"] = (("fast", rows, qkv.shape[2]), pieces)
        found["out"] = (("fast", rows, out.shape[2]), gather_chunk(chunks[1][n]))
        found["gate_up"] = (("fast", rows, gate_up.shape[2]), gather_chunk(chunks[2][n]))
        found["down"] = (("fast", chunks[3].shape[1], down.shape[2]), gather_chunk(chunks[3][n]))
        result.append(found)
    return result


def scatter(left, right):
    if is_fast():
        return scatter_chunk(left, right, left.shape[1] // 16)
    value = lax.dot_general(left, right, (((0,), (0,)), ((), ())), preferred_element_type=F32)
    return lax.psum_scatter(value.astype(BF), BOTH, scatter_dimension=0, tiled=True).astype(F32)


def collect(large):
    if is_fast():
        return last_call([[layer[m] for layer in large] for m in range(4)])
    stacked = [jnp.stack([layer[m] for layer in large]) for m in range(4)]
    ff = stacked[2].shape[2] // 2
    return stacked[0], stacked[1], stacked[2][..., :ff], stacked[2][..., ff:], stacked[3]


def shape(dims, dtype):
    return jax.ShapeDtypeStruct(dims, dtype)


def forward(x, w, bias, head_gain, pos, keep):
    rows = x.shape[0]
    metas = {name: w[name][0] for name in ("qkv", "out", "gate_up", "down")}
    width, ff2 = metas["qkv"][2], metas["gate_up"][2]
    h, proj, beta, edge = weight_call(
        qkv_kernel, [metas["qkv"]], [w["qkv"][1]], (x, w["mix"][None], w["beta"], bias),
        [shape((rows, D), BF), shape((rows, width), F32), shape((rows, HEADS), F32), shape((16, width), BF)],
        [], "norm_qkv", 2 * rows * D * width,
    )
    before = shift(edge, 1)
    o, eff, tot, inv, st = local_call(keep, pos, beta, proj, before, w["conv"])
    sin = chain(tot[:, :, :HEAD_DIM], tot[:, :, HEAD_DIM:], 1)
    o, on, x1, h2 = weight_call(
        out_kernel, [metas["out"]], [w["out"][1]], (o, eff, sin, head_gain, x, w["mlp"][None]),
        [shape((rows, D), F32), shape((rows, D), BF), shape((rows, D), F32), shape((rows, D), BF)],
        [], "head_out", 2 * rows * D * D,
    )
    gu, hid, x2 = weight_call(
        mlp_kernel, [metas["gate_up"], metas["down"]], [w["gate_up"][1], w["down"][1]], (h2, x1),
        [shape((rows, ff2), F32), shape((rows, ff2 // 2), BF), shape((rows, D), F32)],
        [], "mlp", 3 * rows * D * ff2,
    )
    kept = dict(
        x=x, h=h, proj=proj, before=before, beta=beta, o=o, eff=eff, a=tot[:, :, HEAD_DIM:],
        inv=inv, st=st, sin=sin, head_gain=head_gain, on=on, x1=x1, h2=h2, gu=gu, hid=hid, w=w,
    )
    return x2, kept


def backward(g, kept, pos, keep):
    w = kept["w"]
    rows = g.shape[0]
    metas = {name: w[name][0] for name in ("qkv", "out", "gate_up", "down")}
    width, ff2 = metas["qkv"][2], metas["gate_up"][2]
    d_down = scatter(kept["hid"], g.astype(BF))
    dgu, dx1, dy1, d_mlp, do, ds0, d_head = weight_call(
        mlp_back_kernel,
        [metas["down"], metas["gate_up"], metas["out"]],
        [w["down"][1], w["gate_up"][1], w["out"][1]],
        (g, kept["gu"], kept["x1"], w["mlp"][None], kept["o"], kept["eff"], kept["head_gain"]),
        [
            shape((rows, ff2), BF), shape((rows, D), F32), shape((rows, D), BF), shape((1, D), F32),
            shape((rows, D), BF), shape((HEADS, HEAD_DIM, HEAD_DIM), F32), shape((1, HEAD_DIM), F32),
        ],
        [pltpu.VMEM((rows, D), BF), pltpu.VMEM((rows, ff2 // 2), F32), pltpu.VMEM((rows, D), F32)],
        "mlp_back", 3 * rows * D * ff2,
    )
    d_gate_up = scatter(kept["h2"], dgu)
    d_out = scatter(kept["on"], dy1)
    ds = chain(ds0, jnp.swapaxes(kept["a"], 1, 2), -1)
    dproj, tail, dbefore, dtaps, dlogit = back_call(
        keep, pos, kept["beta"], kept["proj"], kept["before"], w["conv"],
        kept["inv"], kept["st"], kept["sin"], ds, do,
    )
    returned = shift(dbefore, -1)
    dproj, g, d_mix, d_beta, d_bias = weight_call(
        qkv_back_kernel, [metas["qkv"]], [w["qkv"][1]],
        (dproj, tail, returned, dlogit, w["beta"], kept["x"], w["mix"][None], dx1, kept["h"]),
        [
            shape((rows, width), BF), shape((rows, D), F32), shape((1, D), F32), shape((D, HEADS), F32),
            shape((1, HEADS), F32),
        ],
        [], "qkv_back", 2 * rows * D * width,
    )
    d_qkv = scatter(kept["h"], dproj)
    large = (d_qkv, d_out, d_gate_up, d_down)
    small = (dtaps, d_beta, d_bias[0], d_head[0], d_mix[0], d_mlp[0])
    return g, large, small


def body(
    tokens, qkv_weight, conv_weight, beta_weight, beta_bias, head_gain, out_weight, mixer_gain, mlp_gain,
    gate_weight, up_weight, down_weight, lengths, cotangent,
):
    rows = tokens.shape[1]
    index = lax.axis_index("seq") * rows + jnp.arange(rows, dtype=jnp.int32)
    seq_lengths = lengths[0]
    starts = jnp.cumsum(seq_lengths) - seq_lengths
    begin = jnp.max(jnp.where(starts[None, :] <= index[:, None], starts[None, :], 0), axis=1)
    positions = (index - begin).astype(jnp.int32)
    keep = (positions[::STRETCH] != 0).astype(F32)
    pos = positions[:, None]
    weights = gather_weights(
        qkv_weight, conv_weight, beta_weight, out_weight, mixer_gain, mlp_gain, gate_weight, up_weight, down_weight
    )
    x = tokens[0].astype(F32)
    saved = []
    for n in range(LAYERS):
        x, kept = forward(x, weights[n], beta_bias[n].astype(F32)[None], head_gain[n][None], pos, keep)
        saved.append(kept)
    mixed = x.astype(BF)[None]
    g = cotangent[0].astype(F32)
    large = [None] * LAYERS
    small = [None] * LAYERS
    place = lax.axis_index("seq") * lax.axis_size("batch") + lax.axis_index("batch")
    for n in reversed(range(LAYERS)):
        g, large[n], parts = backward(g, saved[n], pos, keep)
        sizes = [p.size for p in parts]
        flat = lax.psum(jnp.concatenate([p.reshape(-1) for p in parts]), BOTH)
        pieces = []
        start = 0
        for p, size in zip(parts, sizes):
            pieces.append(flat[start : start + size].reshape(p.shape))
            start += size
        small[n] = pieces

    def own(values, axis):
        size = values.shape[axis] // (lax.axis_size("seq") * lax.axis_size("batch"))
        return lax.dynamic_slice_in_dim(values, place * size, size, axis)

    big = collect(large)
    tiny = [jnp.stack([small[n][m] for n in range(LAYERS)]) for m in range(6)]
    return (
        mixed, g[None], big[0], own(tiny[0], 2), own(tiny[1], 1), tiny[2], tiny[3], big[1],
        own(tiny[4], 1), own(tiny[5], 1), big[2], big[3], big[4],
    )


def solution(mesh):
    rows = P(None, BOTH, None)
    vector = P(None, BOTH)
    cols = P(None, None, BOTH)
    stream = P("batch", "seq", None)
    return jax.shard_map(
        body,
        mesh=mesh,
        in_specs=(
            stream, rows, cols, rows, P(), P(), rows, vector, vector, rows, rows, rows, P("batch", None), stream,
        ),
        out_specs=(stream, stream, rows, cols, rows, P(), P(), rows, vector, vector, rows, rows, rows),
        check_vma=False,
    )
```

```python
from collections import namedtuple
from types import SimpleNamespace

import jax
import jax.numpy as jnp
from jax import lax
from jax.experimental import pallas as pl
from jax.experimental.pallas import tpu as pltpu
from jax.sharding import PartitionSpec as P

D = 1024
HEADS = 8
HEAD_DIM = 128
CONV = 4
STRETCH = 64
LAYERS = 2
EPSILON = 1e-06
BF = jnp.bfloat16
F32 = jnp.float32
BOTH = ("seq", "batch")
VMEM_BYTES = 56 * 1024 * 1024
BACK_BYTES = 63 * 1024 * 1024


def dot(a, b):
    return lax.dot_general(a.astype(BF), b.astype(BF), (((1,), (0,)), ((), ())), preferred_element_type=F32)


def dot_t(a, b):
    return lax.dot_general(a.astype(BF), b.astype(BF), (((1,), (1,)), ((), ())), preferred_element_type=F32)


def t_dot(a, b):
    return lax.dot_general(a.astype(BF), b.astype(BF), (((0,), (0,)), ((), ())), preferred_element_type=F32)


def rms_scale(values, gain):
    return values * lax.rsqrt(jnp.mean(values * values, axis=-1, keepdims=True) + EPSILON) * gain


def rms_back(values, gain, grad):
    r = lax.rsqrt(jnp.mean(values * values, axis=-1, keepdims=True) + EPSILON)
    unit = values * r
    scaled = grad * gain
    back = r * (scaled - unit * jnp.mean(scaled * unit, axis=-1, keepdims=True))
    return back, grad * unit


def masks(rows):
    i = lax.broadcasted_iota(jnp.int32, (rows, rows), 0)
    j = lax.broadcasted_iota(jnp.int32, (rows, rows), 1)
    same = (i // STRETCH) == (j // STRETCH)
    strict = same & (i > j)
    causal = same & (i >= j)
    return i, j, strict, causal


def conv_rows(rows, before, taps, pos):
    total = rows.shape[0]
    padded = jnp.concatenate([before, rows], axis=0)
    acc = taps[CONV - 1 : CONV] * rows
    for tap in range(CONV - 1):
        offset = CONV - 1 - tap
        shifted = padded[8 - offset : 8 - offset + total]
        acc = acc + taps[tap : tap + 1] * jnp.where(pos >= offset, shifted, 0.0)
    return acc, padded


def unit_rows(values):
    return values * lax.rsqrt(jnp.sum(values * values, axis=-1, keepdims=True) + EPSILON)


def columns(ref, start):
    return ref[:, pl.ds(pl.multiple_of(start, HEAD_DIM), HEAD_DIM)]


def head_column(ref, head):
    values = ref[...]
    lane = lax.broadcasted_iota(jnp.int32, values.shape, 1)
    return jnp.sum(jnp.where(lane == head, values, 0.0), axis=1, keepdims=True)


def inverse_less_one(lower, i, j):
    near = (i // 16) == (j // 16)
    base = jnp.where(near, lower, 0.0)
    r = -base
    power = base
    for _ in range(3):
        power = dot(power, power)
        r = r + power + dot(r, power)
    for width in (32, 64):
        step = ((i // width) == (j // width)) & ((i // (width // 2)) != (j // (width // 2)))
        m = jnp.where(step, lower, 0.0)
        y = m + dot(r, m)
        r = r - y - dot(y, r)
    return r


def local_heads(heads, keep_ref, pos_ref, beta_ref, proj_ref, before_ref, taps_ref, o_ref, eff_ref, tot_ref, inv_ref, st_ref):
    rows = proj_ref.shape[0]
    i, j, strict, causal = masks(rows)
    pos = pos_ref[...]
    for head in heads:
        parts = []
        for third in range(3):
            start = third * D + head * HEAD_DIM
            acc, _ = conv_rows(
                columns(proj_ref, start), columns(before_ref, start).astype(F32)[8:],
                columns(taps_ref, start).astype(F32), pos,
            )
            parts.append(acc * jax.nn.sigmoid(acc))
        q = (unit_rows(parts[0]) * HEAD_DIM ** (-0.5)).astype(BF)
        k32 = unit_rows(parts[1])
        k = k32.astype(BF)
        beta = head_column(beta_ref, head)
        lower = jnp.where(strict, beta * dot_t(k, k), 0.0)
        inv = inverse_less_one(lower, i, j).astype(BF)
        inv_ref[head] = inv
        x = jnp.concatenate([beta * k32, beta * parts[2]], axis=1)
        wu = x + dot(inv, x)
        w = wu[:, :HEAD_DIM].astype(BF)
        u = wu[:, HEAD_DIM:]
        scores = jnp.where(causal, dot_t(q, k), 0.0).astype(BF)
        ii = lax.broadcasted_iota(jnp.int32, (HEAD_DIM, 2 * HEAD_DIM), 0)
        jj = lax.broadcasted_iota(jnp.int32, (HEAD_DIM, 2 * HEAD_DIM), 1)
        state = jnp.where(ii + HEAD_DIM == jj, 1.0, 0.0)
        lanes = pl.ds(pl.multiple_of(head * HEAD_DIM, HEAD_DIM), HEAD_DIM)
        for c in range(rows // STRETCH):
            s = slice(c * STRETCH, (c + 1) * STRETCH)
            state = state * keep_ref[c]
            low = state.astype(BF)
            st_ref[head, c] = low
            both = dot(jnp.concatenate([w[s], q[s]], axis=0), low)
            fresh = -both[:STRETCH]
            fresh = jnp.concatenate([fresh[:, :HEAD_DIM] + u[s], fresh[:, HEAD_DIM:]], axis=1).astype(BF)
            out = both[STRETCH:] + dot(scores[s, s], fresh)
            state = state + t_dot(k[s], fresh)
            o_ref[s, lanes] = out[:, :HEAD_DIM]
            eff_ref[s, lanes] = out[:, HEAD_DIM:].astype(BF)
        tot_ref[head] = state


def local_kernel(*refs):
    @pl.loop(0, HEADS // 2)
    def _(pair):
        local_heads([pair * 2, pair * 2 + 1], *refs)


def full(shape):
    return pl.BlockSpec(shape, lambda h: (0,) * len(shape))


def local_call(keep, pos, beta, proj, before, taps):
    rows = proj.shape[0]
    count = rows // STRETCH
    whole = pl.BlockSpec(memory_space=pltpu.VMEM)
    return pl.pallas_call(
        local_kernel,
        in_specs=[pl.BlockSpec(memory_space=pltpu.SMEM)] + [whole] * 5,
        out_specs=[whole] * 5,
        out_shape=[
            jax.ShapeDtypeStruct((rows, D), F32),
            jax.ShapeDtypeStruct((rows, D), BF),
            jax.ShapeDtypeStruct((HEADS, HEAD_DIM, 2 * HEAD_DIM), F32),
            jax.ShapeDtypeStruct((HEADS, rows, rows), BF),
            jax.ShapeDtypeStruct((HEADS, count, HEAD_DIM, 2 * HEAD_DIM), BF),
        ],
        compiler_params=pltpu.CompilerParams(vmem_limit_bytes=VMEM_BYTES),
        name="delta_local",
    )(keep, pos, beta, proj, before, taps)


def back_heads(
    heads, keep_ref, pos_ref, beta_ref, proj_ref, before_ref, taps_ref, inv_ref, st_ref, sin_ref, ds_ref, do_ref,
    dproj_ref, tail_ref, dbefore_ref, dtaps_ref, dbeta_ref,
):
    rows = proj_ref.shape[0]
    count = rows // STRETCH
    i, j, strict, causal = masks(rows)
    pos = pos_ref[...]
    for head in heads:
        lanes = pl.ds(pl.multiple_of(head * HEAD_DIM, HEAD_DIM), HEAD_DIM)
        raw, act, padded = [], [], []
        for third in range(3):
            start = third * D + head * HEAD_DIM
            acc, pad = conv_rows(columns(proj_ref, start), columns(before_ref, start).astype(F32)[8:], columns(taps_ref, start).astype(F32), pos)
            raw.append(acc)
            act.append(acc * jax.nn.sigmoid(acc))
            padded.append(pad)
        rq = lax.rsqrt(jnp.sum(act[0] * act[0], axis=-1, keepdims=True) + EPSILON)
        rk = lax.rsqrt(jnp.sum(act[1] * act[1], axis=-1, keepdims=True) + EPSILON)
        q = (act[0] * rq * HEAD_DIM ** (-0.5)).astype(BF)
        k32 = act[1] * rk
        k = k32.astype(BF)
        beta = head_column(beta_ref, head)
        gram = jnp.where(strict, dot_t(k, k), 0.0)
        inv = inv_ref[head]
        x = jnp.concatenate([beta * k32, beta * act[2]], axis=1)
        wu = x + dot(inv, x)
        w = wu[:, :HEAD_DIM].astype(BF)
        u = wu[:, HEAD_DIM:]
        scores = jnp.where(causal, dot_t(q, k), 0.0).astype(BF)
        dout = do_ref[:, lanes]
        sin = sin_ref[head].astype(BF)
        states, fresh = [], []
        for c in range(count):
            s = slice(c * STRETCH, (c + 1) * STRETCH)
            packed = st_ref[head, c]
            state = (packed[:, :HEAD_DIM].astype(F32) + dot(packed[:, HEAD_DIM:], sin)).astype(BF)
            states.append(state)
            fresh.append((u[s] - dot(w[s], state)).astype(BF))
        fresh_all = jnp.concatenate(fresh, axis=0)
        dscores = jnp.where(causal, dot_t(dout, fresh_all), 0.0).astype(BF)
        dfresh0 = t_dot(scores, dout)
        ds = ds_ref[head].astype(F32)
        dfresh = [None] * count
        dk_state = [None] * count
        dq_state = [None] * count
        dw = [None] * count
        for c in reversed(range(count)):
            s = slice(c * STRETCH, (c + 1) * STRETCH)
            low = ds.astype(BF)
            part = dfresh0[s] + dot(k[s], low)
            dfresh[c] = part
            part_low = part.astype(BF)
            dk_state[c] = dot_t(fresh[c], low)
            both = dot_t(jnp.concatenate([dout[s], part_low], axis=0), states[c])
            dq_state[c] = both[:STRETCH]
            dw[c] = -both[STRETCH:]
            ds = (ds + t_dot(q[s], dout[s]) - t_dot(w[s], part_low)) * keep_ref[c]
        dfresh_all = jnp.concatenate(dfresh, axis=0)
        dq = jnp.concatenate(dq_state, axis=0) + dot(dscores, k)
        dk = jnp.concatenate(dk_state, axis=0) + t_dot(dscores, q)
        dwu = jnp.concatenate([jnp.concatenate(dw, axis=0), dfresh_all], axis=1)
        dx = dwu + t_dot(inv, dwu)
        dlower = jnp.where(strict, -dot_t(dx, wu), 0.0)
        dbeta = jnp.sum(dlower * gram, axis=1, keepdims=True)
        dxk = dx[:, :HEAD_DIM]
        dxv = dx[:, HEAD_DIM:]
        dbeta = dbeta + jnp.sum(dxk * k32 + dxv * act[2], axis=1, keepdims=True)
        dgram = (dlower * beta).astype(BF)
        dk = dk + dot(dgram, k) + t_dot(dgram, k) + beta * dxk
        dv = beta * dxv
        lane = lax.broadcasted_iota(jnp.int32, (rows, HEADS), 1)
        dbeta_ref[...] += jnp.where(lane == head, dbeta * beta * (1.0 - beta), 0.0)
        dq = dq * HEAD_DIM ** (-0.5)
        grads = (
            rq * (dq - act[0] * (rq * rq * jnp.sum(act[0] * dq, axis=-1, keepdims=True))),
            rk * (dk - k32 * jnp.sum(k32 * dk, axis=-1, keepdims=True)),
            dv,
        )
        for third in range(3):
            start = third * D + head * HEAD_DIM
            spot = pl.ds(pl.multiple_of(start, HEAD_DIM), HEAD_DIM)
            sig = jax.nn.sigmoid(raw[third])
            dmix = grads[third] * (sig + act[third] * (1.0 - sig))
            taps = columns(taps_ref, start).astype(F32)
            dpad = jnp.concatenate([jnp.zeros((8, HEAD_DIM), F32), taps[CONV - 1 : CONV] * dmix], axis=0)
            dtap = [None] * CONV
            dtap[CONV - 1] = jnp.sum(dmix * padded[third][8:], axis=0, keepdims=True)
            for tap in range(CONV - 1):
                offset = CONV - 1 - tap
                kept = jnp.where(pos >= offset, dmix, 0.0)
                dtap[tap] = jnp.sum(kept * padded[third][8 - offset : 8 - offset + rows], axis=0, keepdims=True)
                scaled = taps[tap : tap + 1] * kept
                dpad = dpad + jnp.concatenate(
                    [jnp.zeros((8 - offset, HEAD_DIM), F32), scaled, jnp.zeros((offset, HEAD_DIM), F32)], axis=0
                )
            dproj_ref[:, spot] = dpad[8:].astype(BF)
            tail_ref[:, spot] = dpad[rows - 8 :]
            dbefore_ref[:, spot] = jnp.concatenate([jnp.zeros((8, HEAD_DIM), F32), dpad[:8]], axis=0).astype(BF)
            dtaps_ref[:, spot] = jnp.concatenate(dtap, axis=0)


def back_kernel(*refs):
    refs[-1][...] = jnp.zeros_like(refs[-1])

    @pl.loop(0, HEADS // 2)
    def _(pair):
        back_heads([pair * 2, pair * 2 + 1], *refs)


def back_call(*args):
    rows = args[3].shape[0]
    whole = pl.BlockSpec(memory_space=pltpu.VMEM)
    return pl.pallas_call(
        back_kernel,
        in_specs=[pl.BlockSpec(memory_space=pltpu.SMEM)] + [whole] * (len(args) - 1),
        out_specs=[whole] * 5,
        out_shape=[
            jax.ShapeDtypeStruct((rows, 3 * D), BF),
            jax.ShapeDtypeStruct((16, 3 * D), F32),
            jax.ShapeDtypeStruct((16, 3 * D), BF),
            jax.ShapeDtypeStruct((CONV, 3 * D), F32),
            jax.ShapeDtypeStruct((rows, HEADS), F32),
        ],
        compiler_params=pltpu.CompilerParams(vmem_limit_bytes=VMEM_BYTES),
        name="delta_back",
    )(*args)


def shift(values, steps):
    count = lax.axis_size("seq")
    first, last = max(0, -steps), min(count, count - steps)
    return lax.ppermute(values, "seq", [(n, n + steps) for n in range(first, last)])


def chain(tot_b, tot_a, steps):
    peers = lax.axis_size("seq")
    state = jnp.zeros(tot_b.shape, F32)
    low_a = tot_a.astype(BF)
    for turn in range(peers - 1):
        if turn == 0:
            new = tot_b
        else:
            new = tot_b + jnp.einsum("hde,hef->hdf", low_a, state.astype(BF), preferred_element_type=F32)
        state = shift(new.astype(BF), steps).astype(F32)
    return state


def place_xy():
    seq, batch = lax.axis_index("seq"), lax.axis_index("batch")
    return lax.rem(seq, 2), lax.div(batch, 2), lax.rem(batch, 2), lax.div(seq, 2)


def blocks(width, most=512):
    return [(start, min(most, width - start)) for start in range(0, width, most)]


def load_plan(meta):
    return 1, meta[1:], 1


def start_load(meta, refs, vmem, sems):
    width = meta[2]
    copy = pltpu.make_async_copy(refs[0], vmem, sems.at[0])
    copy.start()
    cuts = blocks(width, 1408 if width % 1408 == 0 else 768 if width % 768 == 0 else 512)
    return [(start, size, start, [copy] if start == 0 else []) for start, size in cuts]


def loaded(meta, vmem, start, size):
    return vmem[:, start : start + size]


def spot_of(start, size):
    if isinstance(start, int):
        return pl.ds(start, size)
    return pl.ds(pl.multiple_of(start, 128), size)


def times(meta, left, vmem, groups, store):
    for start, size, place, copies in groups:
        for copy in copies:
            copy.wait()
        store(spot_of(place, size), dot(left, loaded(meta, vmem, start, size)))


def times_t(meta, left_ref, vmem, groups):
    total = None
    for start, size, place, copies in groups:
        for copy in copies:
            copy.wait()
        part = dot_t(left_ref[:, spot_of(place, size)], loaded(meta, vmem, start, size))
        total = part if total is None else total + part
    return total


def weight_call(kernel, metas, weights, args, out_shape, scratch, name, flops):
    counts = [load_plan(m) for m in metas]

    def run(*refs):
        refs = list(refs)
        ins = [refs.pop(0) for _ in args]
        pieces = [[refs.pop(0) for _ in range(c[0])] for c in counts]
        outs = [refs.pop(0) for _ in out_shape]
        buffers = [(refs.pop(0), refs.pop(0)) for _ in counts]
        kernel(metas, ins, pieces, outs, buffers, refs)

    whole = pl.BlockSpec(memory_space=pltpu.VMEM)
    moved = sum(a.size * a.dtype.itemsize for a in list(args) + list(out_shape))
    scratches = []
    for c in counts:
        scratches += [pltpu.VMEM(c[1], BF), pltpu.SemaphoreType.DMA((c[2],))]
    for c in counts:
        size = 2
        for n in c[1]:
            size *= n
        moved += size
    return pl.pallas_call(
        run,
        in_specs=[whole] * len(args) + [pl.BlockSpec(memory_space=pl.ANY)] * sum(c[0] for c in counts),
        out_specs=[whole] * len(out_shape),
        out_shape=out_shape,
        scratch_shapes=scratches + list(scratch),
        compiler_params=pltpu.CompilerParams(vmem_limit_bytes=VMEM_BYTES),
        cost_estimate=pl.CostEstimate(flops=flops, bytes_accessed=moved, transcendentals=0),
        name=name,
    )(*args, *[p for w in weights for p in w])


def qkv_kernel(metas, ins, pieces, outs, buffers, scratch):
    x_ref, gain_ref, wb_ref, bias_ref = ins
    h_ref, proj_ref, beta_ref, edge_ref = outs
    groups = start_load(metas[0], pieces[0], *buffers[0])
    h = rms_scale(x_ref[...], gain_ref[...].astype(F32)).astype(BF)
    h_ref[...] = h
    beta_ref[...] = jax.nn.sigmoid(dot(h, wb_ref[...]) + bias_ref[...])

    def store(spot, value):
        proj_ref[:, spot] = value
        edge_ref[:, spot] = value[-16:].astype(BF)

    times(metas[0], h, buffers[0][0], groups, store)


def out_kernel(metas, ins, pieces, outs, buffers, scratch):
    o_ref, eff_ref, state_ref, head_ref, x_ref, gain_ref = ins
    full_ref, on_ref, x1_ref, h2_ref = outs
    groups = start_load(metas[0], pieces[0], *buffers[0])
    gain = head_ref[...].astype(F32)
    for head in range(HEADS):
        s = slice(head * HEAD_DIM, (head + 1) * HEAD_DIM)
        o = o_ref[:, s] + dot(eff_ref[:, s], state_ref[head])
        full_ref[:, s] = o
        on_ref[:, s] = rms_scale(o, gain).astype(BF)

    def store(spot, value):
        x1_ref[:, spot] = x_ref[:, spot] + value

    times(metas[0], on_ref[...], buffers[0][0], groups, store)
    h2_ref[...] = rms_scale(x1_ref[...], gain_ref[...].astype(F32)).astype(BF)


def mlp_kernel(metas, ins, pieces, outs, buffers, scratch):
    h2_ref, x1_ref = ins
    gu_ref, hid_ref, x2_ref = outs
    groups = start_load(metas[0], pieces[0], *buffers[0])
    later = start_load(metas[1], pieces[1], *buffers[1])

    def store(spot, value):
        gu_ref[:, spot] = value

    times(metas[0], h2_ref[...], buffers[0][0], groups, store)
    ff = hid_ref.shape[1]
    for start, size in blocks(ff):
        gate = gu_ref[:, start : start + size]
        hid_ref[:, start : start + size] = (
            gate * jax.nn.sigmoid(gate) * gu_ref[:, ff + start : ff + start + size]
        ).astype(BF)

    def store_two(spot, value):
        x2_ref[:, spot] = x1_ref[:, spot] + value

    times(metas[1], hid_ref[...], buffers[1][0], later, store_two)


def mlp_back_kernel(metas, ins, pieces, outs, buffers, scratch):
    g_ref, gu_ref, x1_ref, gain_ref, o_ref, eff_ref, head_ref = ins
    dgu_ref, dx1_ref, dy1_ref, dmlp_ref, do_ref, ds_ref, dgain_ref = outs
    dy2_ref, dhid_ref, don_ref = scratch
    down = start_load(metas[0], pieces[0], *buffers[0])
    gate_up = start_load(metas[1], pieces[1], *buffers[1])
    out = start_load(metas[2], pieces[2], *buffers[2])
    dy2_ref[...] = g_ref[...].astype(BF)
    dhid_ref[...] = times_t(metas[0], dy2_ref, buffers[0][0], down)
    ff = dhid_ref.shape[1]
    for start, size in blocks(ff):
        s = slice(start, start + size)
        f = slice(ff + start, ff + start + size)
        gate = gu_ref[:, s]
        sig = jax.nn.sigmoid(gate)
        dhid = dhid_ref[:, s]
        act = gate * sig
        dgu_ref[:, s] = (dhid * gu_ref[:, f] * (sig + act * (1.0 - sig))).astype(BF)
        dgu_ref[:, f] = (dhid * act).astype(BF)
    dh2 = times_t(metas[1], dgu_ref, buffers[1][0], gate_up)
    back, part = rms_back(x1_ref[...], gain_ref[...].astype(F32), dh2)
    dmlp_ref[...] = jnp.sum(part, axis=0, keepdims=True)
    dx1 = g_ref[...] + back
    dx1_ref[...] = dx1
    dy1_ref[...] = dx1.astype(BF)
    don_ref[...] = times_t(metas[2], dy1_ref, buffers[2][0], out)
    gain = head_ref[...].astype(F32)
    dgain = jnp.zeros((1, HEAD_DIM), F32)
    for head in range(HEADS):
        s = slice(head * HEAD_DIM, (head + 1) * HEAD_DIM)
        back, part = rms_back(o_ref[:, s], gain, don_ref[:, s])
        dgain = dgain + jnp.sum(part, axis=0, keepdims=True)
        low = back.astype(BF)
        do_ref[:, s] = low
        ds_ref[head] = t_dot(eff_ref[:, s], low)
    dgain_ref[...] = dgain


def qkv_back_kernel(metas, ins, pieces, outs, buffers, scratch):
    dproj_ref, tail_ref, back_ref, dlogit_ref, wb_ref, x_ref, gain_ref, dx1_ref, h_ref = ins
    fixed_ref, g_ref, dmix_ref, dbeta_ref, dbias_ref = outs
    groups = start_load(metas[0], pieces[0], *buffers[0])
    rows = dproj_ref.shape[0]
    fixed_ref[: rows - 16] = dproj_ref[: rows - 16]
    fixed_ref[rows - 16 :] = (tail_ref[...] + back_ref[...].astype(F32)).astype(BF)
    dlogit = dlogit_ref[...]
    dbias_ref[...] = jnp.sum(dlogit, axis=0, keepdims=True)
    low = dlogit.astype(BF)
    dbeta_ref[...] = t_dot(h_ref[...], low)
    dh = times_t(metas[0], fixed_ref, buffers[0][0], groups) + dot_t(low, wb_ref[...])
    back, part = rms_back(x_ref[...], gain_ref[...].astype(F32), dh)
    dmix_ref[...] = jnp.sum(part, axis=0, keepdims=True)
    g_ref[...] = dx1_ref[...] + back


def gather_weights(qkv, conv, beta, out, mix, mlp, gate, up, down):
    result = []
    for n in range(qkv.shape[0]):
        rows = [lax.all_gather(a[n], BOTH, axis=0, tiled=True) for a in (beta, mix, mlp, qkv, out, gate, up, down)]
        rows[5:7] = [jnp.concatenate(rows[5:7], axis=1)]
        names = ("beta", "mix", "mlp", "qkv", "out", "gate_up", "down")
        found = dict(zip(names[:3], rows[:3]))
        found["conv"] = lax.all_gather(conv[n], BOTH, axis=1, tiled=True)
        for name, value in zip(names[3:], rows[3:]):
            found[name] = (("plain",) + value.shape, [value])
        result.append(found)
    return result


def scatter(left, right):
    value = lax.dot_general(left, right, (((0,), (0,)), ((), ())), preferred_element_type=F32)
    return lax.psum_scatter(value.astype(BF), BOTH, scatter_dimension=0, tiled=True).astype(F32)


MESH = pl.DeviceIdType.MESH


def device(x, y, core, z):
    return (z * 2 + x, y * 2 + core)


def path_place():
    x, y, core, z = place_xy()
    piece = z * 2 + core

    def at(step):
        other = (piece + step + 8) % 8
        return device(x, y, other % 2, other // 2)

    return piece, at(1), at(-1)


def partner():
    x, y, core, z = place_xy()
    return device(1 - x, y, 1 - core, z)


def signal_all(peers):
    barrier = pltpu.get_barrier_semaphore()
    for peer in peers:
        pl.semaphore_signal(barrier, inc=1, device_id=peer, device_id_type=MESH)
    pl.semaphore_wait(barrier, len(peers))


def near_peers():
    x, y, core, z = place_xy()
    peers = [device(1 - x, y, core, z), device(x, 1 - y, core, z), device(x, y, 1 - core, z)]
    return peers + [device(x, y, core, (z + k) % 4) for k in range(1, 4)]


class Gather:
    def __init__(self, mine, full, begin, cut, sends, gots):
        self.mine, self.full, self.begin, self.cut = mine, full, begin, cut
        self.sends, self.gots = sends, gots
        self.size = mine.shape[1]
        self.half = full.shape[4] // 2
        self.pending = []

    def cols(self, core, part=None):
        start, size = self.begin, self.size
        if part == 0:
            size = self.cut
        if part == 1:
            start, size = start + self.cut, size - self.cut
        return pl.ds(pl.multiple_of(core * self.half + start, 128), size)

    def copy(self, n, src, dst, peer):
        return pltpu.make_async_remote_copy(
            src_ref=src, dst_ref=dst, send_sem=self.sends.at[n], recv_sem=self.gots.at[n],
            device_id=peer, device_id_type=MESH,
        )

    def send(self, n, src, dst, peer):
        copy = self.copy(n, src, dst, peer)
        copy.start()
        self.pending.append(copy)

    def got(self, n, region, peer):
        self.copy(n, region, region, peer).wait_recv()

    def stages(self):
        return [self.stage_z, self.stage_one, self.stage_two, self.stage_core, self.stage_end]

    def stage_z(self):
        x, y, core, z = place_xy()
        spot = self.full.at[z, x, y, :, self.cols(core)]
        self.local = pltpu.make_async_copy(self.mine, spot, self.sends.at[8])
        self.local.start()
        for k in range(1, 4):
            self.send(k - 1, self.mine, spot, device(x, y, core, (z + k) % 4))

    def stage_one(self):
        x, y, core, z = place_xy()
        self.local.wait()
        for k in range(1, 4):
            self.got(k - 1, self.full.at[(z + 4 - k) % 4, x, y, :, self.cols(core)], device(x, y, core, (z + 4 - k) % 4))
        a = self.full.at[:, x, y, :, self.cols(core, 0)]
        b = self.full.at[:, x, y, :, self.cols(core, 1)]
        self.send(3, a, a, device(1 - x, y, core, z))
        self.send(4, b, b, device(x, 1 - y, core, z))

    def stage_two(self):
        x, y, core, z = place_xy()
        self.got(3, self.full.at[:, 1 - x, y, :, self.cols(core, 0)], device(1 - x, y, core, z))
        self.got(4, self.full.at[:, x, 1 - y, :, self.cols(core, 1)], device(x, 1 - y, core, z))
        a = self.full.at[:, :, y, :, self.cols(core, 0)]
        b = self.full.at[:, x, :, :, self.cols(core, 1)]
        self.send(5, a, a, device(x, 1 - y, core, z))
        self.send(6, b, b, device(1 - x, y, core, z))

    def stage_core(self):
        x, y, core, z = place_xy()
        self.got(5, self.full.at[:, :, 1 - y, :, self.cols(core, 0)], device(x, 1 - y, core, z))
        self.got(6, self.full.at[:, 1 - x, :, :, self.cols(core, 1)], device(1 - x, y, core, z))
        both = self.full.at[:, :, :, :, self.cols(core)]
        self.send(7, both, both, device(x, y, 1 - core, z))

    def stage_end(self):
        x, y, core, z = place_xy()
        self.got(7, self.full.at[:, :, :, :, self.cols(1 - core)], device(x, y, 1 - core, z))


class Schedule:
    def __init__(self, gathers, swaps):
        self.gathers, self.swaps = gathers, swaps
        self.ready = {}
        self.turn = 0

    def tick(self):
        for stage in reversed(range(5)):
            n = self.turn - stage
            if 0 <= n < len(self.gathers):
                if stage == 0:
                    self.swaps[n].wait()
                    if n in self.ready:
                        self.ready[n]()
                self.gathers[n].stages()[stage]()
        self.turn += 1

    def until(self, n):
        while self.turn < n + 5:
            self.tick()

    def finish(self):
        self.until(len(self.gathers) - 1)
        for gather in self.gathers:
            for copy in gather.pending:
                copy.wait_send()


def swap_rows(shard, mine, begin, send, got):
    x, y, core, z = place_xy()
    size = mine.shape[1]

    def copy_of(source, target):
        return pltpu.make_async_remote_copy(
            src_ref=source, dst_ref=target, send_sem=send, recv_sem=got,
            device_id=device(x, y, 1 - core, z), device_id_type=MESH,
        )

    if len(shard) == 2:
        rows = shard[0].shape[0]
        place = pl.ds(pl.multiple_of(core * rows, rows), rows)
        for side in range(2):

            @pl.when(core == side)
            def _():
                copy_of(shard[1 - side].at[:, pl.ds(begin, size)], mine.at[place, :]).start()
                mine[place, :] = shard[side][:, pl.ds(begin, size)]

        return copy_of(shard[0].at[:, pl.ds(begin, size)], mine.at[place, :])
    shard = shard[0]
    rows = shard.shape[0]
    half = shard.shape[1] // 2
    place = pl.ds(pl.multiple_of(core * rows, rows), rows)
    copy = copy_of(shard.at[:, pl.ds(pl.multiple_of((1 - core) * half + begin, 128), size)], mine.at[place, :])
    copy.start()
    mine[place, :] = shard[:, pl.ds(pl.multiple_of(core * half + begin, 128), size)]
    return copy


CHUNKS = dict(
    out=[(64, 0, 512, 256)],
    down=[(176, 0, 256, 128), (176, 256, 256, 128)],
    qkv=[(64, 0, 768, 384), (64, 768, 768, 384)],
    gate_up=[(64, 0, 768, 384), (64, 768, 640, 256), (64, 1408, 768, 384), (64, 2176, 640, 384)],
)


def load_columns(full, vmem, spans, sems):
    copies = []
    for n, (start, size) in enumerate(spans):
        copy = pltpu.make_async_copy(
            full.at[:, :, :, :, pl.ds(start, size)], vmem.at[:, :, :, :, pl.ds(start, size)], sems.at[n]
        )
        copy.start()
        copies.append(copy)
    return copies


def weight_columns(vmem, start, size):
    dims = vmem.shape
    return vmem[:, :, :, :, start : start + size].reshape(16 * dims[3], size)


def dma(*dims):
    return pltpu.SemaphoreType.DMA(dims)


def stream_place(r, piece, rows):
    first = r.lengths[0, 0]
    second = first + r.lengths[0, 1]
    index = piece * rows + lax.broadcasted_iota(jnp.int32, (rows, 1), 0)
    begin = jnp.where(index >= second, second, jnp.where(index >= first, first, 0))
    r.pos[...] = index - begin
    keep = []
    for start in range(0, rows, STRETCH):
        token = piece * rows + start
        new = (token == 0) | (token == first) | (token == second)
        keep.append(jnp.where(new, 0.0, 1.0))
    return keep


def gather_small(r):
    seq, batch = lax.axis_index("seq"), lax.axis_index("batch")
    me = seq * 4 + batch
    copies = []
    for k in range(1, 32):
        peer = (me + k) % 32
        copy = pltpu.make_async_remote_copy(
            src_ref=r.packed, dst_ref=r.packs.at[me], send_sem=r.small_sends.at[k - 1], recv_sem=r.small_gots.at[k - 1],
            device_id=(peer // 4, peer % 4), device_id_type=MESH,
        )
        copy.start()
        copies.append(copy)
    r.packs[me] = r.packed[...]
    return copies


def lay_out_small(r):
    rows = r.packs[:, 16:48, :].reshape(D, 128)
    i = lax.broadcasted_iota(jnp.int32, (24, 128), 0)
    j = lax.broadcasted_iota(jnp.int32, (24, 128), 1)
    r.smalls[...] = dot_t(jnp.where(i == j, 1.0, 0.0), rows)
    i = lax.broadcasted_iota(jnp.int32, (128, 384), 0)
    j = lax.broadcasted_iota(jnp.int32, (128, 384), 1)
    total = None
    for n in range(4):
        left = jnp.concatenate([r.packs[4 * q + n, 0:16, :].astype(F32)[:8] for q in range(8)], axis=0)
        part = dot(left, jnp.where((j == i + 96 * n) & (i < 96), 1.0, 0.0))
        total = part if total is None else total + part
    for q in range(8):
        for n in range(2):
            r.taps[n, :, 384 * q : 384 * (q + 1)] = total[8 * q + 4 * n : 8 * q + 4 * n + 4]


def forward_kernel(number, chunks, shards, fulls, mines, r):
    piece, after, before = path_place()
    x, y, core, z = place_xy()
    first_block = number == 0
    if first_block:
        seq, batch = lax.axis_index("seq"), lax.axis_index("batch")
        me = seq * 4 + batch
        signal_all([((me + k) % 32 // 4, (me + k) % 32 % 4) for k in range(1, 32)])
    else:
        signal_all(near_peers() + [after, before])
    rows = r.x.shape[0]
    swaps, gathers = [], []
    first = {}
    for n, (name, part) in enumerate(chunks):
        mine = mines[n]
        first.setdefault(name, n)
        shard = shards[name]
        if name == "down":
            half = shard[0].shape[1] // 2
            copy = pltpu.make_async_remote_copy(
                src_ref=shard[0].at[:, pl.ds(pl.multiple_of((1 - core) * half + part[1], 128), part[2])],
                dst_ref=r.other_down.at[:, pl.ds(part[1], part[2])],
                send_sem=r.swap_sends.at[n], recv_sem=r.swap_gots.at[n],
                device_id=device(x, y, 1 - core, z), device_id_type=MESH,
            )
            copy.start()
        else:
            copy = swap_rows(shard, mine, part[1], r.swap_sends.at[n], r.swap_gots.at[n])
        swaps.append(copy)
        gathers.append(Gather(mine, fulls[name], part[1], part[3], r.sends.at[n], r.gots.at[n]))
    if first_block:
        small_copies = gather_small(r)
    schedule = Schedule(gathers, swaps)
    for n, (name, part) in enumerate(chunks):
        if name == "down":
            half = shards[name][0].shape[1] // 2

            def ready(n=n, part=part, half=half):
                own = shards["down"][0][:, pl.ds(pl.multiple_of(core * half + part[1], 128), part[2])].astype(F32)
                other = r.other_down[:, part[1] : part[1] + part[2]].astype(F32)
                low = jnp.where(core == 0, own, other)
                high = jnp.where(core == 0, other, own)
                mines[n][...] = jnp.concatenate([low, high], axis=0).astype(BF)

            schedule.ready[n] = ready
    keep = stream_place(r, piece, rows)
    schedule.tick()
    schedule.tick()
    if first_block:
        for copy in small_copies:
            copy.wait()
        lay_out_small(r)
        schedule.until(first["qkv"] + 1)
    wqkv = fulls["qkv"] if first_block else r.wqkv
    wb = r.smalls[8 * number : 8 * number + 8].astype(BF)
    mix = r.smalls[16 + number : 17 + number]
    mlp = r.smalls[18 + number : 19 + number]
    taps = r.taps.at[number]
    spans = [(n * 768, 768) for n in range(4)]
    loads = load_columns(wqkv, r.vbig, spans, r.load_sems)
    h = rms_scale(r.x[...].astype(F32), mix).astype(BF)
    r.h[...] = h
    bias = r.bias[...].astype(F32)
    r.beta[...] = jax.nn.sigmoid(dot_t(h, wb) + bias)
    for (start, size), copy in zip(spans, loads):
        copy.wait()
        value = dot(h, weight_columns(r.vbig, start, size))
        r.proj[:, start : start + size] = value
        r.edge[:, start : start + size] = value[-16:].astype(BF)
    halo = pltpu.make_async_remote_copy(
        src_ref=r.edge, dst_ref=r.halo, send_sem=r.halo_sems.at[0], recv_sem=r.halo_sems.at[1],
        device_id=after, device_id_type=MESH,
    )

    @pl.when(piece < 7)
    def _():
        halo.start()

    @pl.when(piece == 0)
    def _():
        r.halo[...] = jnp.zeros_like(r.halo)

    @pl.when(piece > 0)
    def _():
        halo.wait_recv()

    r.before[...] = r.halo[...]
    schedule.tick()
    for part in range(2):

        @pl.loop(part * 2, part * 2 + 2)
        def _(pair):
            local_heads(
                [pair * 2, pair * 2 + 1], keep, r.pos, r.beta, r.proj, r.halo, taps,
                r.o, r.eff, r.tot, r.inv, r.st,
            )

        schedule.tick()

    links = [
        pltpu.make_async_remote_copy(
            src_ref=r.next.at[pl.ds(2 * n, 2)], dst_ref=r.last.at[pl.ds(2 * n, 2)],
            send_sem=r.chain_sends.at[n], recv_sem=r.chain_gots.at[n],
            device_id=after, device_id_type=MESH,
        )
        for n in range(4)
    ]

    @pl.when(piece == 0)
    def _():
        r.last[...] = jnp.zeros_like(r.last)

    for n, link in enumerate(links):

        @pl.when(piece > 0)
        def _():
            link.wait_recv()

        for head in (2 * n, 2 * n + 1):
            state = r.last[head]
            r.sin[head] = state
            r.a[head] = r.tot[head, :, HEAD_DIM:].astype(BF)
            r.next[head] = (r.tot[head, :, :HEAD_DIM] + dot(r.a[head], state)).astype(BF)

        @pl.when(piece < 7)
        def _():
            link.start()

    schedule.until(first["out"])
    load = load_columns(fulls["out"], r.vout, [(0, D)], r.load_sems)
    gain = r.head[...].astype(F32)
    for head in range(HEADS):
        s = slice(head * HEAD_DIM, (head + 1) * HEAD_DIM)
        o = r.o[:, s] + dot(r.eff[:, s], r.sin[head])
        r.o[:, s] = o
        r.on[:, s] = rms_scale(o, gain).astype(BF)
    load[0].wait()
    r.x1[...] = r.x[...].astype(F32) + dot(r.on[...], weight_columns(r.vout, 0, D))
    h2 = rms_scale(r.x1[...], mlp).astype(BF)
    r.h2[...] = h2
    ff = r.hid.shape[1]
    for part, (_, start, size, _) in enumerate(CHUNKS["gate_up"]):
        schedule.until(first["gate_up"] + part)
        loads = load_columns(fulls["gate_up"], r.vbig, [(start, size), (start + ff, size)], r.load_sems)
        loads[0].wait()
        gate = dot(h2, weight_columns(r.vbig, start, size))
        r.gu[:, start : start + size] = gate.astype(BF)
        loads[1].wait()
        up = dot(h2, weight_columns(r.vbig, start + ff, size))
        r.gu[:, start + ff : start + ff + size] = up.astype(BF)
        r.hid[:, start : start + size] = (gate * jax.nn.sigmoid(gate) * up).astype(BF)
    for part, (_, start, size, _) in enumerate(CHUNKS["down"]):
        schedule.until(first["down"] + part)
        spans = [(start, size), (start + D // 2, size)]
        loads = load_columns(fulls["down"], r.vdown, spans, r.load_sems)
        for (begin, wide), copy in zip(spans, loads):
            copy.wait()
            value = dot(r.hid[...], weight_columns(r.vdown, begin, wide))
            r.x2[:, begin : begin + wide] = (r.x1[:, begin : begin + wide] + value).astype(r.x2.dtype)
    schedule.finish()

    @pl.when(piece < 7)
    def _():
        halo.wait_send()
        for link in links:
            link.wait_send()


def forward_call(number, x, small, lengths, bias, head, shards, wqkv):
    rows = x.shape[0]
    count = rows // STRETCH
    names = list(shards)
    ff2 = 2 * shards["gate_up"][1].shape[2]
    chunks = [(name, part) for name in names for part in CHUNKS[name[:-5] if name.endswith("_next") else name]]
    whole, anywhere = pl.BlockSpec(memory_space=pltpu.VMEM), pl.BlockSpec(memory_space=pl.ANY)
    scalars = pl.BlockSpec(memory_space=pltpu.SMEM)
    ins = dict(
        lengths=(lengths, scalars), x=(x, whole), bias=(bias, whole), head=(head, whole),
    )
    if number:
        ins.update(wqkv=(wqkv, anywhere), smalls=(small[0], whole), taps=(small[1], whole))
    else:
        ins.update(packed=(small, whole))
    outs = dict(
        h=((rows, D), BF), proj=((rows, 3 * D), F32), beta=((rows, HEADS), F32), before=((16, 3 * D), BF),
        o=((rows, D), F32), eff=((rows, D), BF), a=((HEADS, HEAD_DIM, HEAD_DIM), BF), inv=((HEADS, rows, rows), BF),
        st=((HEADS, count, HEAD_DIM, 2 * HEAD_DIM), BF), sin=((HEADS, HEAD_DIM, HEAD_DIM), BF), on=((rows, D), BF),
        x1=((rows, D), F32), h2=((rows, D), BF), gu=((rows, ff2), BF), hid=((rows, ff2 // 2), BF),
        x2=((rows, D), F32 if number + 1 < LAYERS else BF),
    )
    if not number:
        outs.update(smalls=((24, D), F32), taps=((LAYERS, CONV, 3 * D), F32))
    wide = dict(out=D, gate_up=ff2, down=D, qkv=3 * D, qkv_next=3 * D)
    far = [((4, 2, 2, 176 if name == "down" else 64, wide[name]), BF) for name in names]
    v = pltpu.VMEM
    scratch = dict(
        other_down=v((88, 512), BF), vbig=v((4, 2, 2, 64, ff2), BF), vout=v((4, 2, 2, 64, D), BF),
        vdown=v((4, 2, 2, 176, D), BF), edge=v((16, 3 * D), BF), halo=v((16, 3 * D), BF),
        tot=v((HEADS, HEAD_DIM, 2 * HEAD_DIM), F32), next=v((HEADS, HEAD_DIM, HEAD_DIM), BF),
        last=v((HEADS, HEAD_DIM, HEAD_DIM), BF), pos=v((rows, 1), jnp.int32),
        sends=dma(len(chunks), 9), gots=dma(len(chunks), 9), swap_sends=dma(len(chunks)), swap_gots=dma(len(chunks)),
        load_sems=dma(4), halo_sems=dma(2), chain_sends=dma(4), chain_gots=dma(4),
    )
    if not number:
        scratch.update(packs=v((32, 48, 128), BF), small_sends=dma(31), small_gots=dma(31))
    mine = [v((part[0], part[2]), BF) for _, part in chunks]
    sources = [(value, whole) for name in names for value in shards[name][1:]]

    def run(*refs):
        refs = list(refs)

        def take(count):
            taken = refs[:count]
            del refs[:count]
            return taken

        r = dict(zip(ins, take(len(ins))))
        r.update(bias=r["bias"].at[number], head=r["head"].at[number])
        given = {name: [ref.at[shards[name][0]] for ref in take(len(shards[name]) - 1)] for name in names}
        r.update(zip(outs, take(len(outs))))
        fulls = dict(zip(names, take(len(names))))
        r.update(zip(scratch, take(len(scratch))))
        forward_kernel(number, chunks, given, fulls, refs, SimpleNamespace(**r))

    result = pl.pallas_call(
        run,
        in_specs=[spec for _, spec in list(ins.values()) + sources],
        out_specs=[whole] * len(outs) + [anywhere] * len(names),
        out_shape=[jax.ShapeDtypeStruct(*d) for d in list(outs.values()) + far],
        scratch_shapes=list(scratch.values()) + mine,
        compiler_params=pltpu.CompilerParams(
            collective_id=number + 1, has_side_effects=True, vmem_limit_bytes=VMEM_BYTES
        ),
        name="forward_%d" % number,
    )(*[value for value, _ in list(ins.values()) + sources])
    kept = dict(zip(outs, result))
    fulls = dict(zip(names, result[len(outs) :]))
    kept.update(x=x, w_qkv=fulls.get("qkv", wqkv), w_out=fulls["out"], w_gate_up=fulls["gate_up"], w_down=fulls["down"])
    return kept, fulls.get("qkv_next")


Room = namedtuple(
    "Room", ("sent", "landing", "sums", "one_a", "one_b", "two_a", "two_b", "three", "final")
)


class Scatter:
    def __init__(self, left, right, out, rows, begin, size, cut, room, sends, gots):
        self.left, self.right, self.out = left, right, out
        self.rows, self.begin, self.size, self.cut = rows, begin, size, cut
        self.half = out.shape[1] // 2
        self.room, self.sends, self.gots = Room(*room), sends, gots
        self.stage = 0
        self.stages = [self.start, self.square, self.side, self.line, self.total, self.end]

    def step(self):
        self.stages[self.stage]()
        self.stage += 1
        return self.stage == len(self.stages)

    def copy(self, n, src, dst, peer):
        return pltpu.make_async_remote_copy(
            src_ref=src, dst_ref=dst, send_sem=self.sends.at[n], recv_sem=self.gots.at[n],
            device_id=peer, device_id_type=MESH,
        )

    def products(self, core, store):
        left = self.left[...]
        for start, size in blocks(self.size, 384 if self.rows == 64 else 128):
            spot = pl.multiple_of(core * self.half + self.begin + start, 128)
            store(start, size, t_dot(left, self.right[:, pl.ds(spot, size)]).reshape(4, 2, 2, self.rows, size))

    def start(self):
        x, y, core, z = place_xy()
        sent = self.room.sent.at[:, :, :, :, pl.ds(0, self.size)]

        def store(start, size, value):
            self.room.sent[:, :, :, :, start : start + size] = value.astype(BF)

        self.products(1 - core, store)
        self.to_core = self.copy(0, sent, self.room.landing.at[:, :, :, :, pl.ds(0, self.size)], device(x, y, 1 - core, z))
        self.to_core.start()

    def square(self):
        x, y, core, z = place_xy()
        self.to_core.wait()
        room, cut, size = self.room, self.cut, self.size

        def store(start, width, value):
            got = room.landing[:, :, :, :, start : start + width].astype(F32)
            room.sums[:, :, :, :, start : start + width] = (value + got).astype(BF)

        self.products(core, store)
        self.ones = [
            self.copy(
                1, room.sums.at[:, :, 1 - y, :, pl.ds(0, cut)], room.one_a.at[:, :, :, pl.ds(0, cut)],
                device(x, 1 - y, core, z),
            ),
            self.copy(
                2, room.sums.at[:, 1 - x, :, :, pl.ds(cut, size - cut)], room.one_b.at[:, :, :, pl.ds(0, size - cut)],
                device(1 - x, y, core, z),
            ),
        ]
        for copy in self.ones:
            copy.start()

    def side(self):
        x, y, core, z = place_xy()
        room, cut, size = self.room, self.cut, self.size
        for copy in self.ones:
            copy.wait_recv()
        sums = room.sums
        for dx in range(2):
            part = sums[:, dx, pl.ds(y, 1), :, :cut][:, 0].astype(F32) + room.one_a[:, dx, :, :cut].astype(F32)
            sums[:, dx, pl.ds(y, 1), :, :cut] = part.astype(BF)[:, None]
        for dy in range(2):
            part = sums[:, pl.ds(x, 1), dy, :, cut:size][:, 0].astype(F32)
            part = part + room.one_b[:, dy, :, : size - cut].astype(F32)
            sums[:, pl.ds(x, 1), dy, :, cut:size] = part.astype(BF)[:, None]
        self.twos = [
            self.copy(
                3, sums.at[:, 1 - x, y, :, pl.ds(0, cut)], room.two_a.at[:, :, pl.ds(0, cut)], device(1 - x, y, core, z)
            ),
            self.copy(
                4, sums.at[:, x, 1 - y, :, pl.ds(cut, size - cut)], room.two_b.at[:, :, pl.ds(0, size - cut)],
                device(x, 1 - y, core, z),
            ),
        ]
        for copy in self.twos:
            copy.start()

    def line(self):
        x, y, core, z = place_xy()
        room, cut, size = self.room, self.cut, self.size
        for copy in self.twos:
            copy.wait_recv()
        sums = room.sums
        for n in range(4):
            spot = (n, pl.ds(x, 1), pl.ds(y, 1))
            part = sums[spot + (slice(None), slice(0, cut))][0, 0].astype(F32) + room.two_a[n, :, :cut].astype(F32)
            sums[spot + (slice(None), slice(0, cut))] = part.astype(BF)[None, None]
            part = sums[spot + (slice(None), slice(cut, size))][0, 0].astype(F32)
            part = part + room.two_b[n, :, : size - cut].astype(F32)
            sums[spot + (slice(None), slice(cut, size))] = part.astype(BF)[None, None]
        self.threes = [
            self.copy(
                4 + k, sums.at[(z + k) % 4, x, y, :, pl.ds(0, size)], room.three.at[k - 1, :, pl.ds(0, size)],
                device(x, y, core, (z + k) % 4),
            )
            for k in range(1, 4)
        ]
        for copy in self.threes:
            copy.start()

    def total(self):
        x, y, core, z = place_xy()
        room, size = self.room, self.size
        for copy in self.threes:
            copy.wait()
        for copy in self.ones + self.twos:
            copy.wait_send()
        own = room.sums[pl.ds(z, 1), pl.ds(x, 1), pl.ds(y, 1), :, :size][0, 0, 0].astype(F32)
        for k in range(3):
            own = own + room.three[k, :, :size].astype(F32)
        half = self.rows // 2
        low, high = own[:half], own[half:]
        place = pl.ds(pl.multiple_of(core * self.half + self.begin, 128), size)
        self.out[:, place] = jnp.where(core == 0, low, high)
        room.final[:, :size] = jnp.where(core == 0, high, low)
        self.last = self.copy(8, room.final.at[:, pl.ds(0, size)], self.out.at[:, place], device(x, y, 1 - core, z))
        self.last.start()

    def end(self):
        x, y, core, z = place_xy()
        self.last.wait_send()
        place = pl.ds(pl.multiple_of((1 - core) * self.half + self.begin, 128), self.size)
        self.copy(8, self.room.final.at[:, pl.ds(0, self.size)], self.out.at[:, place], device(x, y, 1 - core, z)).wait_recv()


class SumAll:
    def __init__(self, values, out, low, got, sends, gots):
        self.values, self.out, self.low, self.got = values, out, low, got
        self.sends, self.gots = sends, gots
        self.stage = 0

    def copy(self, n, slot, peer):
        return pltpu.make_async_remote_copy(
            src_ref=self.low.at[slot], dst_ref=self.got.at[n], send_sem=self.sends.at[n], recv_sem=self.gots.at[n],
            device_id=peer, device_id_type=MESH,
        )

    def step(self):
        x, y, core, z = place_xy()
        peers = [device(x, y, 1 - core, z), device(1 - x, y, core, z), device(x, 1 - y, core, z)]
        if self.stage == 0:
            total = self.values[...]
        elif self.stage < 4:
            n = self.stage - 1
            self.flying[0].wait()
            total = self.low[n].astype(F32) + self.got[n].astype(F32)
        else:
            for copy in self.flying:
                copy.wait()
            total = None
            for place in range(4):
                part = self.low[3].astype(F32)
                for k in range(1, 4):
                    part = jnp.where((z + 4 - k) % 4 == place, self.got[2 + k].astype(F32), part)
                total = part if total is None else total + part
            self.out[...] = total
            return True
        self.low[self.stage] = total.astype(BF)
        if self.stage < 3:
            self.flying = [self.copy(self.stage, self.stage, peers[self.stage])]
        else:
            self.flying = [self.copy(2 + k, 3, device(x, y, core, (z + k) % 4)) for k in range(1, 4)]
        for copy in self.flying:
            copy.start()
        self.stage += 1
        return False


class Pipeline:
    def __init__(self):
        self.active, self.queue = [], []

    def add(self, *jobs):
        self.queue += jobs

    def tick(self, times=1):
        for _ in range(times):
            self.active = [job for job in self.active if not job.step()]
            if self.queue:
                job = self.queue.pop(0)
                job.step()
                self.active.append(job)

    def drain(self):
        while self.active or self.queue:
            self.tick()


def backward_kernel(number, last, r):
    piece, after, before = path_place()
    x, y, core, z = place_xy()
    signal_all(near_peers() + [after, before, partner()])
    rows = r.g.shape[0]
    keep = stream_place(r, piece, rows)
    wb = r.smalls[8 * number : 8 * number + 8].astype(BF)
    mix = r.smalls[16 + number : 17 + number]
    mlp = r.smalls[18 + number : 19 + number]
    taps = r.taps.at[number]
    g32 = r.g[...].astype(F32)
    moved = pltpu.make_async_remote_copy(
        src_ref=r.mixed if last else r.g_low, dst_ref=r.mixed_out if last else r.g_got,
        send_sem=r.move_sems.at[0], recv_sem=r.move_sems.at[1], device_id=partner(), device_id_type=MESH,
    )
    if last:
        stays = pltpu.make_async_copy(r.mixed, r.mixed_out, r.move_sems.at[2])

        @pl.when(x != core)
        def _():
            moved.start()

        @pl.when(x == core)
        def _():
            stays.start()
    else:
        ff = r.v_hid.shape[1]
        olds = [
            pltpu.make_async_copy(a, b, r.move_sems.at[3 + n])
            for n, (a, b) in enumerate(
                (
                    (r.old_out, r.d_out.at[1]), (r.old_down, r.d_down.at[1]),
                    (r.old_gate_up.at[:, pl.ds(0, ff)], r.d_gate.at[1]),
                    (r.old_gate_up.at[:, pl.ds(ff, ff)], r.d_up.at[1]),
                )
            )
        ]
        for copy in olds:
            copy.start()
    counts = [0, 0]

    def jobs(left, right, out, parts):
        made = []
        for rows_chip, begin, size, cut in parts:
            wide = rows_chip == 64
            rooms, depths = (r.wide, WIDE) if wide else (r.narrow, NARROW)
            n = counts[wide]
            m = sum(counts)
            counts[wide] += 1
            buffers = [buffer.at[n % depth] for buffer, depth in zip(rooms, depths)]
            if not wide:
                buffers[1] = buffers[2]
            made.append(Scatter(left, right, out, rows_chip, begin, size, cut, buffers, r.sends.at[m], r.gots.at[m]))
        return made

    pipe = Pipeline()
    used = []

    def fetch(source, target):
        copy = pltpu.make_async_copy(source, target, r.load_sems.at[len(used)])
        copy.start()
        used.append(copy)
        return copy

    if not last:
        old = [fetch(r.old_h, r.v_h), fetch(r.old_dproj, r.dproj)]
    hid = fetch(r.hid, r.v_hid)
    down = [fetch(r.w_down.at[pl.ds(0, 2)], r.vdown)]
    gu = fetch(r.gu, r.v_gu)
    big = [fetch(r.w_gate_up.at[n], r.vbig.at[n]) for n in range(2)]
    r.dy2[...] = g32.astype(BF)
    if not last:
        for copy in old:
            copy.wait()
        old_jobs = jobs(r.v_h, r.dproj, r.out_old, CHUNKS["qkv"])
        pipe.add(*old_jobs)
    pipe.add(*jobs(r.v_hid, r.dy2, r.out_down, CHUNKS["down"]))
    hid.wait()
    pipe.tick()
    h2, x1, o, eff, on = (
        fetch(a, b)
        for a, b in ((r.h2, r.v_h2), (r.x1, r.v_x), (r.o, r.v_o), (r.eff, r.v_eff), (r.on, r.v_on))
    )

    def fetch_rows(source, n):
        return fetch(source.at[n], r.vbig.at[n % 2, :, :, :, pl.ds(0, source.shape[4])])

    ff = r.v_hid.shape[1]
    gu.wait()
    for n in range(2):
        down[n].wait()
        dhid_all = dot_t(r.dy2[...], r.vdown[...].reshape(ff // 2, D))
        if n == 0:
            down.append(fetch(r.w_down.at[pl.ds(2, 2)], r.vdown))
        for begin, size in blocks(ff // 2, 384):
            start = n * (ff // 2) + begin
            dhid = dhid_all[:, begin : begin + size]
            gate = r.v_gu[:, start : start + size].astype(F32)
            up = r.v_gu[:, ff + start : ff + start + size].astype(F32)
            sig = jax.nn.sigmoid(gate)
            act = gate * sig
            r.v_gu[:, start : start + size] = (dhid * up * (sig + act * (1.0 - sig))).astype(BF)
            r.v_gu[:, ff + start : ff + start + size] = (dhid * act).astype(BF)
        pipe.tick()
    h2.wait()
    pipe.add(*jobs(r.v_h2, r.v_gu, r.out_gate_up, CHUNKS["gate_up"]))
    for n in range(4):
        big[n].wait()
        r.acc[:, n * 256 : (n + 1) * 256] = dot_t(r.v_gu[...], r.vbig[n % 2].reshape(256, 2 * ff))
        big.append(fetch_rows(r.w_gate_up if n < 2 else r.w_out, (n + 2) % 4))
        if n % 2:
            pipe.tick()
    x1.wait()
    back, part = rms_back(r.v_x[...], mlp, r.acc[...])
    r.values[9:10] = jnp.sum(part, axis=0, keepdims=True)
    r.dx1[...] = r.g[...].astype(F32) + back
    r.dy1[...] = r.dx1[...].astype(BF)
    later = [
        fetch(a, b)
        for a, b in (
            (r.sin, r.v_sin), (r.a, r.v_a), (r.proj, r.v_proj), (r.inv, r.v_inv), (r.st, r.v_st),
            (r.x, r.v_x if last else r.g_low),
        )
    ]
    for n in range(4):
        big[4 + n].wait()
        r.acc[:, n * 256 : (n + 1) * 256] = dot_t(r.dy1[...], r.vbig[n % 2, :, :, :, :D].reshape(256, D))
        big.append(fetch_rows(r.w_out if n < 2 else r.w_qkv, (n + 2) % 4))
    o.wait()
    eff.wait()
    gain = r.head[...].astype(F32)
    dgain = jnp.zeros((1, HEAD_DIM), F32)
    for head in range(HEADS):
        s = slice(head * HEAD_DIM, (head + 1) * HEAD_DIM)
        back, part = rms_back(r.v_o[:, s], gain, r.acc[:, s])
        dgain = dgain + jnp.sum(part, axis=0, keepdims=True)
        low = back.astype(BF)
        r.do[:, s] = low
        r.ds0[head] = t_dot(r.v_eff[:, s], low)
    r.values[22:24] = jnp.zeros((2, D), F32)
    r.values[22:23, HEAD_DIM : 2 * HEAD_DIM] = dgain
    on.wait()
    pipe.add(*jobs(r.v_on, r.dy1, r.out_out, CHUNKS["out"]))
    for copy in later:
        copy.wait()

    links = [
        pltpu.make_async_remote_copy(
            src_ref=r.next.at[pl.ds(2 * n, 2)], dst_ref=r.ds.at[pl.ds(2 * n, 2)],
            send_sem=r.chain_sends.at[n], recv_sem=r.chain_gots.at[n],
            device_id=before, device_id_type=MESH,
        )
        for n in range(4)
    ]

    @pl.when(piece == 7)
    def _():
        r.ds[...] = jnp.zeros_like(r.ds)

    for n, link in enumerate(links):

        @pl.when(piece < 7)
        def _():
            link.wait_recv()

        for head in (2 * n, 2 * n + 1):
            r.next[head] = (r.ds0[head] + t_dot(r.v_a[head], r.ds[head])).astype(BF)

        @pl.when(piece > 0)
        def _():
            link.start()

    pipe.tick()
    if not last:
        while min(job.stage for job in old_jobs) < 2:
            pipe.tick()
        own = fetch(r.h, r.v_h)
    else:
        own = fetch(r.h, r.v_h)
    r.dlogit[...] = jnp.zeros_like(r.dlogit)
    for part in range(2):

        @pl.loop(part * 2, part * 2 + 2)
        def _(pair):
            back_heads(
                [pair * 2, pair * 2 + 1], keep, r.pos, r.beta, r.v_proj, r.before, taps, r.v_inv, r.v_st,
                r.v_sin, r.ds, r.do, r.dproj, r.tail, r.edge, r.dtaps, r.dlogit,
            )

        pipe.tick()
    halo = pltpu.make_async_remote_copy(
        src_ref=r.edge, dst_ref=r.halo, send_sem=r.halo_sems.at[0], recv_sem=r.halo_sems.at[1],
        device_id=before, device_id_type=MESH,
    )

    @pl.when(piece > 0)
    def _():
        halo.start()

    dlogit = r.dlogit[...]
    low = dlogit.astype(BF)
    own.wait()
    r.values[0:8] = t_dot(low, r.v_h[...])
    r.values[22:23, 0:HEADS] = jnp.sum(dlogit, axis=0, keepdims=True)
    for tap in range(CONV):
        for third in range(3):
            row = 10 + tap * 3 + third
            r.values[row : row + 1] = r.dtaps[tap : tap + 1, third * D : (third + 1) * D]

    @pl.when(piece == 7)
    def _():
        r.halo[...] = jnp.zeros_like(r.halo)

    @pl.when(piece < 7)
    def _():
        halo.wait_recv()

    r.dproj[rows - 16 :] = (r.tail[...] + r.halo[...].astype(F32)).astype(BF)
    if last:
        pipe.tick()
    else:
        pipe.add(*jobs(r.v_h, r.dproj, r.out_qkv, CHUNKS["qkv"]))
        pipe.tick()
    for n in range(4):
        big[8 + n].wait()
        r.acc[:, n * 256 : (n + 1) * 256] = dot_t(
            r.dproj[...], r.vbig[n % 2, :, :, :, : 3 * D].reshape(256, 3 * D)
        ) + dot(low, wb[:, n * 256 : (n + 1) * 256])
        if n < 2:
            big.append(fetch_rows(r.w_qkv, n + 2))
    x_in = r.v_x[...] if last else r.g_low[...].astype(F32)
    back, part = rms_back(x_in, mix, r.acc[...])
    r.values[8:9] = jnp.sum(part, axis=0, keepdims=True)
    r.g_out[...] = r.dx1[...] + back
    if not last:

        @pl.when(x != core)
        def _():
            r.g_low[...] = r.g_out[...].astype(BF)
            moved.start()

    pipe.add(SumAll(r.values, r.small, r.small_low, r.small_got, r.small_sends, r.small_gots))
    pipe.drain()
    if last:

        @pl.when(x == core)
        def _():
            stays.wait()

        @pl.when(x != core)
        def _():
            moved.wait()
    else:

        @pl.when(x != core)
        def _():
            moved.wait()
            r.g_out[...] = r.g_got[...].astype(F32)

        ends = [
            pltpu.make_async_copy(a, b, r.move_sems.at[7 + n])
            for n, (a, b) in enumerate(
                (
                    (r.out_qkv, r.d_qkv.at[0]), (r.out_old, r.d_qkv.at[1]), (r.out_out, r.d_out.at[0]),
                    (r.out_down, r.d_down.at[0]), (r.out_gate_up.at[:, pl.ds(0, ff)], r.d_gate.at[0]),
                    (r.out_gate_up.at[:, pl.ds(ff, ff)], r.d_up.at[0]),
                )
            )
        ]
        for copy in ends:
            copy.start()
        for copy in olds + ends:
            copy.wait()

    @pl.when(piece > 0)
    def _():
        halo.wait_send()
        for link in links:
            link.wait_send()


WIDE = (1, 2, 3, 2, 2, 2, 2, 2, 1)
NARROW = (1, 1, 2, 2, 2, 2, 2, 2, 1)


def rooms(depths, rows, size):
    half = size // 2
    dims = (
        (4, 2, 2, rows, size), (4, 2, 2, rows, size), (4, 2, 2, rows, size), (4, 2, rows, half), (4, 2, rows, half),
        (4, rows, half), (4, rows, half), (3, rows, size), (rows // 2, size),
    )
    return [pltpu.VMEM((depth,) + d, F32 if n == 8 else BF) for n, (depth, d) in enumerate(zip(depths, dims))]


def backward_call(number, g, kept, small, lengths, head, old=None):
    rows = g.shape[0]
    count = rows // STRETCH
    last = old is None
    ff2 = kept["gu"].shape[1]
    whole, anywhere = pl.BlockSpec(memory_space=pltpu.VMEM), pl.BlockSpec(memory_space=pl.ANY)
    vmem = dict(g=g, smalls=small[0], taps=small[1], beta=kept["beta"], before=kept["before"])
    names = ("gu", "x1", "hid", "h2", "o", "eff", "on", "proj", "inv", "st", "sin", "a", "x", "h")
    hbm = {key: kept[key] for key in names + ("w_down", "w_gate_up", "w_out", "w_qkv")}
    outs = dict(small=((24, D), F32), g_out=((rows, D), F32))
    grads = dict(
        out_down=((88, D), F32), out_gate_up=((32, ff2), F32), out_out=((32, D), F32),
    )
    far = {}
    if last:
        hbm.update(mixed=kept["x2"])
        outs.update(dproj=((rows, 3 * D), BF), **grads)
        far.update(mixed_out=((rows, D), BF))
        grads = {}
    else:
        hbm.update(
            old_h=old["h"], old_dproj=old["dproj"], old_out=old["out_out"], old_down=old["out_down"],
            old_gate_up=old["out_gate_up"],
        )
        far.update(
            d_qkv=((2, 32, 3 * D), F32), d_out=((2, 32, D), F32), d_gate=((2, 32, ff2 // 2), F32),
            d_up=((2, 32, ff2 // 2), F32), d_down=((2, 88, D), F32),
        )
        grads.update(out_old=((32, 3 * D), F32), out_qkv=((32, 3 * D), F32))
    v = pltpu.VMEM
    scratch = dict(
        v_gu=v((rows, ff2), BF), v_x=v((rows, D), F32), v_hid=v((rows, ff2 // 2), BF), v_h2=v((rows, D), BF),
        v_o=v((rows, D), F32), v_eff=v((rows, D), BF), v_on=v((rows, D), BF), v_proj=v((rows, 3 * D), F32),
        v_inv=v((HEADS, rows, rows), BF), v_st=v((HEADS, count, HEAD_DIM, 2 * HEAD_DIM), BF),
        v_sin=v((HEADS, HEAD_DIM, HEAD_DIM), BF), v_a=v((HEADS, HEAD_DIM, HEAD_DIM), BF), v_h=v((rows, D), BF),
        acc=v((rows, D), F32), dy2=v((rows, D), BF), dy1=v((rows, D), BF), dx1=v((rows, D), F32), do=v((rows, D), BF),
        ds=v((HEADS, HEAD_DIM, HEAD_DIM), BF), next=v((HEADS, HEAD_DIM, HEAD_DIM), BF),
        ds0=v((HEADS, HEAD_DIM, HEAD_DIM), F32), tail=v((16, 3 * D), F32), edge=v((16, 3 * D), BF),
        halo=v((16, 3 * D), BF), dtaps=v((CONV, 3 * D), F32), dlogit=v((rows, HEADS), F32), values=v((24, D), F32),
        small_low=v((4, 24, D), BF), small_got=v((6, 24, D), BF),
        vdown=v((2, 2, 2, 176, D), BF), vbig=v((2, 2, 2, 64, ff2), BF),
        sends=dma(12, 9), gots=dma(12, 9), small_sends=dma(6), small_gots=dma(6), load_sems=dma(32), halo_sems=dma(2),
        chain_sends=dma(4), chain_gots=dma(4), move_sems=dma(13), pos=v((rows, 1), jnp.int32),
    )
    scratch.update({key: v(*d) for key, d in grads.items()})
    if not last:
        del scratch["dx1"]
        scratch.update(dproj=v((rows, 3 * D), BF), g_low=v((rows, D), BF), g_got=v((rows, D), BF))
    wide, narrow = rooms(WIDE, 64, 768), rooms(NARROW, 176, 256)
    names = ["lengths", "head"] + list(vmem) + list(hbm) + list(outs) + list(far) + list(scratch)

    def run(*refs):
        found = dict(zip(names, refs))
        found.update(head=found["head"].at[number], dx1=found.get("dx1", found["v_x"]))
        rest = refs[len(names) :]
        backward_kernel(number, last, SimpleNamespace(wide=rest[: len(wide)], narrow=rest[len(wide) :], **found))

    result = pl.pallas_call(
        run,
        in_specs=[pl.BlockSpec(memory_space=pltpu.SMEM), whole]
        + [whole] * len(vmem) + [anywhere] * len(hbm),
        out_specs=[whole] * len(outs) + [anywhere] * len(far),
        out_shape=[jax.ShapeDtypeStruct(*d) for d in list(outs.values()) + list(far.values())],
        scratch_shapes=list(scratch.values()) + wide + narrow,
        compiler_params=pltpu.CompilerParams(
            collective_id=number + 3, has_side_effects=True, vmem_limit_bytes=BACK_BYTES
        ),
        name="backward_%d" % number,
    )(lengths, head, *vmem.values(), *hbm.values())
    return dict(zip(list(outs) + list(far), result))


def shape(dims, dtype):
    return jax.ShapeDtypeStruct(dims, dtype)


def forward(x, w, bias, head_gain, pos, keep):
    rows = x.shape[0]
    metas = {name: w[name][0] for name in ("qkv", "out", "gate_up", "down")}
    width, ff2 = metas["qkv"][2], metas["gate_up"][2]
    h, proj, beta, edge = weight_call(
        qkv_kernel, [metas["qkv"]], [w["qkv"][1]], (x, w["mix"][None], w["beta"], bias),
        [shape((rows, D), BF), shape((rows, width), F32), shape((rows, HEADS), F32), shape((16, width), BF)],
        [], "norm_qkv", 2 * rows * D * width,
    )
    before = shift(edge, 1)
    o, eff, tot, inv, st = local_call(keep, pos, beta, proj, before, w["conv"])
    sin = chain(tot[:, :, :HEAD_DIM], tot[:, :, HEAD_DIM:], 1)
    o, on, x1, h2 = weight_call(
        out_kernel, [metas["out"]], [w["out"][1]], (o, eff, sin, head_gain, x, w["mlp"][None]),
        [shape((rows, D), F32), shape((rows, D), BF), shape((rows, D), F32), shape((rows, D), BF)],
        [], "head_out", 2 * rows * D * D,
    )
    gu, hid, x2 = weight_call(
        mlp_kernel, [metas["gate_up"], metas["down"]], [w["gate_up"][1], w["down"][1]], (h2, x1),
        [shape((rows, ff2), F32), shape((rows, ff2 // 2), BF), shape((rows, D), F32)],
        [], "mlp", 3 * rows * D * ff2,
    )
    kept = dict(
        x=x, h=h, proj=proj, before=before, beta=beta, o=o, eff=eff, a=tot[:, :, HEAD_DIM:],
        inv=inv, st=st, sin=sin, head_gain=head_gain, on=on, x1=x1, h2=h2, gu=gu, hid=hid, w=w,
    )
    return x2, kept


def backward(g, kept, pos, keep):
    w = kept["w"]
    rows = g.shape[0]
    metas = {name: w[name][0] for name in ("qkv", "out", "gate_up", "down")}
    width, ff2 = metas["qkv"][2], metas["gate_up"][2]
    d_down = scatter(kept["hid"], g.astype(BF))
    dgu, dx1, dy1, d_mlp, do, ds0, d_head = weight_call(
        mlp_back_kernel,
        [metas["down"], metas["gate_up"], metas["out"]],
        [w["down"][1], w["gate_up"][1], w["out"][1]],
        (g, kept["gu"], kept["x1"], w["mlp"][None], kept["o"], kept["eff"], kept["head_gain"]),
        [
            shape((rows, ff2), BF), shape((rows, D), F32), shape((rows, D), BF), shape((1, D), F32),
            shape((rows, D), BF), shape((HEADS, HEAD_DIM, HEAD_DIM), F32), shape((1, HEAD_DIM), F32),
        ],
        [pltpu.VMEM((rows, D), BF), pltpu.VMEM((rows, ff2 // 2), F32), pltpu.VMEM((rows, D), F32)],
        "mlp_back", 3 * rows * D * ff2,
    )
    d_gate_up = scatter(kept["h2"], dgu)
    d_out = scatter(kept["on"], dy1)
    ds = chain(ds0, jnp.swapaxes(kept["a"], 1, 2), -1)
    dproj, tail, dbefore, dtaps, dlogit = back_call(
        keep, pos, kept["beta"], kept["proj"], kept["before"], w["conv"],
        kept["inv"], kept["st"], kept["sin"], ds, do,
    )
    returned = shift(dbefore, -1)
    dproj, g, d_mix, d_beta, d_bias = weight_call(
        qkv_back_kernel, [metas["qkv"]], [w["qkv"][1]],
        (dproj, tail, returned, dlogit, w["beta"], kept["x"], w["mix"][None], dx1, kept["h"]),
        [
            shape((rows, width), BF), shape((rows, D), F32), shape((1, D), F32), shape((D, HEADS), F32),
            shape((1, HEADS), F32),
        ],
        [], "qkv_back", 2 * rows * D * width,
    )
    d_qkv = scatter(kept["h"], dproj)
    large = (d_qkv, d_out, d_gate_up, d_down)
    small = (dtaps, d_beta, d_bias[0], d_head[0], d_mix[0], d_mlp[0])
    return g, large, small


def fast_body(
    tokens, qkv_weight, conv_weight, beta_weight, beta_bias, head_gain, out_weight, mixer_gain, mlp_gain,
    gate_weight, up_weight, down_weight, lengths, cotangent,
):
    pairs = []
    for seq in range(8):
        for batch in range(4):
            z, x, y, core = seq // 2, seq % 2, batch // 2, batch % 2
            pairs.append((seq * 4 + batch, (z * 2 + core) * 4 + y * 2 + x))
    tokens, cotangent, lengths = (lax.ppermute(v, BOTH, pairs) for v in (tokens[0], cotangent[0], lengths))
    conv = jnp.pad(conv_weight.reshape(LAYERS * CONV, -1), ((0, 8), (0, 32)))
    columns_of = jnp.concatenate([beta_weight[0], beta_weight[1], mixer_gain.T, mlp_gain.T], axis=1)
    packed = jnp.concatenate([conv, jnp.pad(columns_of, ((0, 0), (0, 128 - columns_of.shape[1])))], axis=0)
    bias, head = beta_bias[:, None], head_gain[:, None]
    x, small, wqkv = tokens, packed, None
    saved = []
    for n in range(LAYERS):
        shards = dict(out=(n, out_weight), gate_up=(n, gate_weight, up_weight), down=(n, down_weight))
        if n == 0:
            shards = dict(qkv=(0, qkv_weight), **shards)
        if n + 1 < LAYERS:
            shards["qkv_next"] = (n + 1, qkv_weight)
        kept, wqkv = forward_call(n, x, small, lengths, bias, head, shards, wqkv)
        if n == 0:
            small = (kept["smalls"], kept["taps"])
        x = kept["x2"]
        saved.append(kept)
    late = backward_call(1, cotangent, saved[1], small, lengths, head)
    late["h"] = saved[1]["h"]
    early = backward_call(0, late["g_out"], saved[0], small, lengths, head, late)
    tiny = jnp.stack([early["small"], late["small"]])
    place = lax.axis_index("seq") * lax.axis_size("batch") + lax.axis_index("batch")

    def own(values, axis):
        return lax.dynamic_slice_in_dim(values, place * (values.shape[axis] // 32), values.shape[axis] // 32, axis)

    beta = jnp.swapaxes(own(tiny[:, 0:8], 2), 1, 2)
    return (
        late["mixed_out"][None], early["g_out"][None], early["d_qkv"], own(tiny[:, 10:22].reshape(LAYERS, CONV, -1), 2),
        beta, tiny[:, 22, :HEADS], tiny[:, 22, HEAD_DIM : 2 * HEAD_DIM], early["d_out"], own(tiny[:, 8], 1),
        own(tiny[:, 9], 1), early["d_gate"], early["d_up"], early["d_down"],
    )


def general_body(
    tokens, qkv_weight, conv_weight, beta_weight, beta_bias, head_gain, out_weight, mixer_gain, mlp_gain,
    gate_weight, up_weight, down_weight, lengths, cotangent,
):
    rows = tokens.shape[1]
    tokens, cotangent = tokens[0], cotangent[0]
    index = lax.axis_index("seq") * rows + jnp.arange(rows, dtype=jnp.int32)
    seq_lengths = lengths[0]
    starts = jnp.cumsum(seq_lengths) - seq_lengths
    begin = jnp.max(jnp.where(starts[None, :] <= index[:, None], starts[None, :], 0), axis=1)
    positions = (index - begin).astype(jnp.int32)
    keep = (positions[::STRETCH] != 0).astype(F32)
    pos = positions[:, None]
    x = tokens.astype(F32)
    saved = []
    weights = gather_weights(
        qkv_weight, conv_weight, beta_weight, out_weight, mixer_gain, mlp_gain, gate_weight, up_weight, down_weight
    )
    for n in range(LAYERS):
        x, kept = forward(x, weights[n], beta_bias[n].astype(F32)[None], head_gain[n][None], pos, keep)
        saved.append(kept)
    mixed = x.astype(BF)
    g = cotangent.astype(F32)
    large = [None] * LAYERS
    small = [None] * LAYERS
    place = lax.axis_index("seq") * lax.axis_size("batch") + lax.axis_index("batch")
    for n in reversed(range(LAYERS)):
        g, large[n], parts = backward(g, saved[n], pos, keep)
        sizes = [p.size for p in parts]
        flat = lax.psum(jnp.concatenate([p.reshape(-1) for p in parts]), BOTH)
        pieces = []
        start = 0
        for p, size in zip(parts, sizes):
            pieces.append(flat[start : start + size].reshape(p.shape))
            start += size
        small[n] = pieces

    def own(values, axis):
        size = values.shape[axis] // (lax.axis_size("seq") * lax.axis_size("batch"))
        return lax.dynamic_slice_in_dim(values, place * size, size, axis)

    big = [jnp.stack([layer[m] for layer in large]) for m in range(4)]
    ff = big[2].shape[2] // 2
    big[2:3] = [big[2][..., :ff], big[2][..., ff:]]
    tiny = [jnp.stack([small[n][m] for n in range(LAYERS)]) for m in range(6)]
    return (
        mixed[None], g[None], big[0], own(tiny[0], 2), own(tiny[1], 1), tiny[2], tiny[3], big[1],
        own(tiny[4], 1), own(tiny[5], 1), big[2], big[3], big[4],
    )


def solution(mesh):
    rows = P(None, BOTH, None)
    vector = P(None, BOTH)
    cols = P(None, None, BOTH)
    stream = P("batch", "seq", None)
    return jax.shard_map(
        fast_body if (mesh.shape["seq"], mesh.shape["batch"]) == (8, 4) else general_body,
        mesh=mesh,
        in_specs=(
            stream, rows, cols, rows, P(), P(), rows, vector, vector, rows, rows, rows, P("batch", None), stream,
        ),
        out_specs=(stream, stream, rows, cols, rows, P(), P(), rows, vector, vector, rows, rows, rows),
        check_vma=False,
    )
```

```python
from collections import namedtuple
from types import SimpleNamespace

import jax
import jax.numpy as jnp
from jax import lax
from jax.experimental import pallas as pl
from jax.experimental.pallas import tpu as pltpu
from jax.sharding import PartitionSpec as P

D = 1024
HEADS = 8
HEAD_DIM = 128
CONV = 4
STRETCH = 64
LAYERS = 2
EPSILON = 1e-06
BF = jnp.bfloat16
F32 = jnp.float32
BOTH = ("seq", "batch")
VMEM_BYTES = 56 * 1024 * 1024
BACK_BYTES = 63 * 1024 * 1024


def dot(a, b):
    return lax.dot_general(a.astype(BF), b.astype(BF), (((1,), (0,)), ((), ())), preferred_element_type=F32)


def dot_t(a, b):
    return lax.dot_general(a.astype(BF), b.astype(BF), (((1,), (1,)), ((), ())), preferred_element_type=F32)


def t_dot(a, b):
    return lax.dot_general(a.astype(BF), b.astype(BF), (((0,), (0,)), ((), ())), preferred_element_type=F32)


def rms_scale(values, gain):
    return values * lax.rsqrt(jnp.mean(values * values, axis=-1, keepdims=True) + EPSILON) * gain


def rms_back(values, gain, grad):
    r = lax.rsqrt(jnp.mean(values * values, axis=-1, keepdims=True) + EPSILON)
    unit = values * r
    scaled = grad * gain
    back = r * (scaled - unit * jnp.mean(scaled * unit, axis=-1, keepdims=True))
    return back, grad * unit


def masks(rows):
    i = lax.broadcasted_iota(jnp.int32, (rows, rows), 0)
    j = lax.broadcasted_iota(jnp.int32, (rows, rows), 1)
    same = (i // STRETCH) == (j // STRETCH)
    strict = same & (i > j)
    causal = same & (i >= j)
    return i, j, strict, causal


def conv_rows(rows, before, taps, pos):
    total = rows.shape[0]
    padded = jnp.concatenate([before, rows], axis=0)
    acc = taps[CONV - 1 : CONV] * rows
    for tap in range(CONV - 1):
        offset = CONV - 1 - tap
        shifted = padded[8 - offset : 8 - offset + total]
        acc = acc + taps[tap : tap + 1] * jnp.where(pos >= offset, shifted, 0.0)
    return acc, padded


def unit_rows(values):
    return values * lax.rsqrt(jnp.sum(values * values, axis=-1, keepdims=True) + EPSILON)


def lane_span(start):
    return pl.ds(start if isinstance(start, int) else pl.multiple_of(start, HEAD_DIM), HEAD_DIM)


def columns(ref, start):
    return ref[:, lane_span(start)]


def head_column(ref, head):
    values = ref[...]
    lane = lax.broadcasted_iota(jnp.int32, values.shape, 1)
    return jnp.sum(jnp.where(lane == head, values, 0.0), axis=1, keepdims=True)


def inverse_less_one(lower, i, j):
    near = (i // 16) == (j // 16)
    base = jnp.where(near, lower, 0.0)
    r = -base
    power = base
    for _ in range(3):
        power = dot(power, power)
        r = r + power + dot(r, power)
    for width in (32, 64):
        step = ((i // width) == (j // width)) & ((i // (width // 2)) != (j // (width // 2)))
        m = jnp.where(step, lower, 0.0)
        y = m + dot(r, m)
        r = r - y - dot(y, r)
    return r


def local_heads(heads, keep_ref, pos_ref, beta_ref, proj_ref, before_ref, taps_ref, o_ref, eff_ref, tot_ref, inv_ref, st_ref):
    rows = proj_ref.shape[0]
    i, j, strict, causal = masks(rows)
    pos = pos_ref[...]
    for head in heads:
        parts = []
        for third in range(3):
            start = third * D + head * HEAD_DIM
            acc, _ = conv_rows(
                columns(proj_ref, start), columns(before_ref, start).astype(F32)[8:],
                columns(taps_ref, start).astype(F32), pos,
            )
            parts.append(acc * jax.nn.sigmoid(acc))
        q = (unit_rows(parts[0]) * HEAD_DIM ** (-0.5)).astype(BF)
        k32 = unit_rows(parts[1])
        k = k32.astype(BF)
        beta = head_column(beta_ref, head)
        lower = jnp.where(strict, beta * dot_t(k, k), 0.0)
        inv = inverse_less_one(lower, i, j).astype(BF)
        inv_ref[head] = inv
        x = jnp.concatenate([beta * k32, beta * parts[2]], axis=1)
        wu = x + dot(inv, x)
        w = wu[:, :HEAD_DIM].astype(BF)
        u = wu[:, HEAD_DIM:]
        scores = jnp.where(causal, dot_t(q, k), 0.0).astype(BF)
        ii = lax.broadcasted_iota(jnp.int32, (HEAD_DIM, 2 * HEAD_DIM), 0)
        jj = lax.broadcasted_iota(jnp.int32, (HEAD_DIM, 2 * HEAD_DIM), 1)
        state = jnp.where(ii + HEAD_DIM == jj, 1.0, 0.0)
        lanes = lane_span(head * HEAD_DIM)
        for c in range(rows // STRETCH):
            s = slice(c * STRETCH, (c + 1) * STRETCH)
            state = state * keep_ref[c]
            low = state.astype(BF)
            st_ref[head, c] = low
            both = dot(jnp.concatenate([w[s], q[s]], axis=0), low)
            fresh = -both[:STRETCH]
            fresh = jnp.concatenate([fresh[:, :HEAD_DIM] + u[s], fresh[:, HEAD_DIM:]], axis=1).astype(BF)
            out = both[STRETCH:] + dot(scores[s, s], fresh)
            state = state + t_dot(k[s], fresh)
            o_ref[s, lanes] = out[:, :HEAD_DIM]
            eff_ref[s, lanes] = out[:, HEAD_DIM:].astype(BF)
        tot_ref[head] = state


def local_kernel(*refs):
    @pl.loop(0, HEADS // 2)
    def _(pair):
        local_heads([pair * 2, pair * 2 + 1], *refs)


def full(shape):
    return pl.BlockSpec(shape, lambda h: (0,) * len(shape))


def local_call(keep, pos, beta, proj, before, taps):
    rows = proj.shape[0]
    count = rows // STRETCH
    whole = pl.BlockSpec(memory_space=pltpu.VMEM)
    return pl.pallas_call(
        local_kernel,
        in_specs=[pl.BlockSpec(memory_space=pltpu.SMEM)] + [whole] * 5,
        out_specs=[whole] * 5,
        out_shape=[
            jax.ShapeDtypeStruct((rows, D), F32),
            jax.ShapeDtypeStruct((rows, D), BF),
            jax.ShapeDtypeStruct((HEADS, HEAD_DIM, 2 * HEAD_DIM), F32),
            jax.ShapeDtypeStruct((HEADS, rows, rows), BF),
            jax.ShapeDtypeStruct((HEADS, count, HEAD_DIM, 2 * HEAD_DIM), BF),
        ],
        compiler_params=pltpu.CompilerParams(vmem_limit_bytes=VMEM_BYTES),
        name="delta_local",
    )(keep, pos, beta, proj, before, taps)


def back_heads(
    heads, keep_ref, pos_ref, beta_ref, proj_ref, before_ref, taps_ref, inv_ref, st_ref, sin_ref, ds_ref, do_ref,
    dproj_ref, tail_ref, dbefore_ref, dtaps_ref, dbeta_ref,
):
    rows = proj_ref.shape[0]
    count = rows // STRETCH
    i, j, strict, causal = masks(rows)
    pos = pos_ref[...]
    for head in heads:
        lanes = lane_span(head * HEAD_DIM)
        raw, act, padded = [], [], []
        for third in range(3):
            start = third * D + head * HEAD_DIM
            acc, pad = conv_rows(columns(proj_ref, start), columns(before_ref, start).astype(F32)[8:], columns(taps_ref, start).astype(F32), pos)
            raw.append(acc)
            act.append(acc * jax.nn.sigmoid(acc))
            padded.append(pad)
        rq = lax.rsqrt(jnp.sum(act[0] * act[0], axis=-1, keepdims=True) + EPSILON)
        rk = lax.rsqrt(jnp.sum(act[1] * act[1], axis=-1, keepdims=True) + EPSILON)
        q = (act[0] * rq * HEAD_DIM ** (-0.5)).astype(BF)
        k32 = act[1] * rk
        k = k32.astype(BF)
        beta = head_column(beta_ref, head)
        gram = jnp.where(strict, dot_t(k, k), 0.0)
        inv = inv_ref[head]
        x = jnp.concatenate([beta * k32, beta * act[2]], axis=1)
        wu = x + dot(inv, x)
        w = wu[:, :HEAD_DIM].astype(BF)
        u = wu[:, HEAD_DIM:]
        scores = jnp.where(causal, dot_t(q, k), 0.0).astype(BF)
        dout = do_ref[:, lanes]
        sin = sin_ref[head].astype(BF)
        states, fresh = [], []
        for c in range(count):
            s = slice(c * STRETCH, (c + 1) * STRETCH)
            packed = st_ref[head, c]
            state = (packed[:, :HEAD_DIM].astype(F32) + dot(packed[:, HEAD_DIM:], sin)).astype(BF)
            states.append(state)
            fresh.append((u[s] - dot(w[s], state)).astype(BF))
        fresh_all = jnp.concatenate(fresh, axis=0)
        dscores = jnp.where(causal, dot_t(dout, fresh_all), 0.0).astype(BF)
        dfresh0 = t_dot(scores, dout)
        ds = ds_ref[head].astype(F32)
        dfresh = [None] * count
        dk_state = [None] * count
        dq_state = [None] * count
        dw = [None] * count
        for c in reversed(range(count)):
            s = slice(c * STRETCH, (c + 1) * STRETCH)
            low = ds.astype(BF)
            part = dfresh0[s] + dot(k[s], low)
            dfresh[c] = part
            part_low = part.astype(BF)
            dk_state[c] = dot_t(fresh[c], low)
            both = dot_t(jnp.concatenate([dout[s], part_low], axis=0), states[c])
            dq_state[c] = both[:STRETCH]
            dw[c] = -both[STRETCH:]
            ds = (ds + t_dot(q[s], dout[s]) - t_dot(w[s], part_low)) * keep_ref[c]
        dfresh_all = jnp.concatenate(dfresh, axis=0)
        dq = jnp.concatenate(dq_state, axis=0) + dot(dscores, k)
        dk = jnp.concatenate(dk_state, axis=0) + t_dot(dscores, q)
        dwu = jnp.concatenate([jnp.concatenate(dw, axis=0), dfresh_all], axis=1)
        dx = dwu + t_dot(inv, dwu)
        dlower = jnp.where(strict, -dot_t(dx, wu), 0.0)
        dbeta = jnp.sum(dlower * gram, axis=1, keepdims=True)
        dxk = dx[:, :HEAD_DIM]
        dxv = dx[:, HEAD_DIM:]
        dbeta = dbeta + jnp.sum(dxk * k32 + dxv * act[2], axis=1, keepdims=True)
        dgram = (dlower * beta).astype(BF)
        dk = dk + dot(dgram, k) + t_dot(dgram, k) + beta * dxk
        dv = beta * dxv
        lane = lax.broadcasted_iota(jnp.int32, (rows, HEADS), 1)
        dbeta_ref[...] += jnp.where(lane == head, dbeta * beta * (1.0 - beta), 0.0)
        dq = dq * HEAD_DIM ** (-0.5)
        grads = (
            rq * (dq - act[0] * (rq * rq * jnp.sum(act[0] * dq, axis=-1, keepdims=True))),
            rk * (dk - k32 * jnp.sum(k32 * dk, axis=-1, keepdims=True)),
            dv,
        )
        for third in range(3):
            start = third * D + head * HEAD_DIM
            spot = lane_span(start)
            sig = jax.nn.sigmoid(raw[third])
            dmix = grads[third] * (sig + act[third] * (1.0 - sig))
            taps = columns(taps_ref, start).astype(F32)
            dpad = jnp.concatenate([jnp.zeros((8, HEAD_DIM), F32), taps[CONV - 1 : CONV] * dmix], axis=0)
            dtap = [None] * CONV
            dtap[CONV - 1] = jnp.sum(dmix * padded[third][8:], axis=0, keepdims=True)
            for tap in range(CONV - 1):
                offset = CONV - 1 - tap
                kept = jnp.where(pos >= offset, dmix, 0.0)
                dtap[tap] = jnp.sum(kept * padded[third][8 - offset : 8 - offset + rows], axis=0, keepdims=True)
                scaled = taps[tap : tap + 1] * kept
                dpad = dpad + jnp.concatenate(
                    [jnp.zeros((8 - offset, HEAD_DIM), F32), scaled, jnp.zeros((offset, HEAD_DIM), F32)], axis=0
                )
            dproj_ref[:, spot] = dpad[8:].astype(BF)
            tail_ref[:, spot] = dpad[rows - 8 :]
            dbefore_ref[:, spot] = jnp.concatenate([jnp.zeros((8, HEAD_DIM), F32), dpad[:8]], axis=0).astype(BF)
            dtaps_ref[:, spot] = jnp.concatenate(dtap, axis=0)


def back_kernel(*refs):
    refs[-1][...] = jnp.zeros_like(refs[-1])

    @pl.loop(0, HEADS // 2)
    def _(pair):
        back_heads([pair * 2, pair * 2 + 1], *refs)


def back_call(*args):
    rows = args[3].shape[0]
    whole = pl.BlockSpec(memory_space=pltpu.VMEM)
    return pl.pallas_call(
        back_kernel,
        in_specs=[pl.BlockSpec(memory_space=pltpu.SMEM)] + [whole] * (len(args) - 1),
        out_specs=[whole] * 5,
        out_shape=[
            jax.ShapeDtypeStruct((rows, 3 * D), BF),
            jax.ShapeDtypeStruct((16, 3 * D), F32),
            jax.ShapeDtypeStruct((16, 3 * D), BF),
            jax.ShapeDtypeStruct((CONV, 3 * D), F32),
            jax.ShapeDtypeStruct((rows, HEADS), F32),
        ],
        compiler_params=pltpu.CompilerParams(vmem_limit_bytes=VMEM_BYTES),
        name="delta_back",
    )(*args)


def shift(values, steps):
    count = lax.axis_size("seq")
    first, last = max(0, -steps), min(count, count - steps)
    return lax.ppermute(values, "seq", [(n, n + steps) for n in range(first, last)])


def chain(tot_b, tot_a, steps):
    peers = lax.axis_size("seq")
    state = jnp.zeros(tot_b.shape, F32)
    low_a = tot_a.astype(BF)
    for turn in range(peers - 1):
        if turn == 0:
            new = tot_b
        else:
            new = tot_b + jnp.einsum("hde,hef->hdf", low_a, state.astype(BF), preferred_element_type=F32)
        state = shift(new.astype(BF), steps).astype(F32)
    return state


def place_xy():
    seq, batch = lax.axis_index("seq"), lax.axis_index("batch")
    return lax.rem(seq, 2), lax.div(batch, 2), lax.rem(batch, 2), lax.div(seq, 2)


def blocks(width, most=512):
    return [(start, min(most, width - start)) for start in range(0, width, most)]


def load_plan(meta):
    return 1, meta[1:], 1


def start_load(meta, refs, vmem, sems):
    width = meta[2]
    copy = pltpu.make_async_copy(refs[0], vmem, sems.at[0])
    copy.start()
    cuts = blocks(width, 1408 if width % 1408 == 0 else 768 if width % 768 == 0 else 512)
    return [(start, size, start, [copy] if start == 0 else []) for start, size in cuts]


def loaded(meta, vmem, start, size):
    return vmem[:, start : start + size]


def spot_of(start, size):
    if isinstance(start, int):
        return pl.ds(start, size)
    return pl.ds(pl.multiple_of(start, 128), size)


def times(meta, left, vmem, groups, store):
    for start, size, place, copies in groups:
        for copy in copies:
            copy.wait()
        store(spot_of(place, size), dot(left, loaded(meta, vmem, start, size)))


def times_t(meta, left_ref, vmem, groups):
    total = None
    for start, size, place, copies in groups:
        for copy in copies:
            copy.wait()
        part = dot_t(left_ref[:, spot_of(place, size)], loaded(meta, vmem, start, size))
        total = part if total is None else total + part
    return total


def weight_call(kernel, metas, weights, args, out_shape, scratch, name, flops):
    counts = [load_plan(m) for m in metas]

    def run(*refs):
        refs = list(refs)
        ins = [refs.pop(0) for _ in args]
        pieces = [[refs.pop(0) for _ in range(c[0])] for c in counts]
        outs = [refs.pop(0) for _ in out_shape]
        buffers = [(refs.pop(0), refs.pop(0)) for _ in counts]
        kernel(metas, ins, pieces, outs, buffers, refs)

    whole = pl.BlockSpec(memory_space=pltpu.VMEM)
    moved = sum(a.size * a.dtype.itemsize for a in list(args) + list(out_shape))
    scratches = []
    for c in counts:
        scratches += [pltpu.VMEM(c[1], BF), pltpu.SemaphoreType.DMA((c[2],))]
    for c in counts:
        size = 2
        for n in c[1]:
            size *= n
        moved += size
    return pl.pallas_call(
        run,
        in_specs=[whole] * len(args) + [pl.BlockSpec(memory_space=pl.ANY)] * sum(c[0] for c in counts),
        out_specs=[whole] * len(out_shape),
        out_shape=out_shape,
        scratch_shapes=scratches + list(scratch),
        compiler_params=pltpu.CompilerParams(vmem_limit_bytes=VMEM_BYTES),
        cost_estimate=pl.CostEstimate(flops=flops, bytes_accessed=moved, transcendentals=0),
        name=name,
    )(*args, *[p for w in weights for p in w])


def qkv_kernel(metas, ins, pieces, outs, buffers, scratch):
    x_ref, gain_ref, wb_ref, bias_ref = ins
    h_ref, proj_ref, beta_ref, edge_ref = outs
    groups = start_load(metas[0], pieces[0], *buffers[0])
    h = rms_scale(x_ref[...], gain_ref[...].astype(F32)).astype(BF)
    h_ref[...] = h
    beta_ref[...] = jax.nn.sigmoid(dot(h, wb_ref[...]) + bias_ref[...])

    def store(spot, value):
        proj_ref[:, spot] = value
        edge_ref[:, spot] = value[-16:].astype(BF)

    times(metas[0], h, buffers[0][0], groups, store)


def out_kernel(metas, ins, pieces, outs, buffers, scratch):
    o_ref, eff_ref, state_ref, head_ref, x_ref, gain_ref = ins
    full_ref, on_ref, x1_ref, h2_ref = outs
    groups = start_load(metas[0], pieces[0], *buffers[0])
    gain = head_ref[...].astype(F32)
    for head in range(HEADS):
        s = slice(head * HEAD_DIM, (head + 1) * HEAD_DIM)
        o = o_ref[:, s] + dot(eff_ref[:, s], state_ref[head])
        full_ref[:, s] = o
        on_ref[:, s] = rms_scale(o, gain).astype(BF)

    def store(spot, value):
        x1_ref[:, spot] = x_ref[:, spot] + value

    times(metas[0], on_ref[...], buffers[0][0], groups, store)
    h2_ref[...] = rms_scale(x1_ref[...], gain_ref[...].astype(F32)).astype(BF)


def mlp_kernel(metas, ins, pieces, outs, buffers, scratch):
    h2_ref, x1_ref = ins
    gu_ref, hid_ref, x2_ref = outs
    groups = start_load(metas[0], pieces[0], *buffers[0])
    later = start_load(metas[1], pieces[1], *buffers[1])

    def store(spot, value):
        gu_ref[:, spot] = value

    times(metas[0], h2_ref[...], buffers[0][0], groups, store)
    ff = hid_ref.shape[1]
    for start, size in blocks(ff):
        gate = gu_ref[:, start : start + size]
        hid_ref[:, start : start + size] = (
            gate * jax.nn.sigmoid(gate) * gu_ref[:, ff + start : ff + start + size]
        ).astype(BF)

    def store_two(spot, value):
        x2_ref[:, spot] = x1_ref[:, spot] + value

    times(metas[1], hid_ref[...], buffers[1][0], later, store_two)


def mlp_back_kernel(metas, ins, pieces, outs, buffers, scratch):
    g_ref, gu_ref, x1_ref, gain_ref, o_ref, eff_ref, head_ref = ins
    dgu_ref, dx1_ref, dy1_ref, dmlp_ref, do_ref, ds_ref, dgain_ref = outs
    dy2_ref, dhid_ref, don_ref = scratch
    down = start_load(metas[0], pieces[0], *buffers[0])
    gate_up = start_load(metas[1], pieces[1], *buffers[1])
    out = start_load(metas[2], pieces[2], *buffers[2])
    dy2_ref[...] = g_ref[...].astype(BF)
    dhid_ref[...] = times_t(metas[0], dy2_ref, buffers[0][0], down)
    ff = dhid_ref.shape[1]
    for start, size in blocks(ff):
        s = slice(start, start + size)
        f = slice(ff + start, ff + start + size)
        gate = gu_ref[:, s]
        sig = jax.nn.sigmoid(gate)
        dhid = dhid_ref[:, s]
        act = gate * sig
        dgu_ref[:, s] = (dhid * gu_ref[:, f] * (sig + act * (1.0 - sig))).astype(BF)
        dgu_ref[:, f] = (dhid * act).astype(BF)
    dh2 = times_t(metas[1], dgu_ref, buffers[1][0], gate_up)
    back, part = rms_back(x1_ref[...], gain_ref[...].astype(F32), dh2)
    dmlp_ref[...] = jnp.sum(part, axis=0, keepdims=True)
    dx1 = g_ref[...] + back
    dx1_ref[...] = dx1
    dy1_ref[...] = dx1.astype(BF)
    don_ref[...] = times_t(metas[2], dy1_ref, buffers[2][0], out)
    gain = head_ref[...].astype(F32)
    dgain = jnp.zeros((1, HEAD_DIM), F32)
    for head in range(HEADS):
        s = slice(head * HEAD_DIM, (head + 1) * HEAD_DIM)
        back, part = rms_back(o_ref[:, s], gain, don_ref[:, s])
        dgain = dgain + jnp.sum(part, axis=0, keepdims=True)
        low = back.astype(BF)
        do_ref[:, s] = low
        ds_ref[head] = t_dot(eff_ref[:, s], low)
    dgain_ref[...] = dgain


def qkv_back_kernel(metas, ins, pieces, outs, buffers, scratch):
    dproj_ref, tail_ref, back_ref, dlogit_ref, wb_ref, x_ref, gain_ref, dx1_ref, h_ref = ins
    fixed_ref, g_ref, dmix_ref, dbeta_ref, dbias_ref = outs
    groups = start_load(metas[0], pieces[0], *buffers[0])
    rows = dproj_ref.shape[0]
    fixed_ref[: rows - 16] = dproj_ref[: rows - 16]
    fixed_ref[rows - 16 :] = (tail_ref[...] + back_ref[...].astype(F32)).astype(BF)
    dlogit = dlogit_ref[...]
    dbias_ref[...] = jnp.sum(dlogit, axis=0, keepdims=True)
    low = dlogit.astype(BF)
    dbeta_ref[...] = t_dot(h_ref[...], low)
    dh = times_t(metas[0], fixed_ref, buffers[0][0], groups) + dot_t(low, wb_ref[...])
    back, part = rms_back(x_ref[...], gain_ref[...].astype(F32), dh)
    dmix_ref[...] = jnp.sum(part, axis=0, keepdims=True)
    g_ref[...] = dx1_ref[...] + back


def gather_weights(qkv, conv, beta, out, mix, mlp, gate, up, down):
    result = []
    for n in range(qkv.shape[0]):
        rows = [lax.all_gather(a[n], BOTH, axis=0, tiled=True) for a in (beta, mix, mlp, qkv, out, gate, up, down)]
        rows[5:7] = [jnp.concatenate(rows[5:7], axis=1)]
        names = ("beta", "mix", "mlp", "qkv", "out", "gate_up", "down")
        found = dict(zip(names[:3], rows[:3]))
        found["conv"] = lax.all_gather(conv[n], BOTH, axis=1, tiled=True)
        for name, value in zip(names[3:], rows[3:]):
            found[name] = (("plain",) + value.shape, [value])
        result.append(found)
    return result


def scatter(left, right):
    value = lax.dot_general(left, right, (((0,), (0,)), ((), ())), preferred_element_type=F32)
    return lax.psum_scatter(value.astype(BF), BOTH, scatter_dimension=0, tiled=True).astype(F32)


MESH = pl.DeviceIdType.MESH


def device(x, y, core, z):
    return (z * 2 + x, y * 2 + core)


def path_place():
    x, y, core, z = place_xy()
    piece = z * 2 + core

    def at(step):
        other = (piece + step + 8) % 8
        return device(x, y, other % 2, other // 2)

    return piece, at(1), at(-1)


def partner():
    x, y, core, z = place_xy()
    return device(1 - x, y, 1 - core, z)


def signal_all(peers):
    barrier = pltpu.get_barrier_semaphore()
    for peer in peers:
        pl.semaphore_signal(barrier, inc=1, device_id=peer, device_id_type=MESH)
    pl.semaphore_wait(barrier, len(peers))


def near_peers():
    x, y, core, z = place_xy()
    peers = [device(1 - x, y, core, z), device(x, 1 - y, core, z), device(x, y, 1 - core, z)]
    return peers + [device(x, y, core, (z + k) % 4) for k in range(1, 4)]


class Gather:
    def __init__(self, mine, full, begin, cut, sends, gots):
        self.mine, self.full, self.begin, self.cut = mine, full, begin, cut
        self.sends, self.gots = sends, gots
        self.size = mine.shape[1]
        self.half = full.shape[4] // 2
        self.pending = {}

    def cols(self, core, part=None):
        start, size = self.begin, self.size
        if part == 0:
            size = self.cut
        if part == 1:
            start, size = start + self.cut, size - self.cut
        return pl.ds(pl.multiple_of(core * self.half + start, 128), size)

    def copy(self, n, src, dst, peer):
        return pltpu.make_async_remote_copy(
            src_ref=src, dst_ref=dst, send_sem=self.sends.at[n], recv_sem=self.gots.at[n],
            device_id=peer, device_id_type=MESH,
        )

    def send(self, n, source):
        self.copy(n, *source()).start()
        self.pending[n] = source

    def got(self, n, region, peer):
        self.copy(n, region, region, peer).wait_recv()

    def finish(self):
        for n, source in self.pending.items():
            self.copy(n, *source()).wait_send()

    def stages(self):
        return [self.stage_z, self.stage_one, self.stage_two, self.stage_core, self.stage_end]

    def parts(self):
        return [n for n, size in enumerate((self.cut, self.size - self.cut)) if size]

    def local(self):
        x, y, core, z = place_xy()
        return pltpu.make_async_copy(self.mine, self.full.at[z, x, y, :, self.cols(core)], self.sends.at[8])

    def stage_z(self):
        self.local().start()
        for k in range(1, 4):

            def source(k=k):
                x, y, core, z = place_xy()
                return self.mine, self.full.at[z, x, y, :, self.cols(core)], device(x, y, core, (z + k) % 4)

            self.send(k - 1, source)

    def stage_one(self):
        x, y, core, z = place_xy()
        self.local().wait()
        for k in range(1, 4):
            far = (z + 4 - k) % 4
            self.got(k - 1, self.full.at[far, x, y, :, self.cols(core)], device(x, y, core, far))
        for n in self.parts():

            def source(n=n):
                x, y, core, z = place_xy()
                spot = self.full.at[:, x, y, :, self.cols(core, n)]
                return spot, spot, device(x, 1 - y, core, z) if n else device(1 - x, y, core, z)

            self.send(3 + n, source)

    def stage_two(self):
        x, y, core, z = place_xy()
        for n in self.parts():
            if n == 0:
                self.got(3, self.full.at[:, 1 - x, y, :, self.cols(core, 0)], device(1 - x, y, core, z))
            else:
                self.got(4, self.full.at[:, x, 1 - y, :, self.cols(core, 1)], device(x, 1 - y, core, z))

            def source(n=n):
                x, y, core, z = place_xy()
                if n == 0:
                    spots = self.full.at[:, :, y, :, self.cols(core, 0)]
                else:
                    spots = self.full.at[:, x, :, :, self.cols(core, 1)]
                return spots, spots, device(1 - x, y, core, z) if n else device(x, 1 - y, core, z)

            self.send(5 + n, source)

    def stage_core(self):
        x, y, core, z = place_xy()
        for n in self.parts():
            if n == 0:
                self.got(5, self.full.at[:, :, 1 - y, :, self.cols(core, 0)], device(x, 1 - y, core, z))
            else:
                self.got(6, self.full.at[:, 1 - x, :, :, self.cols(core, 1)], device(1 - x, y, core, z))

        def source():
            x, y, core, z = place_xy()
            both = self.full.at[:, :, :, :, self.cols(core)]
            return both, both, device(x, y, 1 - core, z)

        self.send(7, source)

    def stage_end(self):
        x, y, core, z = place_xy()
        self.got(7, self.full.at[:, :, :, :, self.cols(1 - core)], device(x, y, 1 - core, z))


class Schedule:
    def __init__(self, gathers, swaps):
        self.gathers, self.swaps = gathers, swaps
        self.ready = {}
        self.turn = 0

    def tick(self, times=1):
        for _ in range(times):
            self.one_tick()

    def one_tick(self):
        for stage in reversed(range(5)):
            n = self.turn - LAGS[stage]
            if 0 <= n < len(self.gathers):
                if stage == 0:
                    self.swaps[n].wait()
                    if n in self.ready:
                        self.ready[n]()
                self.gathers[n].stages()[stage]()
        self.turn += 1

    def until(self, n):
        self.tick(max(0, n + LAGS[4] + 1 - self.turn))

    def finish(self):
        self.until(len(self.gathers) - 1)
        for gather in self.gathers:
            gather.finish()

    def save(self):
        return self.turn

    def restore(self, state):
        self.turn = state


def around(engine, times, early, middle):
    state = engine.save()

    @pl.when(early)
    def _():
        engine.tick(times)

    engine.restore(state)
    middle()

    @pl.when(jnp.logical_not(early))
    def _():
        engine.tick(times)


def swap_rows(shard, mine, begin, send, got):
    x, y, core, z = place_xy()
    size = mine.shape[1]

    def copy_of(source, target):
        return pltpu.make_async_remote_copy(
            src_ref=source, dst_ref=target, send_sem=send, recv_sem=got,
            device_id=device(x, y, 1 - core, z), device_id_type=MESH,
        )

    if len(shard) == 2:
        rows = shard[0].shape[0]
        place = pl.ds(pl.multiple_of(core * rows, rows), rows)
        for side in range(2):

            @pl.when(core == side)
            def _():
                copy_of(shard[1 - side].at[:, pl.ds(begin, size)], mine.at[place, :]).start()
                mine[place, :] = shard[side][:, pl.ds(begin, size)]

        return copy_of(shard[0].at[:, pl.ds(begin, size)], mine.at[place, :])
    shard = shard[0]
    rows = shard.shape[0]
    half = shard.shape[1] // 2
    place = pl.ds(pl.multiple_of(core * rows, rows), rows)
    copy = copy_of(shard.at[:, pl.ds(pl.multiple_of((1 - core) * half + begin, 128), size)], mine.at[place, :])
    copy.start()
    mine[place, :] = shard[:, pl.ds(pl.multiple_of(core * half + begin, 128), size)]
    return copy


def cut_chunks(rows, sizes):
    parts = []
    start = 0
    for n, size in enumerate(sizes):
        cut = (size // 128 + n % 2) // 2 * 128
        parts.append((rows, start, size, cut))
        start += size
    return parts


CHUNKS = dict(
    out=cut_chunks(64, [256] * 2),
    down=cut_chunks(176, [128] * 4),
    qkv=cut_chunks(64, [384] * 4),
    gate_up=cut_chunks(64, [384] * 6 + [256] * 2),
)
LAGS = (0, 2, 4, 6, 8, 9)


def load_columns(full, vmem, spans, sems):
    copies = []
    for n, (start, size) in enumerate(spans):
        copy = pltpu.make_async_copy(
            full.at[:, :, :, :, pl.ds(start, size)], vmem.at[:, :, :, :, pl.ds(start, size)], sems.at[n]
        )
        copy.start()
        copies.append(copy)
    return copies


def weight_columns(vmem, start, size):
    dims = vmem.shape
    return vmem[:, :, :, :, start : start + size].reshape(16 * dims[3], size)


def dma(*dims):
    return pltpu.SemaphoreType.DMA(dims)


def stream_place(r, piece, rows):
    first = r.lengths[0, 0]
    second = first + r.lengths[0, 1]
    index = piece * rows + lax.broadcasted_iota(jnp.int32, (rows, 1), 0)
    begin = jnp.where(index >= second, second, jnp.where(index >= first, first, 0))
    r.pos[...] = index - begin
    keep = []
    for start in range(0, rows, STRETCH):
        token = piece * rows + start
        new = (token == 0) | (token == first) | (token == second)
        keep.append(jnp.where(new, 0.0, 1.0))
    return keep


def gather_small(r):
    seq, batch = lax.axis_index("seq"), lax.axis_index("batch")
    me = seq * 4 + batch
    copies = []
    for k in range(1, 32):
        peer = (me + k) % 32
        copy = pltpu.make_async_remote_copy(
            src_ref=r.packed, dst_ref=r.packs.at[me], send_sem=r.small_sends.at[k - 1], recv_sem=r.small_gots.at[k - 1],
            device_id=(peer // 4, peer % 4), device_id_type=MESH,
        )
        copy.start()
        copies.append(copy)
    r.packs[me] = r.packed[...]
    return copies


def lay_out_small(r):
    rows = r.packs[:, 16:48, :].reshape(D, 128)
    i = lax.broadcasted_iota(jnp.int32, (24, 128), 0)
    j = lax.broadcasted_iota(jnp.int32, (24, 128), 1)
    r.smalls[...] = dot_t(jnp.where(i == j, 1.0, 0.0), rows)
    i = lax.broadcasted_iota(jnp.int32, (128, 384), 0)
    j = lax.broadcasted_iota(jnp.int32, (128, 384), 1)
    total = None
    for n in range(4):
        left = jnp.concatenate([r.packs[4 * q + n, 0:16, :].astype(F32)[:8] for q in range(8)], axis=0)
        part = dot(left, jnp.where((j == i + 96 * n) & (i < 96), 1.0, 0.0))
        total = part if total is None else total + part
    for q in range(8):
        for n in range(2):
            r.taps[n, :, 384 * q : 384 * (q + 1)] = total[8 * q + 4 * n : 8 * q + 4 * n + 4]


def forward_kernel(chunks, shards, fulls, mines, r):
    piece, after, before = path_place()
    x, y, core, z = place_xy()
    seq, batch = lax.axis_index("seq"), lax.axis_index("batch")
    me = seq * 4 + batch
    signal_all([((me + k) % 32 // 4, (me + k) % 32 % 4) for k in range(1, 32)])
    rows = r.x.shape[0]
    swaps, gathers = [], []
    first = {}
    schedule = Schedule(gathers, swaps)
    for n, (layer, name, part) in enumerate(chunks):
        mine = mines[n]
        first.setdefault((layer, name), n)
        shard = [ref.at[layer] for ref in shards[name]]
        if name == "down":
            half = shard[0].shape[1] // 2
            other = r.other_down.at[layer, :, pl.ds(part[1], part[2])]
            copy = pltpu.make_async_remote_copy(
                src_ref=shard[0].at[:, pl.ds(pl.multiple_of((1 - core) * half + part[1], 128), part[2])],
                dst_ref=other, send_sem=r.swap_sends.at[n], recv_sem=r.swap_gots.at[n],
                device_id=device(x, y, 1 - core, z), device_id_type=MESH,
            )
            copy.start()

            def ready(shard=shard[0], mine=mine, part=part, half=half, other=other):
                own = shard[:, pl.ds(pl.multiple_of(core * half + part[1], 128), part[2])].astype(F32)
                got = other[...].astype(F32)
                low = jnp.where(core == 0, own, got)
                high = jnp.where(core == 0, got, own)
                mine[...] = jnp.concatenate([low, high], axis=0).astype(BF)

            schedule.ready[n] = ready
        else:
            copy = swap_rows(shard, mine, part[1], r.swap_sends.at[n], r.swap_gots.at[n])
        swaps.append(copy)
        gathers.append(
            Gather(mine, fulls[layer, name], part[1], part[3], r.sends.at[n], r.gots.at[n])
        )
        if n == 3:
            small_copies = gather_small(r)
            schedule.tick()
    keep = stream_place(r, piece, rows)
    schedule.tick(2)
    for copy in small_copies:
        copy.wait()
    lay_out_small(r)
    for layer in range(LAYERS):
        forward_block(layer, first, fulls, schedule, keep, r)
    schedule.finish()
    for copy in r.puts:
        copy.wait()


def forward_block(layer, first, fulls, schedule, keep, r):
    piece, after, before = path_place()
    x_ref = r.x2 if layer else r.x
    count = {name: len(parts) for name, parts in CHUNKS.items()}

    def until(name, part):
        schedule.until(first[layer, name] + part)

    def put(*names):
        for name in names:
            n = len(r.puts)
            copy = pltpu.make_async_copy(getattr(r, name), r.saved[layer][name], r.put_sems.at[n])
            copy.start()
            r.puts.append(copy)

    until("qkv", count["qkv"] - 1)
    wb = r.smalls[8 * layer : 8 * layer + 8].astype(BF)
    mix = r.smalls[16 + layer : 17 + layer]
    mlp = r.smalls[18 + layer : 19 + layer]
    taps = r.taps.at[layer]
    spans = [(n * 768, 768) for n in range(4)]
    loads = load_columns(fulls[layer, "qkv"], r.vbig, spans, r.load_sems.at[0])
    for copy in r.puts:
        copy.wait()
    r.puts.clear()
    if layer:
        put("x2")
    h = rms_scale(x_ref[...].astype(F32), mix).astype(BF)
    r.h[...] = h
    r.beta[...] = jax.nn.sigmoid(dot_t(h, wb) + r.bias[layer].astype(F32))
    for (start, size), copy in zip(spans, loads):
        copy.wait()
        value = dot(h, weight_columns(r.vbig, start, size))
        r.proj[:, start : start + size] = value
        r.edge[:, start : start + size] = value[-16:].astype(BF)
        if start:
            schedule.tick()
    halo_ref = r.halo.at[layer]
    halo = pltpu.make_async_remote_copy(
        src_ref=r.edge, dst_ref=halo_ref, send_sem=r.halo_sems.at[0, layer], recv_sem=r.halo_sems.at[1, layer],
        device_id=after, device_id_type=MESH,
    )

    @pl.when(piece < 7)
    def _():
        halo.start()

    put("h", "proj", "beta")

    @pl.when(piece == 0)
    def _():
        halo_ref[...] = jnp.zeros_like(halo_ref)

    @pl.when(piece > 0)
    def _():
        halo.wait_recv()

    r.before[...] = halo_ref[...]
    schedule.tick()
    for head in range(0, HEADS, 2):
        local_heads(
            [head, head + 1], keep, r.pos, r.beta, r.proj, halo_ref, taps, r.o, r.eff, r.tot, r.inv, r.st,
        )
        schedule.tick(2)
    last = r.last.at[layer]
    links = [
        pltpu.make_async_remote_copy(
            src_ref=r.next.at[pl.ds(2 * n, 2)], dst_ref=last.at[pl.ds(2 * n, 2)],
            send_sem=r.chain_sends.at[layer, n], recv_sem=r.chain_gots.at[layer, n],
            device_id=after, device_id_type=MESH,
        )
        for n in range(4)
    ]

    @pl.when(piece == 0)
    def _():
        last[...] = jnp.zeros_like(last)

    def pass_on():
        for n, link in enumerate(links):

            @pl.when(piece > 0)
            def _():
                link.wait_recv()

            for head in (2 * n, 2 * n + 1):
                state = last[head]
                r.sin[head] = state
                r.a[head] = r.tot[head, :, HEAD_DIM:].astype(BF)
                r.next[head] = (r.tot[head, :, :HEAD_DIM] + dot(r.a[head], state)).astype(BF)

            @pl.when(piece < 7)
            def _():
                link.start()

    around(schedule, 2, piece >= 4, pass_on)
    put("before", "inv", "st", "eff", "sin", "a")
    until("out", count["out"] - 1)
    load = load_columns(fulls[layer, "out"], r.vout, [(0, D)], r.load_sems.at[0])
    gain = r.head[layer].astype(F32)
    for head in range(HEADS):
        s = slice(head * HEAD_DIM, (head + 1) * HEAD_DIM)
        o = r.o[:, s] + dot(r.eff[:, s], r.sin[head])
        r.o[:, s] = o
        r.on[:, s] = rms_scale(o, gain).astype(BF)
    load[0].wait()
    r.x1[...] = x_ref[...].astype(F32) + dot(r.on[...], weight_columns(r.vout, 0, D))
    h2 = rms_scale(r.x1[...], mlp).astype(BF)
    r.h2[...] = h2
    put("o", "on", "x1", "h2")
    ff = r.hid.shape[1]
    waiting = []

    def gate_up_part(start, size, loads):
        loads[0].wait()
        gate = dot(h2, weight_columns(r.vbig, start, size))
        r.gu[:, start : start + size] = gate.astype(BF)
        loads[1].wait()
        up = dot(h2, weight_columns(r.vbig, start + ff, size))
        r.gu[:, start + ff : start + ff + size] = up.astype(BF)
        r.hid[:, start : start + size] = (gate * jax.nn.sigmoid(gate) * up).astype(BF)

    for part, (_, start, size, _) in enumerate(CHUNKS["gate_up"]):
        until("gate_up", part)
        spans = [(start, size), (start + ff, size)]
        waiting.append((start, size, load_columns(fulls[layer, "gate_up"], r.vbig, spans, r.load_sems.at[part % 2])))
        if part:
            gate_up_part(*waiting.pop(0))
    gate_up_part(*waiting.pop(0))
    put("gu", "hid")
    x2 = r.mixed if layer else r.x2
    for part, (_, start, size, _) in enumerate(CHUNKS["down"]):
        until("down", part)
        spans = [(start, size), (start + D // 2, size)]
        loads = load_columns(fulls[layer, "down"], r.vdown, spans, r.load_sems.at[0])
        for (begin, wide), copy in zip(spans, loads):
            copy.wait()
            value = dot(r.hid[...], weight_columns(r.vdown, begin, wide))
            x2[:, begin : begin + wide] = (r.x1[:, begin : begin + wide] + value).astype(x2.dtype)
    if layer:
        put("mixed")

    @pl.when(piece < 7)
    def _():
        halo.wait_send()
        for link in links:
            link.wait_send()


def saved_shapes(rows, ff2):
    count = rows // STRETCH
    return dict(
        h=((rows, D), BF), proj=((rows, 3 * D), F32), beta=((rows, HEADS), F32), before=((16, 3 * D), BF),
        o=((rows, D), F32), eff=((rows, D), BF), a=((HEADS, HEAD_DIM, HEAD_DIM), BF), inv=((HEADS, rows, rows), BF),
        st=((HEADS, count, HEAD_DIM, 2 * HEAD_DIM), BF), sin=((HEADS, HEAD_DIM, HEAD_DIM), BF), on=((rows, D), BF),
        x1=((rows, D), F32), h2=((rows, D), BF), gu=((rows, ff2), BF), hid=((rows, ff2 // 2), BF),
    )


def forward_call(x, packed, lengths, bias, head, shards):
    rows = x.shape[0]
    ff2 = 2 * shards["gate_up"][0].shape[2]
    names = list(shards)
    chunks = [(n, name, part) for n in range(LAYERS) for name in names for part in CHUNKS[name]]
    whole, anywhere = pl.BlockSpec(memory_space=pltpu.VMEM), pl.BlockSpec(memory_space=pl.ANY)
    ins = dict(lengths=lengths, x=x, bias=bias, head=head, packed=packed)
    sources = [value for name in names for value in shards[name]]
    saved = saved_shapes(rows, ff2)
    layers = [saved, dict(saved, x2=((rows, D), F32), mixed=((rows, D), BF))]
    wide = dict(out=D, gate_up=ff2, down=D, qkv=3 * D)
    far = [((4, 2, 2, 176 if name == "down" else 64, wide[name]), BF) for _ in range(LAYERS) for name in names]
    outs = dict(smalls=((24, D), F32), taps=((LAYERS, CONV, 3 * D), F32))
    v = pltpu.VMEM
    scratch = {key: v(*d) for key, d in layers[1].items()}
    scratch.update(
        other_down=v((LAYERS, 88, 512), BF), vbig=v((4, 2, 2, 64, ff2), BF), vout=v((4, 2, 2, 64, D), BF),
        vdown=v((4, 2, 2, 176, D), BF), edge=v((16, 3 * D), BF), halo=v((LAYERS, 16, 3 * D), BF),
        tot=v((HEADS, HEAD_DIM, 2 * HEAD_DIM), F32), next=v((HEADS, HEAD_DIM, HEAD_DIM), BF),
        last=v((LAYERS, HEADS, HEAD_DIM, HEAD_DIM), BF), pos=v((rows, 1), jnp.int32),
        sends=dma(len(chunks), 9), gots=dma(len(chunks), 9), swap_sends=dma(len(chunks)), swap_gots=dma(len(chunks)),
        load_sems=dma(2, 4), halo_sems=dma(2, LAYERS), chain_sends=dma(LAYERS, 4), chain_gots=dma(LAYERS, 4),
        put_sems=dma(len(layers[1])), packs=v((32, 48, 128), BF), small_sends=dma(31), small_gots=dma(31),
    )
    mine = [v((part[0], part[2]), BF) for _, _, part in chunks]

    def run(*refs):
        refs = list(refs)

        def take(count):
            taken = refs[:count]
            del refs[:count]
            return taken

        r = dict(zip(ins, take(len(ins))))
        given = {name: take(len(shards[name])) for name in names}
        r.update(zip(outs, take(len(outs))))
        kept = [dict(zip(d, take(len(d)))) for d in layers]
        fulls = {(n, name): take(1)[0] for n in range(LAYERS) for name in names}
        r.update(zip(scratch, take(len(scratch))))
        forward_kernel(chunks, given, fulls, refs, SimpleNamespace(saved=kept, puts=[], **r))

    shapes = list(outs.values()) + [d for layer in layers for d in layer.values()] + far
    result = list(
        pl.pallas_call(
            run,
            in_specs=[pl.BlockSpec(memory_space=pltpu.SMEM)] + [whole] * (len(ins) - 1 + len(sources)),
            out_specs=[whole] * len(outs) + [anywhere] * (len(shapes) - len(outs)),
            out_shape=[jax.ShapeDtypeStruct(*d) for d in shapes],
            scratch_shapes=list(scratch.values()) + mine,
            compiler_params=pltpu.CompilerParams(
                collective_id=1, has_side_effects=True, vmem_limit_bytes=VMEM_BYTES
            ),
            name="forward",
        )(*ins.values(), *sources)
    )
    small = [result.pop(0) for _ in outs]
    kept = [{key: result.pop(0) for key in d} for d in layers]
    for n in range(LAYERS):
        kept[n].update({"w_" + name: result.pop(0) for name in names})
    mixed = kept[1].pop("mixed")
    kept[1]["x"] = kept[1].pop("x2")
    kept[0]["x"] = x
    return kept, small, mixed


Room = namedtuple(
    "Room", ("sent", "landing", "sums", "one_a", "one_b", "two_a", "two_b", "three", "final", "own")
)


class Scatter:
    def __init__(self, left, right, outs, rows, begin, size, cut, room, sends, gots):
        self.left, self.right, self.outs = left, right, outs
        self.rows, self.begin, self.size, self.cut = rows, begin, size, cut
        self.half = right.shape[1] // 2
        self.room, self.sends, self.gots = Room(*room), sends, gots
        self.stage = 0
        self.stages = [self.start, self.square, self.side, self.line, self.total, self.end]

    def step(self):
        self.stages[self.stage]()
        self.stage += 1
        return self.stage == len(self.stages)

    def copy(self, n, src, dst, peer):
        return pltpu.make_async_remote_copy(
            src_ref=src, dst_ref=dst, send_sem=self.sends.at[n], recv_sem=self.gots.at[n],
            device_id=peer, device_id_type=MESH,
        )

    def products(self, core, store):
        left = self.left[...]
        for start, size in blocks(self.size, 384 if self.rows == 64 else 128):
            spot = pl.multiple_of(core * self.half + self.begin + start, 128)
            store(start, size, t_dot(left, self.right[:, pl.ds(spot, size)]).reshape(4, 2, 2, self.rows, size))

    def parts(self):
        return [n for n, size in enumerate((self.cut, self.size - self.cut)) if size]

    def span(self, n):
        return (0, self.cut) if n == 0 else (self.cut, self.size - self.cut)

    def to_core(self):
        x, y, core, z = place_xy()
        cols = pl.ds(0, self.size)
        sent, landing = (ref.at[:, :, :, :, cols] for ref in (self.room.sent, self.room.landing))
        return self.copy(0, sent, landing, device(x, y, 1 - core, z))

    def ones(self):
        x, y, core, z = place_xy()
        made = []
        for n in self.parts():
            start, size = self.span(n)
            if n == 0:
                source, peer = self.room.sums.at[:, :, 1 - y, :, pl.ds(start, size)], device(x, 1 - y, core, z)
            else:
                source, peer = self.room.sums.at[:, 1 - x, :, :, pl.ds(start, size)], device(1 - x, y, core, z)
            target = (self.room.one_a, self.room.one_b)[n].at[:, :, :, pl.ds(0, size)]
            made.append(self.copy(1 + n, source, target, peer))
        return made

    def twos(self):
        x, y, core, z = place_xy()
        made = []
        for n in self.parts():
            start, size = self.span(n)
            if n == 0:
                source, peer = self.room.sums.at[:, 1 - x, y, :, pl.ds(start, size)], device(1 - x, y, core, z)
            else:
                source, peer = self.room.sums.at[:, x, 1 - y, :, pl.ds(start, size)], device(x, 1 - y, core, z)
            target = (self.room.two_a, self.room.two_b)[n].at[:, :, pl.ds(0, size)]
            made.append(self.copy(3 + n, source, target, peer))
        return made

    def threes(self):
        x, y, core, z = place_xy()
        cols = pl.ds(0, self.size)
        return [
            self.copy(
                4 + k, self.room.sums.at[(z + k) % 4, x, y, :, cols], self.room.three.at[k - 1, :, cols],
                device(x, y, core, (z + k) % 4),
            )
            for k in range(1, 4)
        ]

    def place(self, ref, core):
        if len(self.outs) == 2:
            return ref.at[:, pl.ds(self.begin, self.size)]
        return ref.at[:, pl.ds(pl.multiple_of(core * self.half + self.begin, 128), self.size)]

    def sides(self):
        core = place_xy()[2]
        if len(self.outs) == 2:
            return [(core == side, ref) for side, ref in enumerate(self.outs)]
        return [(None, self.outs[0])]

    def finals(self, ref):
        x, y, core, z = place_xy()
        cols = pl.ds(0, self.size)
        return (
            pltpu.make_async_copy(self.room.own.at[:, cols], self.place(ref, core), self.sends.at[9]),
            self.copy(8, self.room.final.at[:, cols], self.place(ref, core), device(x, y, 1 - core, z)),
        )

    def start(self):
        def store(start, size, value):
            self.room.sent[:, :, :, :, start : start + size] = value.astype(BF)

        self.products(1 - place_xy()[2], store)
        self.to_core().start()

    def square(self):
        self.to_core().wait()
        room = self.room

        def store(start, width, value):
            got = room.landing[:, :, :, :, start : start + width].astype(F32)
            room.sums[:, :, :, :, start : start + width] = (value + got).astype(BF)

        self.products(place_xy()[2], store)
        for copy in self.ones():
            copy.start()

    def side(self):
        x, y, core, z = place_xy()
        room, sums = self.room, self.room.sums
        for copy in self.ones():
            copy.wait_recv()
        for n in self.parts():
            start, size = self.span(n)
            end = start + size
            for far in range(2):
                if n == 0:
                    part = sums[:, far, pl.ds(y, 1), :, start:end][:, 0].astype(F32)
                    part = part + room.one_a[:, far, :, :size].astype(F32)
                    sums[:, far, pl.ds(y, 1), :, start:end] = part.astype(BF)[:, None]
                else:
                    part = sums[:, pl.ds(x, 1), far, :, start:end][:, 0].astype(F32)
                    part = part + room.one_b[:, far, :, :size].astype(F32)
                    sums[:, pl.ds(x, 1), far, :, start:end] = part.astype(BF)[:, None]
        for copy in self.twos():
            copy.start()

    def line(self):
        x, y, core, z = place_xy()
        room, sums = self.room, self.room.sums
        for copy in self.twos():
            copy.wait_recv()
        for n in self.parts():
            start, size = self.span(n)
            got = (room.two_a, room.two_b)[n]
            for k in range(4):
                spot = (k, pl.ds(x, 1), pl.ds(y, 1), slice(None), slice(start, start + size))
                part = sums[spot][0, 0].astype(F32) + got[k, :, :size].astype(F32)
                sums[spot] = part.astype(BF)[None, None]
        for copy in self.threes():
            copy.start()

    def total(self):
        x, y, core, z = place_xy()
        room, size = self.room, self.size
        for copy in self.threes():
            copy.wait()
        for copy in self.ones() + self.twos():
            copy.wait_send()
        own = room.sums[pl.ds(z, 1), pl.ds(x, 1), pl.ds(y, 1), :, :size][0, 0, 0].astype(F32)
        for k in range(3):
            own = own + room.three[k, :, :size].astype(F32)
        half = self.rows // 2
        low, high = own[:half], own[half:]
        room.own[:, :size] = jnp.where(core == 0, low, high)
        room.final[:, :size] = jnp.where(core == 0, high, low)
        for condition, ref in self.sides():

            def go(ref=ref):
                for copy in self.finals(ref):
                    copy.start()

            go() if condition is None else pl.when(condition)(go)

    def end(self):
        x, y, core, z = place_xy()
        for condition, ref in self.sides():

            def stay(ref=ref):
                local, away = self.finals(ref)
                local.wait()
                away.wait_send()

            def come(ref=ref):
                target = self.place(ref, 1 - core)
                self.copy(8, self.room.final.at[:, pl.ds(0, self.size)], target, device(x, y, 1 - core, z)).wait_recv()

            if condition is None:
                stay()
                come()
            else:
                pl.when(condition)(stay)
                pl.when(jnp.logical_not(condition))(come)


class SumAll:
    def __init__(self, values, out, low, got, sends, gots):
        self.values, self.out, self.low, self.got = values, out, low, got
        self.sends, self.gots = sends, gots
        self.stage = 0

    def flying(self, stage):
        x, y, core, z = place_xy()
        peers = [device(x, y, 1 - core, z), device(1 - x, y, core, z), device(x, 1 - y, core, z)]
        moves = [(stage, peers[stage])] if stage < 3 else [(2 + k, device(x, y, core, (z + k) % 4)) for k in range(1, 4)]
        return [
            pltpu.make_async_remote_copy(
                src_ref=self.low.at[stage], dst_ref=self.got.at[n], send_sem=self.sends.at[n], recv_sem=self.gots.at[n],
                device_id=peer, device_id_type=MESH,
            )
            for n, peer in moves
        ]

    def step(self):
        z = place_xy()[3]
        if self.stage:
            for copy in self.flying(self.stage - 1):
                copy.wait()
        if self.stage == 0:
            total = self.values[...]
        elif self.stage < 4:
            total = self.low[self.stage - 1].astype(F32) + self.got[self.stage - 1].astype(F32)
        else:
            total = None
            for place in range(4):
                part = self.low[3].astype(F32)
                for k in range(1, 4):
                    part = jnp.where((z + 4 - k) % 4 == place, self.got[2 + k].astype(F32), part)
                total = part if total is None else total + part
            self.out[...] = total
            return True
        self.low[self.stage] = total.astype(BF)
        for copy in self.flying(self.stage):
            copy.start()
        self.stage += 1
        return False


class Pipeline:
    def __init__(self):
        self.active, self.queue = [], []

    def add(self, *jobs):
        self.queue += jobs

    def tick(self, times=1):
        for _ in range(times):
            self.one_tick()

    def one_tick(self):
        left = []
        for entry in self.active:
            job = entry[0]
            entry[1] += 1
            due = not isinstance(job, Scatter) or entry[1] == LAGS[job.stage]
            if not (due and job.step()):
                left.append(entry)
        self.active = left
        if self.queue:
            job = self.queue.pop(0)
            job.step()
            self.active.append([job, 0])

    def drain(self):
        while self.active or self.queue:
            self.tick()

    def settle(self, jobs):
        while min(job.stage for job in jobs) < 2:
            self.tick()

    def save(self):
        return [list(entry) + [entry[0].stage] for entry in self.active], list(self.queue)

    def restore(self, state):
        self.active = [entry[:2] for entry in state[0]]
        for job, _, stage in state[0]:
            job.stage = stage
        self.queue = list(state[1])
        for job in self.queue:
            job.stage = 0


class Backward:
    def __init__(self, r):
        self.r = r
        self.pipe = Pipeline()
        self.counts = [0, 0]
        self.loads = 0

    def jobs(self, left, right, outs, parts):
        r = self.r
        made = []
        for rows_chip, begin, size, cut in parts:
            wide = rows_chip == 64
            rooms, depths = (r.wide, WIDE) if wide else (r.narrow, NARROW)
            n = self.counts[wide]
            m = sum(self.counts)
            self.counts[wide] += 1
            buffers = [buffer.at[n % depth] for buffer, depth in zip(rooms, depths)]
            if not wide:
                buffers[1], buffers[4], buffers[6] = buffers[2], buffers[3], buffers[5]
            made.append(Scatter(left, right, outs, rows_chip, begin, size, cut, buffers, r.sends.at[m], r.gots.at[m]))
        self.pipe.add(*made)
        return made

    def fetch(self, source, target):
        copy = pltpu.make_async_copy(source, target, self.r.load_sems.at[self.loads])
        copy.start()
        self.loads += 1
        return copy


def backward_kernel(r):
    piece, after, before = path_place()
    x, y, core, z = place_xy()
    signal_all(near_peers() + [after, before, partner()])
    keep = stream_place(r, piece, r.g.shape[0])
    mixed = pltpu.make_async_remote_copy(
        src_ref=r.mixed, dst_ref=r.mixed_out, send_sem=r.move_sems.at[0], recv_sem=r.move_sems.at[1],
        device_id=partner(), device_id_type=MESH,
    )
    stays = pltpu.make_async_copy(r.mixed, r.mixed_out, r.move_sems.at[2])

    @pl.when(x != core)
    def _():
        mixed.start()

    @pl.when(x == core)
    def _():
        stays.start()

    r.g_out[...] = r.g[...].astype(F32)
    shared = Backward(r)
    old = []
    for layer in reversed(range(LAYERS)):
        old = backward_block(layer, shared, keep, old, r)
    moved = pltpu.make_async_remote_copy(
        src_ref=r.g_low, dst_ref=r.g_got, send_sem=r.move_sems.at[3], recv_sem=r.move_sems.at[4],
        device_id=partner(), device_id_type=MESH,
    )

    @pl.when(x != core)
    def _():
        r.g_low[...] = r.g_out[...].astype(BF)
        moved.start()

    shared.pipe.drain()

    @pl.when(x == core)
    def _():
        stays.wait()

    @pl.when(x != core)
    def _():
        mixed.wait()
        moved.wait()
        r.g_out[...] = r.g_got[...].astype(F32)


def backward_block(layer, shared, keep, old, r):
    piece, after, before = path_place()
    saved, pipe, fetch = SimpleNamespace(**r.saved[layer]), shared.pipe, shared.fetch
    rows = r.g.shape[0]
    wb = r.smalls[8 * layer : 8 * layer + 8].astype(BF)
    mix = r.smalls[16 + layer : 17 + layer]
    mlp = r.smalls[18 + layer : 19 + layer]
    taps = r.taps.at[layer]
    values, ds, halo_ref = r.values.at[layer], r.ds.at[layer], r.halo.at[layer]
    grads = {key: [ref.at[layer] for ref in refs] for key, refs in r.grads.items()}
    hid = fetch(saved.hid, r.v_hid)
    down = [fetch(saved.w_down.at[pl.ds(0, 2)], r.vdown)]
    gu = fetch(saved.gu, r.v_gu)
    big = [fetch(saved.w_gate_up.at[n], r.vbig.at[n]) for n in range(2)]
    r.dy2[...] = r.g_out[...].astype(BF)
    made = shared.jobs(r.v_hid, r.dy2, grads["down"], CHUNKS["down"])
    hid.wait()
    pipe.tick()
    h2, x1, o, eff, on = (
        fetch(a, b)
        for a, b in ((saved.h2, r.v_h2), (saved.x1, r.v_x), (saved.o, r.v_o), (saved.eff, r.v_eff), (saved.on, r.v_on))
    )

    def fetch_rows(source, n):
        return fetch(source.at[n], r.vbig.at[n % 2, :, :, :, pl.ds(0, source.shape[4])])

    ff = r.v_hid.shape[1]
    gu.wait()
    for n in range(2):
        down[n].wait()
        dhid_all = dot_t(r.dy2[...], r.vdown[...].reshape(ff // 2, D))
        if n == 0:
            down.append(fetch(saved.w_down.at[pl.ds(2, 2)], r.vdown))
        for begin, size in blocks(ff // 2, 384):
            start = n * (ff // 2) + begin
            dhid = dhid_all[:, begin : begin + size]
            gate = r.v_gu[:, start : start + size].astype(F32)
            up = r.v_gu[:, ff + start : ff + start + size].astype(F32)
            sig = jax.nn.sigmoid(gate)
            act = gate * sig
            r.v_gu[:, start : start + size] = (dhid * up * (sig + act * (1.0 - sig))).astype(BF)
            r.v_gu[:, ff + start : ff + start + size] = (dhid * act).astype(BF)
        pipe.tick()
    h2.wait()
    made += shared.jobs(r.v_h2, r.v_gu, grads["gate_up"], CHUNKS["gate_up"])
    for n in range(4):
        big[n].wait()
        r.acc[:, n * 256 : (n + 1) * 256] = dot_t(r.v_gu[...], r.vbig[n % 2].reshape(256, 2 * ff))
        big.append(fetch_rows(saved.w_gate_up if n < 2 else saved.w_out, (n + 2) % 4))
        if n % 2:
            pipe.tick()
    x1.wait()
    back, part = rms_back(r.v_x[...], mlp, r.acc[...])
    values[9:10] = jnp.sum(part, axis=0, keepdims=True)
    r.dx1[...] = r.g_out[...] + back
    r.dy1[...] = r.dx1[...].astype(BF)
    later = [
        fetch(a, b)
        for a, b in (
            (saved.sin, r.v_sin), (saved.a, r.v_a), (saved.beta, r.v_beta), (saved.before, r.v_before),
            (saved.proj, r.v_proj), (saved.inv, r.v_inv), (saved.st, r.v_st),
            (saved.x, r.v_x if layer else r.g_low),
        )
    ]
    on.wait()
    made += shared.jobs(r.v_on, r.dy1, grads["out"], CHUNKS["out"])
    for n in range(4):
        big[4 + n].wait()
        r.acc[:, n * 256 : (n + 1) * 256] = dot_t(r.dy1[...], r.vbig[n % 2, :, :, :, :D].reshape(256, D))
        big.append(fetch_rows(saved.w_out if n < 2 else saved.w_qkv, (n + 2) % 4))
    pipe.tick()
    o.wait()
    eff.wait()
    gain = r.head[layer].astype(F32)
    dgain = jnp.zeros((1, HEAD_DIM), F32)
    for head in range(HEADS):
        s = slice(head * HEAD_DIM, (head + 1) * HEAD_DIM)
        back, part = rms_back(r.v_o[:, s], gain, r.acc[:, s])
        dgain = dgain + jnp.sum(part, axis=0, keepdims=True)
        low = back.astype(BF)
        r.do[:, s] = low
        r.ds0[head] = t_dot(r.v_eff[:, s], low)
    values[22:24] = jnp.zeros((2, D), F32)
    values[22:23, HEAD_DIM : 2 * HEAD_DIM] = dgain
    for copy in later:
        copy.wait()
    pipe.tick()
    links = [
        pltpu.make_async_remote_copy(
            src_ref=r.next.at[pl.ds(2 * n, 2)], dst_ref=ds.at[pl.ds(2 * n, 2)],
            send_sem=r.chain_sends.at[layer, n], recv_sem=r.chain_gots.at[layer, n],
            device_id=before, device_id_type=MESH,
        )
        for n in range(4)
    ]

    @pl.when(piece == 7)
    def _():
        ds[...] = jnp.zeros_like(ds)

    def pass_on():
        for n, link in enumerate(links):

            @pl.when(piece < 7)
            def _():
                link.wait_recv()

            for head in (2 * n, 2 * n + 1):
                r.next[head] = (r.ds0[head] + t_dot(r.v_a[head], ds[head])).astype(BF)

            @pl.when(piece > 0)
            def _():
                link.start()

    around(pipe, 2, piece < 4, pass_on)
    if old:
        pipe.settle(old)
    own = fetch(saved.h, r.v_h)
    r.dlogit[...] = jnp.zeros_like(r.dlogit)
    for head in range(0, HEADS, 2):
        back_heads(
            [head, head + 1], keep, r.pos, r.v_beta, r.v_proj, r.v_before, taps, r.v_inv, r.v_st,
            r.v_sin, ds, r.do, r.dproj, r.tail, r.edge, r.dtaps, r.dlogit,
        )
        pipe.tick(2)
    halo = pltpu.make_async_remote_copy(
        src_ref=r.edge, dst_ref=halo_ref, send_sem=r.halo_sems.at[0, layer], recv_sem=r.halo_sems.at[1, layer],
        device_id=before, device_id_type=MESH,
    )

    @pl.when(piece > 0)
    def _():
        halo.start()

    dlogit = r.dlogit[...]
    low = dlogit.astype(BF)
    own.wait()
    values[0:8] = t_dot(low, r.v_h[...])
    values[22:23, 0:HEADS] = jnp.sum(dlogit, axis=0, keepdims=True)
    for tap in range(CONV):
        for third in range(3):
            row = 10 + tap * 3 + third
            values[row : row + 1] = r.dtaps[tap : tap + 1, third * D : (third + 1) * D]

    @pl.when(piece == 7)
    def _():
        halo_ref[...] = jnp.zeros_like(halo_ref)

    @pl.when(piece < 7)
    def _():
        halo.wait_recv()

    r.dproj[rows - 16 :] = (r.tail[...] + halo_ref[...].astype(F32)).astype(BF)
    mine = shared.jobs(r.v_h, r.dproj, grads["qkv"], CHUNKS["qkv"])
    pipe.tick()
    for n in range(4):
        big[8 + n].wait()
        r.acc[:, n * 256 : (n + 1) * 256] = dot_t(
            r.dproj[...], r.vbig[n % 2, :, :, :, : 3 * D].reshape(256, 3 * D)
        ) + dot(low, wb[:, n * 256 : (n + 1) * 256])
        if n < 2:
            big.append(fetch_rows(saved.w_qkv, n + 2))
        if n % 2:
            pipe.tick()
    x_in = r.v_x[...] if layer else r.g_low[...].astype(F32)
    back, part = rms_back(x_in, mix, r.acc[...])
    values[8:9] = jnp.sum(part, axis=0, keepdims=True)
    r.g_out[...] = r.dx1[...] + back
    pipe.add(
        SumAll(
            values, r.small.at[layer], r.small_low.at[layer], r.small_got.at[layer],
            r.small_sends.at[layer], r.small_gots.at[layer],
        )
    )
    pipe.settle(made)

    @pl.when(piece > 0)
    def _():
        halo.wait_send()
        for link in links:
            link.wait_send()

    return mine


WIDE = (2, 4, 6, 4, 4, 4, 4, 4, 1, 1)
NARROW = (2, 1, 4, 4, 1, 4, 1, 4, 1, 1)


def rooms(depths, rows, size):
    half = (size // 128 + 1) // 2 * 128
    dims = (
        (4, 2, 2, rows, size), (4, 2, 2, rows, size), (4, 2, 2, rows, size), (4, 2, rows, half), (4, 2, rows, half),
        (4, rows, half), (4, rows, half), (3, rows, size), (rows // 2, size),
        (rows // 2, size),
    )
    return [pltpu.VMEM((depth,) + d, F32 if n >= 8 else BF) for n, (depth, d) in enumerate(zip(depths, dims))]


def backward_call(g, saved, small, mixed, lengths, head):
    rows = g.shape[0]
    count = rows // STRETCH
    ff2 = saved[0]["gu"].shape[1]
    whole, anywhere = pl.BlockSpec(memory_space=pltpu.VMEM), pl.BlockSpec(memory_space=pl.ANY)
    vmem = dict(head=head, g=g, smalls=small[0], taps=small[1])
    keys = [key for key in saved[0]]
    hbm = [layer[key] for layer in saved for key in keys]
    outs = dict(small=((LAYERS, 24, D), F32), g_out=((rows, D), F32))
    far = [
        ((rows, D), BF), ((LAYERS, 32, 3 * D), F32), ((LAYERS, 32, D), F32), ((LAYERS, 32, ff2 // 2), F32),
        ((LAYERS, 32, ff2 // 2), F32), ((LAYERS, 88, D), F32),
    ]
    v = pltpu.VMEM
    scratch = dict(
        v_gu=v((rows, ff2), BF), v_x=v((rows, D), F32), v_hid=v((rows, ff2 // 2), BF), v_h2=v((rows, D), BF),
        v_o=v((rows, D), F32), v_eff=v((rows, D), BF), v_on=v((rows, D), BF), v_proj=v((rows, 3 * D), F32),
        v_inv=v((HEADS, rows, rows), BF), v_st=v((HEADS, count, HEAD_DIM, 2 * HEAD_DIM), BF),
        v_sin=v((HEADS, HEAD_DIM, HEAD_DIM), BF), v_a=v((HEADS, HEAD_DIM, HEAD_DIM), BF), v_h=v((rows, D), BF),
        v_beta=v((rows, HEADS), F32), v_before=v((16, 3 * D), BF),
        acc=v((rows, D), F32), dy2=v((rows, D), BF), dy1=v((rows, D), BF), dx1=v((rows, D), F32), do=v((rows, D), BF),
        ds=v((LAYERS, HEADS, HEAD_DIM, HEAD_DIM), BF), next=v((HEADS, HEAD_DIM, HEAD_DIM), BF),
        ds0=v((HEADS, HEAD_DIM, HEAD_DIM), F32), tail=v((16, 3 * D), F32), edge=v((16, 3 * D), BF),
        halo=v((LAYERS, 16, 3 * D), BF), dtaps=v((CONV, 3 * D), F32), dlogit=v((rows, HEADS), F32),
        values=v((LAYERS, 24, D), F32), small_low=v((LAYERS, 4, 24, D), BF), small_got=v((LAYERS, 6, 24, D), BF),
        vdown=v((2, 2, 2, 176, D), BF), vbig=v((2, 2, 2, 64, ff2), BF), dproj=v((rows, 3 * D), BF),
        g_low=v((rows, D), BF), g_got=v((rows, D), BF), pos=v((rows, 1), jnp.int32),
        sends=dma(36, 10), gots=dma(36, 10), small_sends=dma(LAYERS, 6), small_gots=dma(LAYERS, 6), load_sems=dma(80),
        halo_sems=dma(2, LAYERS), chain_sends=dma(LAYERS, 4), chain_gots=dma(LAYERS, 4), move_sems=dma(5),
    )
    wide, narrow = rooms(WIDE, 64, 384), rooms(NARROW, 176, 128)

    def run(*refs):
        refs = list(refs)

        def take(count):
            taken = refs[:count]
            del refs[:count]
            return taken

        r = dict(lengths=take(1)[0], **dict(zip(vmem, take(len(vmem)))))
        kept = [dict(zip(keys, take(len(keys)))) for _ in saved]
        r["mixed"] = take(1)[0]
        r.update(zip(outs, take(len(outs))))
        r["mixed_out"], qkv, out, gate, up, down = take(len(far))
        r.update(zip(scratch, take(len(scratch))))
        r["wide"], r["narrow"] = take(len(wide)), take(len(narrow))
        r["grads"] = dict(qkv=[qkv], out=[out], gate_up=[gate, up], down=[down])
        backward_kernel(SimpleNamespace(saved=kept, **r))

    return pl.pallas_call(
        run,
        in_specs=[pl.BlockSpec(memory_space=pltpu.SMEM)] + [whole] * len(vmem) + [anywhere] * (len(hbm) + 1),
        out_specs=[whole] * len(outs) + [anywhere] * len(far),
        out_shape=[jax.ShapeDtypeStruct(*d) for d in list(outs.values()) + far],
        scratch_shapes=list(scratch.values()) + wide + narrow,
        compiler_params=pltpu.CompilerParams(
            collective_id=2, has_side_effects=True, vmem_limit_bytes=BACK_BYTES
        ),
        name="backward",
    )(lengths, *vmem.values(), *hbm, mixed)


def shape(dims, dtype):
    return jax.ShapeDtypeStruct(dims, dtype)


def forward(x, w, bias, head_gain, pos, keep):
    rows = x.shape[0]
    metas = {name: w[name][0] for name in ("qkv", "out", "gate_up", "down")}
    width, ff2 = metas["qkv"][2], metas["gate_up"][2]
    h, proj, beta, edge = weight_call(
        qkv_kernel, [metas["qkv"]], [w["qkv"][1]], (x, w["mix"][None], w["beta"], bias),
        [shape((rows, D), BF), shape((rows, width), F32), shape((rows, HEADS), F32), shape((16, width), BF)],
        [], "norm_qkv", 2 * rows * D * width,
    )
    before = shift(edge, 1)
    o, eff, tot, inv, st = local_call(keep, pos, beta, proj, before, w["conv"])
    sin = chain(tot[:, :, :HEAD_DIM], tot[:, :, HEAD_DIM:], 1)
    o, on, x1, h2 = weight_call(
        out_kernel, [metas["out"]], [w["out"][1]], (o, eff, sin, head_gain, x, w["mlp"][None]),
        [shape((rows, D), F32), shape((rows, D), BF), shape((rows, D), F32), shape((rows, D), BF)],
        [], "head_out", 2 * rows * D * D,
    )
    gu, hid, x2 = weight_call(
        mlp_kernel, [metas["gate_up"], metas["down"]], [w["gate_up"][1], w["down"][1]], (h2, x1),
        [shape((rows, ff2), F32), shape((rows, ff2 // 2), BF), shape((rows, D), F32)],
        [], "mlp", 3 * rows * D * ff2,
    )
    kept = dict(
        x=x, h=h, proj=proj, before=before, beta=beta, o=o, eff=eff, a=tot[:, :, HEAD_DIM:],
        inv=inv, st=st, sin=sin, head_gain=head_gain, on=on, x1=x1, h2=h2, gu=gu, hid=hid, w=w,
    )
    return x2, kept


def backward(g, kept, pos, keep):
    w = kept["w"]
    rows = g.shape[0]
    metas = {name: w[name][0] for name in ("qkv", "out", "gate_up", "down")}
    width, ff2 = metas["qkv"][2], metas["gate_up"][2]
    d_down = scatter(kept["hid"], g.astype(BF))
    dgu, dx1, dy1, d_mlp, do, ds0, d_head = weight_call(
        mlp_back_kernel,
        [metas["down"], metas["gate_up"], metas["out"]],
        [w["down"][1], w["gate_up"][1], w["out"][1]],
        (g, kept["gu"], kept["x1"], w["mlp"][None], kept["o"], kept["eff"], kept["head_gain"]),
        [
            shape((rows, ff2), BF), shape((rows, D), F32), shape((rows, D), BF), shape((1, D), F32),
            shape((rows, D), BF), shape((HEADS, HEAD_DIM, HEAD_DIM), F32), shape((1, HEAD_DIM), F32),
        ],
        [pltpu.VMEM((rows, D), BF), pltpu.VMEM((rows, ff2 // 2), F32), pltpu.VMEM((rows, D), F32)],
        "mlp_back", 3 * rows * D * ff2,
    )
    d_gate_up = scatter(kept["h2"], dgu)
    d_out = scatter(kept["on"], dy1)
    ds = chain(ds0, jnp.swapaxes(kept["a"], 1, 2), -1)
    dproj, tail, dbefore, dtaps, dlogit = back_call(
        keep, pos, kept["beta"], kept["proj"], kept["before"], w["conv"],
        kept["inv"], kept["st"], kept["sin"], ds, do,
    )
    returned = shift(dbefore, -1)
    dproj, g, d_mix, d_beta, d_bias = weight_call(
        qkv_back_kernel, [metas["qkv"]], [w["qkv"][1]],
        (dproj, tail, returned, dlogit, w["beta"], kept["x"], w["mix"][None], dx1, kept["h"]),
        [
            shape((rows, width), BF), shape((rows, D), F32), shape((1, D), F32), shape((D, HEADS), F32),
            shape((1, HEADS), F32),
        ],
        [], "qkv_back", 2 * rows * D * width,
    )
    d_qkv = scatter(kept["h"], dproj)
    large = (d_qkv, d_out, d_gate_up, d_down)
    small = (dtaps, d_beta, d_bias[0], d_head[0], d_mix[0], d_mlp[0])
    return g, large, small


def fast_body(
    tokens, qkv_weight, conv_weight, beta_weight, beta_bias, head_gain, out_weight, mixer_gain, mlp_gain,
    gate_weight, up_weight, down_weight, lengths, cotangent,
):
    pairs = []
    for seq in range(8):
        for batch in range(4):
            z, x, y, core = seq // 2, seq % 2, batch // 2, batch % 2
            pairs.append((seq * 4 + batch, (z * 2 + core) * 4 + y * 2 + x))
    tokens, cotangent, lengths = (lax.ppermute(v, BOTH, pairs) for v in (tokens[0], cotangent[0], lengths))
    conv = jnp.pad(conv_weight.reshape(LAYERS * CONV, -1), ((0, 8), (0, 32)))
    columns_of = jnp.concatenate([beta_weight[0], beta_weight[1], mixer_gain.T, mlp_gain.T], axis=1)
    packed = jnp.concatenate([conv, jnp.pad(columns_of, ((0, 0), (0, 128 - columns_of.shape[1])))], axis=0)
    bias, head = beta_bias[:, None], head_gain[:, None]
    shards = dict(qkv=(qkv_weight,), out=(out_weight,), gate_up=(gate_weight, up_weight), down=(down_weight,))
    saved, small, mixed = forward_call(tokens, packed, lengths, bias, head, shards)
    tiny, g, mixed, *large = backward_call(cotangent, saved, small, mixed, lengths, head)
    place = lax.axis_index("seq") * lax.axis_size("batch") + lax.axis_index("batch")

    def own(values, axis):
        return lax.dynamic_slice_in_dim(values, place * (values.shape[axis] // 32), values.shape[axis] // 32, axis)

    beta = jnp.swapaxes(own(tiny[:, 0:8], 2), 1, 2)
    return (
        mixed[None], g[None], large[0], own(tiny[:, 10:22].reshape(LAYERS, CONV, -1), 2),
        beta, tiny[:, 22, :HEADS], tiny[:, 22, HEAD_DIM : 2 * HEAD_DIM], large[1], own(tiny[:, 8], 1),
        own(tiny[:, 9], 1), large[2], large[3], large[4],
    )


def general_body(
    tokens, qkv_weight, conv_weight, beta_weight, beta_bias, head_gain, out_weight, mixer_gain, mlp_gain,
    gate_weight, up_weight, down_weight, lengths, cotangent,
):
    rows = tokens.shape[1]
    tokens, cotangent = tokens[0], cotangent[0]
    index = lax.axis_index("seq") * rows + jnp.arange(rows, dtype=jnp.int32)
    seq_lengths = lengths[0]
    starts = jnp.cumsum(seq_lengths) - seq_lengths
    begin = jnp.max(jnp.where(starts[None, :] <= index[:, None], starts[None, :], 0), axis=1)
    positions = (index - begin).astype(jnp.int32)
    keep = (positions[::STRETCH] != 0).astype(F32)
    pos = positions[:, None]
    x = tokens.astype(F32)
    saved = []
    weights = gather_weights(
        qkv_weight, conv_weight, beta_weight, out_weight, mixer_gain, mlp_gain, gate_weight, up_weight, down_weight
    )
    for n in range(LAYERS):
        x, kept = forward(x, weights[n], beta_bias[n].astype(F32)[None], head_gain[n][None], pos, keep)
        saved.append(kept)
    mixed = x.astype(BF)
    g = cotangent.astype(F32)
    large = [None] * LAYERS
    small = [None] * LAYERS
    place = lax.axis_index("seq") * lax.axis_size("batch") + lax.axis_index("batch")
    for n in reversed(range(LAYERS)):
        g, large[n], parts = backward(g, saved[n], pos, keep)
        sizes = [p.size for p in parts]
        flat = lax.psum(jnp.concatenate([p.reshape(-1) for p in parts]), BOTH)
        pieces = []
        start = 0
        for p, size in zip(parts, sizes):
            pieces.append(flat[start : start + size].reshape(p.shape))
            start += size
        small[n] = pieces

    def own(values, axis):
        size = values.shape[axis] // (lax.axis_size("seq") * lax.axis_size("batch"))
        return lax.dynamic_slice_in_dim(values, place * size, size, axis)

    big = [jnp.stack([layer[m] for layer in large]) for m in range(4)]
    ff = big[2].shape[2] // 2
    big[2:3] = [big[2][..., :ff], big[2][..., ff:]]
    tiny = [jnp.stack([small[n][m] for n in range(LAYERS)]) for m in range(6)]
    return (
        mixed[None], g[None], big[0], own(tiny[0], 2), own(tiny[1], 1), tiny[2], tiny[3], big[1],
        own(tiny[4], 1), own(tiny[5], 1), big[2], big[3], big[4],
    )


def solution(mesh):
    rows = P(None, BOTH, None)
    vector = P(None, BOTH)
    cols = P(None, None, BOTH)
    stream = P("batch", "seq", None)
    return jax.shard_map(
        fast_body if (mesh.shape["seq"], mesh.shape["batch"]) == (8, 4) else general_body,
        mesh=mesh,
        in_specs=(
            stream, rows, cols, rows, P(), P(), rows, vector, vector, rows, rows, rows, P("batch", None), stream,
        ),
        out_specs=(stream, stream, rows, cols, rows, P(), P(), rows, vector, vector, rows, rows, rows),
        check_vma=False,
    )
```

```python
from collections import namedtuple
from types import SimpleNamespace

import jax
import jax.numpy as jnp
from jax import lax
from jax.experimental import pallas as pl
from jax.experimental.pallas import tpu as pltpu
from jax.sharding import PartitionSpec as P

D = 1024
HEADS = 8
HEAD_DIM = 128
CONV = 4
STRETCH = 64
LAYERS = 2
EPSILON = 1e-06
BF = jnp.bfloat16
F32 = jnp.float32
BOTH = ("seq", "batch")
VMEM_BYTES = 56 * 1024 * 1024
BACK_BYTES = 63 * 1024 * 1024


def dot(a, b):
    return lax.dot_general(a.astype(BF), b.astype(BF), (((1,), (0,)), ((), ())), preferred_element_type=F32)


def dot_t(a, b):
    return lax.dot_general(a.astype(BF), b.astype(BF), (((1,), (1,)), ((), ())), preferred_element_type=F32)


def t_dot(a, b):
    return lax.dot_general(a.astype(BF), b.astype(BF), (((0,), (0,)), ((), ())), preferred_element_type=F32)


def two_parts(values):
    high = values.astype(BF)
    return high, (values - high.astype(F32)).astype(BF)


def dot_fine(a, b):
    high, low = two_parts(b)
    return dot(a, high) + dot(a, low)


def dot_t_fine(a, b):
    high, low = two_parts(b)
    return dot_t(a, high) + dot_t(a, low)


def rms_scale(values, gain):
    return values * lax.rsqrt(jnp.mean(values * values, axis=-1, keepdims=True) + EPSILON) * gain


def rms_back(values, gain, grad):
    r = lax.rsqrt(jnp.mean(values * values, axis=-1, keepdims=True) + EPSILON)
    unit = values * r
    scaled = grad * gain
    back = r * (scaled - unit * jnp.mean(scaled * unit, axis=-1, keepdims=True))
    return back, grad * unit


def masks(rows):
    i = lax.broadcasted_iota(jnp.int32, (rows, rows), 0)
    j = lax.broadcasted_iota(jnp.int32, (rows, rows), 1)
    same = (i // STRETCH) == (j // STRETCH)
    strict = same & (i > j)
    causal = same & (i >= j)
    return i, j, strict, causal


def conv_rows(rows, before, taps, pos):
    total = rows.shape[0]
    padded = jnp.concatenate([before, rows], axis=0)
    acc = taps[CONV - 1 : CONV] * rows
    for tap in range(CONV - 1):
        offset = CONV - 1 - tap
        shifted = padded[8 - offset : 8 - offset + total]
        acc = acc + taps[tap : tap + 1] * jnp.where(pos >= offset, shifted, 0.0)
    return acc, padded


def unit_rows(values):
    return values * lax.rsqrt(jnp.sum(values * values, axis=-1, keepdims=True) + EPSILON)


def lane_span(start):
    return pl.ds(start if isinstance(start, int) else pl.multiple_of(start, HEAD_DIM), HEAD_DIM)


def columns(ref, start):
    return ref[:, lane_span(start)]


def head_column(ref, head):
    values = ref[...]
    lane = lax.broadcasted_iota(jnp.int32, values.shape, 1)
    return jnp.sum(jnp.where(lane == head, values, 0.0), axis=1, keepdims=True)


def inverse_less_one(lower, i, j):
    near = (i // 16) == (j // 16)
    base = jnp.where(near, lower, 0.0)
    r = -base
    power = base
    for _ in range(3):
        power = dot(power, power)
        r = r + power + dot(r, power)
    for width in (32, 64):
        step = ((i // width) == (j // width)) & ((i // (width // 2)) != (j // (width // 2)))
        m = jnp.where(step, lower, 0.0)
        y = m + dot(r, m)
        r = r - y - dot(y, r)
    return r


def local_heads(heads, keep_ref, pos_ref, beta_ref, proj_ref, before_ref, taps_ref, o_ref, eff_ref, tot_ref, inv_ref, st_ref):
    rows = proj_ref.shape[0]
    i, j, strict, causal = masks(rows)
    pos = pos_ref[...]
    for head in heads:
        parts = []
        for third in range(3):
            start = third * D + head * HEAD_DIM
            acc, _ = conv_rows(
                columns(proj_ref, start), columns(before_ref, start).astype(F32)[8:],
                columns(taps_ref, start).astype(F32), pos,
            )
            parts.append(acc * jax.nn.sigmoid(acc))
        q = (unit_rows(parts[0]) * HEAD_DIM ** (-0.5)).astype(BF)
        k32 = unit_rows(parts[1])
        k = k32.astype(BF)
        beta = head_column(beta_ref, head)
        lower = jnp.where(strict, beta * dot_t(k, k), 0.0)
        inv = inverse_less_one(lower, i, j).astype(BF)
        inv_ref[head] = inv
        x = jnp.concatenate([beta * k32, beta * parts[2]], axis=1)
        wu = x + dot(inv, x)
        w = wu[:, :HEAD_DIM].astype(BF)
        u = wu[:, HEAD_DIM:]
        scores = jnp.where(causal, dot_t(q, k), 0.0).astype(BF)
        ii = lax.broadcasted_iota(jnp.int32, (HEAD_DIM, 2 * HEAD_DIM), 0)
        jj = lax.broadcasted_iota(jnp.int32, (HEAD_DIM, 2 * HEAD_DIM), 1)
        one = jnp.where(ii + HEAD_DIM == jj, 1.0, 0.0)
        state = jnp.zeros_like(one)
        lanes = lane_span(head * HEAD_DIM)
        for c in range(rows // STRETCH):
            s = slice(c * STRETCH, (c + 1) * STRETCH)
            state = state * keep_ref[c] - one * (1.0 - keep_ref[c])
            st_ref[head, c] = state.astype(BF)
            both = dot_fine(jnp.concatenate([w[s], q[s]], axis=0), state)
            fresh = -both[:STRETCH]
            fresh = jnp.concatenate([fresh[:, :HEAD_DIM] + u[s], fresh[:, HEAD_DIM:] - w[s].astype(F32)], axis=1).astype(BF)
            out = both[STRETCH:] + dot(scores[s, s], fresh)
            state = state + t_dot(k[s], fresh)
            o_ref[s, lanes] = out[:, :HEAD_DIM]
            eff_ref[s, lanes] = (out[:, HEAD_DIM:] + q[s].astype(F32)).astype(BF)
        tot_ref[head] = state


def local_kernel(*refs):
    @pl.loop(0, HEADS // 2)
    def _(pair):
        local_heads([pair * 2, pair * 2 + 1], *refs)


def full(shape):
    return pl.BlockSpec(shape, lambda h: (0,) * len(shape))


def local_call(keep, pos, beta, proj, before, taps):
    rows = proj.shape[0]
    count = rows // STRETCH
    whole = pl.BlockSpec(memory_space=pltpu.VMEM)
    return pl.pallas_call(
        local_kernel,
        in_specs=[pl.BlockSpec(memory_space=pltpu.SMEM)] + [whole] * 5,
        out_specs=[whole] * 5,
        out_shape=[
            jax.ShapeDtypeStruct((rows, D), F32),
            jax.ShapeDtypeStruct((rows, D), BF),
            jax.ShapeDtypeStruct((HEADS, HEAD_DIM, 2 * HEAD_DIM), F32),
            jax.ShapeDtypeStruct((HEADS, rows, rows), BF),
            jax.ShapeDtypeStruct((HEADS, count, HEAD_DIM, 2 * HEAD_DIM), BF),
        ],
        compiler_params=pltpu.CompilerParams(vmem_limit_bytes=VMEM_BYTES),
        name="delta_local",
    )(keep, pos, beta, proj, before, taps)


def back_heads(
    heads, keep_ref, pos_ref, beta_ref, proj_ref, before_ref, taps_ref, inv_ref, st_ref, sin_ref, ds_ref, do_ref,
    dproj_ref, tail_ref, dbefore_ref, dtaps_ref, dbeta_ref,
):
    rows = proj_ref.shape[0]
    count = rows // STRETCH
    i, j, strict, causal = masks(rows)
    pos = pos_ref[...]
    for head in heads:
        lanes = lane_span(head * HEAD_DIM)
        raw, act, padded = [], [], []
        for third in range(3):
            start = third * D + head * HEAD_DIM
            acc, pad = conv_rows(columns(proj_ref, start), columns(before_ref, start).astype(F32)[8:], columns(taps_ref, start).astype(F32), pos)
            raw.append(acc)
            act.append(acc * jax.nn.sigmoid(acc))
            padded.append(pad)
        rq = lax.rsqrt(jnp.sum(act[0] * act[0], axis=-1, keepdims=True) + EPSILON)
        rk = lax.rsqrt(jnp.sum(act[1] * act[1], axis=-1, keepdims=True) + EPSILON)
        q = (act[0] * rq * HEAD_DIM ** (-0.5)).astype(BF)
        k32 = act[1] * rk
        k = k32.astype(BF)
        beta = head_column(beta_ref, head)
        gram = jnp.where(strict, dot_t(k, k), 0.0)
        inv = inv_ref[head]
        x = jnp.concatenate([beta * k32, beta * act[2]], axis=1)
        wu = x + dot(inv, x)
        w = wu[:, :HEAD_DIM].astype(BF)
        u = wu[:, HEAD_DIM:]
        scores = jnp.where(causal, dot_t(q, k), 0.0).astype(BF)
        dout = do_ref[:, lanes]
        sin = sin_ref[head]
        states, fresh = [], []
        for c in range(count):
            s = slice(c * STRETCH, (c + 1) * STRETCH)
            packed = st_ref[head, c]
            state = packed[:, :HEAD_DIM].astype(F32) + sin + dot_fine(packed[:, HEAD_DIM:], sin)
            states.append(state)
            fresh.append((u[s] - dot_fine(w[s], state)).astype(BF))
        fresh_all = jnp.concatenate(fresh, axis=0)
        dscores = jnp.where(causal, dot_t(dout, fresh_all), 0.0).astype(BF)
        dfresh0 = t_dot(scores, dout)
        ds = ds_ref[head].astype(F32)
        dfresh = [None] * count
        dk_state = [None] * count
        dq_state = [None] * count
        dw = [None] * count
        for c in reversed(range(count)):
            s = slice(c * STRETCH, (c + 1) * STRETCH)
            part = dfresh0[s] + dot_fine(k[s], ds)
            dfresh[c] = part
            part_low = part.astype(BF)
            dk_state[c] = dot_t_fine(fresh[c], ds)
            both = dot_t_fine(jnp.concatenate([dout[s], part_low], axis=0), states[c])
            dq_state[c] = both[:STRETCH]
            dw[c] = -both[STRETCH:]
            ds = (ds + t_dot(q[s], dout[s]) - t_dot(w[s], part_low)) * keep_ref[c]
        dfresh_all = jnp.concatenate(dfresh, axis=0)
        dq = jnp.concatenate(dq_state, axis=0) + dot(dscores, k)
        dk = jnp.concatenate(dk_state, axis=0) + t_dot(dscores, q)
        dwu = jnp.concatenate([jnp.concatenate(dw, axis=0), dfresh_all], axis=1)
        dx = dwu + t_dot(inv, dwu)
        dlower = jnp.where(strict, -dot_t(dx, wu), 0.0)
        dbeta = jnp.sum(dlower * gram, axis=1, keepdims=True)
        dxk = dx[:, :HEAD_DIM]
        dxv = dx[:, HEAD_DIM:]
        dbeta = dbeta + jnp.sum(dxk * k32 + dxv * act[2], axis=1, keepdims=True)
        dgram = (dlower * beta).astype(BF)
        dk = dk + dot(dgram, k) + t_dot(dgram, k) + beta * dxk
        dv = beta * dxv
        lane = lax.broadcasted_iota(jnp.int32, (rows, HEADS), 1)
        dbeta_ref[...] += jnp.where(lane == head, dbeta * beta * (1.0 - beta), 0.0)
        dq = dq * HEAD_DIM ** (-0.5)
        grads = (
            rq * (dq - act[0] * (rq * rq * jnp.sum(act[0] * dq, axis=-1, keepdims=True))),
            rk * (dk - k32 * jnp.sum(k32 * dk, axis=-1, keepdims=True)),
            dv,
        )
        for third in range(3):
            start = third * D + head * HEAD_DIM
            spot = lane_span(start)
            sig = jax.nn.sigmoid(raw[third])
            dmix = grads[third] * (sig + act[third] * (1.0 - sig))
            taps = columns(taps_ref, start).astype(F32)
            dpad = jnp.concatenate([jnp.zeros((8, HEAD_DIM), F32), taps[CONV - 1 : CONV] * dmix], axis=0)
            dtap = [None] * CONV
            dtap[CONV - 1] = jnp.sum(dmix * padded[third][8:], axis=0, keepdims=True)
            for tap in range(CONV - 1):
                offset = CONV - 1 - tap
                kept = jnp.where(pos >= offset, dmix, 0.0)
                dtap[tap] = jnp.sum(kept * padded[third][8 - offset : 8 - offset + rows], axis=0, keepdims=True)
                scaled = taps[tap : tap + 1] * kept
                dpad = dpad + jnp.concatenate(
                    [jnp.zeros((8 - offset, HEAD_DIM), F32), scaled, jnp.zeros((offset, HEAD_DIM), F32)], axis=0
                )
            dproj_ref[:, spot] = dpad[8:].astype(BF)
            tail_ref[:, spot] = dpad[rows - 8 :]
            dbefore_ref[:, spot] = jnp.concatenate([jnp.zeros((8, HEAD_DIM), F32), dpad[:8]], axis=0).astype(BF)
            dtaps_ref[:, spot] = jnp.concatenate(dtap, axis=0)


def back_kernel(*refs):
    refs[-1][...] = jnp.zeros_like(refs[-1])

    @pl.loop(0, HEADS // 2)
    def _(pair):
        back_heads([pair * 2, pair * 2 + 1], *refs)


def back_call(*args):
    rows = args[3].shape[0]
    whole = pl.BlockSpec(memory_space=pltpu.VMEM)
    return pl.pallas_call(
        back_kernel,
        in_specs=[pl.BlockSpec(memory_space=pltpu.SMEM)] + [whole] * (len(args) - 1),
        out_specs=[whole] * 5,
        out_shape=[
            jax.ShapeDtypeStruct((rows, 3 * D), BF),
            jax.ShapeDtypeStruct((16, 3 * D), F32),
            jax.ShapeDtypeStruct((16, 3 * D), BF),
            jax.ShapeDtypeStruct((CONV, 3 * D), F32),
            jax.ShapeDtypeStruct((rows, HEADS), F32),
        ],
        compiler_params=pltpu.CompilerParams(vmem_limit_bytes=VMEM_BYTES),
        name="delta_back",
    )(*args)


def shift(values, steps):
    count = lax.axis_size("seq")
    first, last = max(0, -steps), min(count, count - steps)
    return lax.ppermute(values, "seq", [(n, n + steps) for n in range(first, last)])


def chain(tot_b, tot_a, steps):
    peers = lax.axis_size("seq")
    state = jnp.zeros(tot_b.shape, F32)
    low_a = tot_a.astype(BF)
    for turn in range(peers - 1):
        if turn == 0:
            new = tot_b
        else:
            new = tot_b + state + jnp.einsum("hde,hef->hdf", low_a, state.astype(BF), preferred_element_type=F32)
        state = shift(new.astype(BF), steps).astype(F32)
    return state


def place_xy():
    seq, batch = lax.axis_index("seq"), lax.axis_index("batch")
    return lax.rem(seq, 2), lax.div(batch, 2), lax.rem(batch, 2), lax.div(seq, 2)


def blocks(width, most=512):
    return [(start, min(most, width - start)) for start in range(0, width, most)]


def load_plan(meta):
    return 1, meta[1:], 1


def start_load(meta, refs, vmem, sems):
    width = meta[2]
    copy = pltpu.make_async_copy(refs[0], vmem, sems.at[0])
    copy.start()
    cuts = blocks(width, 1408 if width % 1408 == 0 else 768 if width % 768 == 0 else 512)
    return [(start, size, start, [copy] if start == 0 else []) for start, size in cuts]


def loaded(meta, vmem, start, size):
    return vmem[:, start : start + size]


def spot_of(start, size):
    if isinstance(start, int):
        return pl.ds(start, size)
    return pl.ds(pl.multiple_of(start, 128), size)


def times(meta, left, vmem, groups, store):
    for start, size, place, copies in groups:
        for copy in copies:
            copy.wait()
        store(spot_of(place, size), dot(left, loaded(meta, vmem, start, size)))


def times_t(meta, left_ref, vmem, groups):
    total = None
    for start, size, place, copies in groups:
        for copy in copies:
            copy.wait()
        part = dot_t(left_ref[:, spot_of(place, size)], loaded(meta, vmem, start, size))
        total = part if total is None else total + part
    return total


def weight_call(kernel, metas, weights, args, out_shape, scratch, name, flops):
    counts = [load_plan(m) for m in metas]

    def run(*refs):
        refs = list(refs)
        ins = [refs.pop(0) for _ in args]
        pieces = [[refs.pop(0) for _ in range(c[0])] for c in counts]
        outs = [refs.pop(0) for _ in out_shape]
        buffers = [(refs.pop(0), refs.pop(0)) for _ in counts]
        kernel(metas, ins, pieces, outs, buffers, refs)

    whole = pl.BlockSpec(memory_space=pltpu.VMEM)
    moved = sum(a.size * a.dtype.itemsize for a in list(args) + list(out_shape))
    scratches = []
    for c in counts:
        scratches += [pltpu.VMEM(c[1], BF), pltpu.SemaphoreType.DMA((c[2],))]
    for c in counts:
        size = 2
        for n in c[1]:
            size *= n
        moved += size
    return pl.pallas_call(
        run,
        in_specs=[whole] * len(args) + [pl.BlockSpec(memory_space=pl.ANY)] * sum(c[0] for c in counts),
        out_specs=[whole] * len(out_shape),
        out_shape=out_shape,
        scratch_shapes=scratches + list(scratch),
        compiler_params=pltpu.CompilerParams(vmem_limit_bytes=VMEM_BYTES),
        cost_estimate=pl.CostEstimate(flops=flops, bytes_accessed=moved, transcendentals=0),
        name=name,
    )(*args, *[p for w in weights for p in w])


def qkv_kernel(metas, ins, pieces, outs, buffers, scratch):
    x_ref, gain_ref, wb_ref, bias_ref = ins
    h_ref, proj_ref, beta_ref, edge_ref = outs
    groups = start_load(metas[0], pieces[0], *buffers[0])
    h = rms_scale(x_ref[...], gain_ref[...].astype(F32)).astype(BF)
    h_ref[...] = h
    beta_ref[...] = jax.nn.sigmoid(dot(h, wb_ref[...]) + bias_ref[...])

    def store(spot, value):
        proj_ref[:, spot] = value
        edge_ref[:, spot] = value[-16:].astype(BF)

    times(metas[0], h, buffers[0][0], groups, store)


def out_kernel(metas, ins, pieces, outs, buffers, scratch):
    o_ref, eff_ref, state_ref, head_ref, x_ref, gain_ref = ins
    full_ref, on_ref, x1_ref, h2_ref = outs
    groups = start_load(metas[0], pieces[0], *buffers[0])
    gain = head_ref[...].astype(F32)
    for head in range(HEADS):
        s = slice(head * HEAD_DIM, (head + 1) * HEAD_DIM)
        o = o_ref[:, s] + dot(eff_ref[:, s], state_ref[head])
        full_ref[:, s] = o
        on_ref[:, s] = rms_scale(o, gain).astype(BF)

    def store(spot, value):
        x1_ref[:, spot] = x_ref[:, spot] + value

    times(metas[0], on_ref[...], buffers[0][0], groups, store)
    h2_ref[...] = rms_scale(x1_ref[...], gain_ref[...].astype(F32)).astype(BF)


def mlp_kernel(metas, ins, pieces, outs, buffers, scratch):
    h2_ref, x1_ref = ins
    gu_ref, hid_ref, x2_ref = outs
    groups = start_load(metas[0], pieces[0], *buffers[0])
    later = start_load(metas[1], pieces[1], *buffers[1])

    def store(spot, value):
        gu_ref[:, spot] = value

    times(metas[0], h2_ref[...], buffers[0][0], groups, store)
    ff = hid_ref.shape[1]
    for start, size in blocks(ff):
        gate = gu_ref[:, start : start + size]
        hid_ref[:, start : start + size] = (
            gate * jax.nn.sigmoid(gate) * gu_ref[:, ff + start : ff + start + size]
        ).astype(BF)

    def store_two(spot, value):
        x2_ref[:, spot] = x1_ref[:, spot] + value

    times(metas[1], hid_ref[...], buffers[1][0], later, store_two)


def mlp_back_kernel(metas, ins, pieces, outs, buffers, scratch):
    g_ref, gu_ref, x1_ref, gain_ref, o_ref, eff_ref, head_ref = ins
    dgu_ref, dx1_ref, dy1_ref, dmlp_ref, do_ref, ds_ref, dgain_ref = outs
    dy2_ref, dhid_ref, don_ref = scratch
    down = start_load(metas[0], pieces[0], *buffers[0])
    gate_up = start_load(metas[1], pieces[1], *buffers[1])
    out = start_load(metas[2], pieces[2], *buffers[2])
    dy2_ref[...] = g_ref[...].astype(BF)
    dhid_ref[...] = times_t(metas[0], dy2_ref, buffers[0][0], down)
    ff = dhid_ref.shape[1]
    for start, size in blocks(ff):
        s = slice(start, start + size)
        f = slice(ff + start, ff + start + size)
        gate = gu_ref[:, s]
        sig = jax.nn.sigmoid(gate)
        dhid = dhid_ref[:, s]
        act = gate * sig
        dgu_ref[:, s] = (dhid * gu_ref[:, f] * (sig + act * (1.0 - sig))).astype(BF)
        dgu_ref[:, f] = (dhid * act).astype(BF)
    dh2 = times_t(metas[1], dgu_ref, buffers[1][0], gate_up)
    back, part = rms_back(x1_ref[...], gain_ref[...].astype(F32), dh2)
    dmlp_ref[...] = jnp.sum(part, axis=0, keepdims=True)
    dx1 = g_ref[...] + back
    dx1_ref[...] = dx1
    dy1_ref[...] = dx1.astype(BF)
    don_ref[...] = times_t(metas[2], dy1_ref, buffers[2][0], out)
    gain = head_ref[...].astype(F32)
    dgain = jnp.zeros((1, HEAD_DIM), F32)
    for head in range(HEADS):
        s = slice(head * HEAD_DIM, (head + 1) * HEAD_DIM)
        back, part = rms_back(o_ref[:, s], gain, don_ref[:, s])
        dgain = dgain + jnp.sum(part, axis=0, keepdims=True)
        low = back.astype(BF)
        do_ref[:, s] = low
        ds_ref[head] = t_dot(eff_ref[:, s], low)
    dgain_ref[...] = dgain


def qkv_back_kernel(metas, ins, pieces, outs, buffers, scratch):
    dproj_ref, tail_ref, back_ref, dlogit_ref, wb_ref, x_ref, gain_ref, dx1_ref, h_ref = ins
    fixed_ref, g_ref, dmix_ref, dbeta_ref, dbias_ref = outs
    groups = start_load(metas[0], pieces[0], *buffers[0])
    rows = dproj_ref.shape[0]
    fixed_ref[: rows - 16] = dproj_ref[: rows - 16]
    fixed_ref[rows - 16 :] = (tail_ref[...] + back_ref[...].astype(F32)).astype(BF)
    dlogit = dlogit_ref[...]
    dbias_ref[...] = jnp.sum(dlogit, axis=0, keepdims=True)
    low = dlogit.astype(BF)
    dbeta_ref[...] = t_dot(h_ref[...], low)
    dh = times_t(metas[0], fixed_ref, buffers[0][0], groups) + dot_t(low, wb_ref[...])
    back, part = rms_back(x_ref[...], gain_ref[...].astype(F32), dh)
    dmix_ref[...] = jnp.sum(part, axis=0, keepdims=True)
    g_ref[...] = dx1_ref[...] + back


def gather_weights(qkv, conv, beta, out, mix, mlp, gate, up, down):
    result = []
    for n in range(qkv.shape[0]):
        rows = [lax.all_gather(a[n], BOTH, axis=0, tiled=True) for a in (beta, mix, mlp, qkv, out, gate, up, down)]
        rows[5:7] = [jnp.concatenate(rows[5:7], axis=1)]
        names = ("beta", "mix", "mlp", "qkv", "out", "gate_up", "down")
        found = dict(zip(names[:3], rows[:3]))
        found["conv"] = lax.all_gather(conv[n], BOTH, axis=1, tiled=True)
        for name, value in zip(names[3:], rows[3:]):
            found[name] = (("plain",) + value.shape, [value])
        result.append(found)
    return result


def scatter(left, right):
    value = lax.dot_general(left, right, (((0,), (0,)), ((), ())), preferred_element_type=F32)
    return lax.psum_scatter(value.astype(BF), BOTH, scatter_dimension=0, tiled=True).astype(F32)


MESH = pl.DeviceIdType.MESH


def device(x, y, core, z):
    return (z * 2 + x, y * 2 + core)


def path_place():
    x, y, core, z = place_xy()
    piece = z * 2 + core

    def at(step):
        other = (piece + step + 8) % 8
        return device(x, y, other % 2, other // 2)

    return piece, at(1), at(-1)


def partner():
    x, y, core, z = place_xy()
    return device(1 - x, y, 1 - core, z)


def signal_all(peers):
    barrier = pltpu.get_barrier_semaphore()
    for peer in peers:
        pl.semaphore_signal(barrier, inc=1, device_id=peer, device_id_type=MESH)
    pl.semaphore_wait(barrier, len(peers))


def near_peers():
    x, y, core, z = place_xy()
    peers = [device(1 - x, y, core, z), device(x, 1 - y, core, z), device(x, y, 1 - core, z)]
    return peers + [device(x, y, core, (z + k) % 4) for k in range(1, 4)]


class Gather:
    def __init__(self, mine, full, begin, cut, sends, gots):
        self.mine, self.full, self.begin, self.cut = mine, full, begin, cut
        self.sends, self.gots = sends, gots
        self.size = mine.shape[1]
        self.half = full.shape[4] // 2
        self.pending = {}

    def cols(self, core, part=None):
        start, size = self.begin, self.size
        if part == 0:
            size = self.cut
        if part == 1:
            start, size = start + self.cut, size - self.cut
        return pl.ds(pl.multiple_of(core * self.half + start, 128), size)

    def copy(self, n, src, dst, peer):
        return pltpu.make_async_remote_copy(
            src_ref=src, dst_ref=dst, send_sem=self.sends.at[n], recv_sem=self.gots.at[n],
            device_id=peer, device_id_type=MESH,
        )

    def send(self, n, source):
        self.copy(n, *source()).start()
        self.pending[n] = source

    def got(self, n, region, peer):
        self.copy(n, region, region, peer).wait_recv()

    def finish(self):
        for n, source in self.pending.items():
            self.copy(n, *source()).wait_send()

    def stages(self):
        return [self.stage_z, self.stage_one, self.stage_two, self.stage_core, self.stage_end]

    def parts(self):
        return [n for n, size in enumerate((self.cut, self.size - self.cut)) if size]

    def local(self):
        x, y, core, z = place_xy()
        return pltpu.make_async_copy(self.mine, self.full.at[z, x, y, :, self.cols(core)], self.sends.at[8])

    def stage_z(self):
        self.local().start()
        for k in range(1, 4):

            def source(k=k):
                x, y, core, z = place_xy()
                return self.mine, self.full.at[z, x, y, :, self.cols(core)], device(x, y, core, (z + k) % 4)

            self.send(k - 1, source)

    def stage_one(self):
        x, y, core, z = place_xy()
        self.local().wait()
        for k in range(1, 4):
            far = (z + 4 - k) % 4
            self.got(k - 1, self.full.at[far, x, y, :, self.cols(core)], device(x, y, core, far))
        for n in self.parts():

            def source(n=n):
                x, y, core, z = place_xy()
                spot = self.full.at[:, x, y, :, self.cols(core, n)]
                return spot, spot, device(x, 1 - y, core, z) if n else device(1 - x, y, core, z)

            self.send(3 + n, source)

    def stage_two(self):
        x, y, core, z = place_xy()
        for n in self.parts():
            if n == 0:
                self.got(3, self.full.at[:, 1 - x, y, :, self.cols(core, 0)], device(1 - x, y, core, z))
            else:
                self.got(4, self.full.at[:, x, 1 - y, :, self.cols(core, 1)], device(x, 1 - y, core, z))

            def source(n=n):
                x, y, core, z = place_xy()
                if n == 0:
                    spots = self.full.at[:, :, y, :, self.cols(core, 0)]
                else:
                    spots = self.full.at[:, x, :, :, self.cols(core, 1)]
                return spots, spots, device(1 - x, y, core, z) if n else device(x, 1 - y, core, z)

            self.send(5 + n, source)

    def stage_core(self):
        x, y, core, z = place_xy()
        for n in self.parts():
            if n == 0:
                self.got(5, self.full.at[:, :, 1 - y, :, self.cols(core, 0)], device(x, 1 - y, core, z))
            else:
                self.got(6, self.full.at[:, 1 - x, :, :, self.cols(core, 1)], device(1 - x, y, core, z))

        def source():
            x, y, core, z = place_xy()
            both = self.full.at[:, :, :, :, self.cols(core)]
            return both, both, device(x, y, 1 - core, z)

        self.send(7, source)

    def stage_end(self):
        x, y, core, z = place_xy()
        self.got(7, self.full.at[:, :, :, :, self.cols(1 - core)], device(x, y, 1 - core, z))


class Schedule:
    def __init__(self, gathers, swaps):
        self.gathers, self.swaps = gathers, swaps
        self.ready = {}
        self.turn = 0

    def tick(self, times=1):
        for _ in range(times):
            self.one_tick()

    def one_tick(self):
        for stage in reversed(range(5)):
            n = self.turn - LAGS[stage]
            if 0 <= n < len(self.gathers):
                if stage == 0:
                    self.swaps[n].wait()
                    if n in self.ready:
                        self.ready[n]()
                self.gathers[n].stages()[stage]()
        self.turn += 1

    def until(self, n):
        self.tick(max(0, n + LAGS[4] + 1 - self.turn))

    def finish(self):
        self.until(len(self.gathers) - 1)
        for gather in self.gathers:
            gather.finish()

    def save(self):
        return self.turn

    def restore(self, state):
        self.turn = state


def around(engine, times, early, middle):
    state = engine.save()

    @pl.when(early)
    def _():
        engine.tick(times)

    engine.restore(state)
    middle()

    @pl.when(jnp.logical_not(early))
    def _():
        engine.tick(times)


def swap_rows(shard, mine, begin, send, got):
    x, y, core, z = place_xy()
    size = mine.shape[1]

    def copy_of(source, target):
        return pltpu.make_async_remote_copy(
            src_ref=source, dst_ref=target, send_sem=send, recv_sem=got,
            device_id=device(x, y, 1 - core, z), device_id_type=MESH,
        )

    if len(shard) == 2:
        rows = shard[0].shape[0]
        place = pl.ds(pl.multiple_of(core * rows, rows), rows)
        for side in range(2):

            @pl.when(core == side)
            def _():
                copy_of(shard[1 - side].at[:, pl.ds(begin, size)], mine.at[place, :]).start()
                mine[place, :] = shard[side][:, pl.ds(begin, size)]

        return copy_of(shard[0].at[:, pl.ds(begin, size)], mine.at[place, :])
    shard = shard[0]
    rows = shard.shape[0]
    half = shard.shape[1] // 2
    place = pl.ds(pl.multiple_of(core * rows, rows), rows)
    copy = copy_of(shard.at[:, pl.ds(pl.multiple_of((1 - core) * half + begin, 128), size)], mine.at[place, :])
    copy.start()
    mine[place, :] = shard[:, pl.ds(pl.multiple_of(core * half + begin, 128), size)]
    return copy


def cut_chunks(rows, sizes):
    parts = []
    start = 0
    for n, size in enumerate(sizes):
        cut = (size // 128 + n % 2) // 2 * 128
        parts.append((rows, start, size, cut))
        start += size
    return parts


CHUNKS = dict(
    out=cut_chunks(64, [256] * 2),
    down=cut_chunks(176, [128] * 4),
    qkv=cut_chunks(64, [384] * 4),
    gate_up=cut_chunks(64, [384] * 6 + [256] * 2),
)
LAGS = (0, 2, 4, 6, 8, 9)


def load_columns(full, vmem, spans, sems):
    copies = []
    for n, (start, size) in enumerate(spans):
        copy = pltpu.make_async_copy(
            full.at[:, :, :, :, pl.ds(start, size)], vmem.at[:, :, :, :, pl.ds(start, size)], sems.at[n]
        )
        copy.start()
        copies.append(copy)
    return copies


def weight_columns(vmem, start, size):
    dims = vmem.shape
    return vmem[:, :, :, :, start : start + size].reshape(16 * dims[3], size)


def dma(*dims):
    return pltpu.SemaphoreType.DMA(dims)


def stream_place(r, piece, rows):
    first = r.lengths[0, 0]
    second = first + r.lengths[0, 1]
    index = piece * rows + lax.broadcasted_iota(jnp.int32, (rows, 1), 0)
    begin = jnp.where(index >= second, second, jnp.where(index >= first, first, 0))
    r.pos[...] = index - begin
    keep = []
    for start in range(0, rows, STRETCH):
        token = piece * rows + start
        new = (token == 0) | (token == first) | (token == second)
        keep.append(jnp.where(new, 0.0, 1.0))
    return keep


def gather_small(r):
    seq, batch = lax.axis_index("seq"), lax.axis_index("batch")
    me = seq * 4 + batch
    copies = []
    for k in range(1, 32):
        peer = (me + k) % 32
        copy = pltpu.make_async_remote_copy(
            src_ref=r.packed, dst_ref=r.packs.at[me], send_sem=r.small_sends.at[k - 1], recv_sem=r.small_gots.at[k - 1],
            device_id=(peer // 4, peer % 4), device_id_type=MESH,
        )
        copy.start()
        copies.append(copy)
    r.packs[me] = r.packed[...]
    return copies


def lay_out_small(r):
    rows = r.packs[:, 16:48, :].reshape(D, 128)
    i = lax.broadcasted_iota(jnp.int32, (24, 128), 0)
    j = lax.broadcasted_iota(jnp.int32, (24, 128), 1)
    r.smalls[...] = dot_t(jnp.where(i == j, 1.0, 0.0), rows)
    i = lax.broadcasted_iota(jnp.int32, (128, 384), 0)
    j = lax.broadcasted_iota(jnp.int32, (128, 384), 1)
    total = None
    for n in range(4):
        left = jnp.concatenate([r.packs[4 * q + n, 0:16, :].astype(F32)[:8] for q in range(8)], axis=0)
        part = dot(left, jnp.where((j == i + 96 * n) & (i < 96), 1.0, 0.0))
        total = part if total is None else total + part
    for q in range(8):
        for n in range(2):
            r.taps[n, :, 384 * q : 384 * (q + 1)] = total[8 * q + 4 * n : 8 * q + 4 * n + 4]


def forward_kernel(chunks, shards, fulls, mines, r):
    piece, after, before = path_place()
    x, y, core, z = place_xy()
    seq, batch = lax.axis_index("seq"), lax.axis_index("batch")
    me = seq * 4 + batch
    signal_all([((me + k) % 32 // 4, (me + k) % 32 % 4) for k in range(1, 32)])
    swap_x = pltpu.make_async_remote_copy(
        src_ref=r.x, dst_ref=r.x_got, send_sem=r.move_sems.at[0], recv_sem=r.move_sems.at[1],
        device_id=partner(), device_id_type=MESH,
    )
    swap_g = pltpu.make_async_remote_copy(
        src_ref=r.g, dst_ref=r.g_moved, send_sem=r.move_sems.at[2], recv_sem=r.move_sems.at[3],
        device_id=partner(), device_id_type=MESH,
    )
    stay_g = pltpu.make_async_copy(r.g, r.g_moved, r.move_sems.at[4])
    rows = r.x.shape[0]
    swaps, gathers = [], []
    first = {}
    schedule = Schedule(gathers, swaps)
    for n, (layer, name, part) in enumerate(chunks):
        mine = mines[n]
        first.setdefault((layer, name), n)
        shard = [ref.at[layer] for ref in shards[name]]
        if name == "down":
            half = shard[0].shape[1] // 2
            other = r.other_down.at[layer, :, pl.ds(part[1], part[2])]
            copy = pltpu.make_async_remote_copy(
                src_ref=shard[0].at[:, pl.ds(pl.multiple_of((1 - core) * half + part[1], 128), part[2])],
                dst_ref=other, send_sem=r.swap_sends.at[n], recv_sem=r.swap_gots.at[n],
                device_id=device(x, y, 1 - core, z), device_id_type=MESH,
            )
            copy.start()

            def ready(shard=shard[0], mine=mine, part=part, half=half, other=other):
                own = shard[:, pl.ds(pl.multiple_of(core * half + part[1], 128), part[2])].astype(F32)
                got = other[...].astype(F32)
                low = jnp.where(core == 0, own, got)
                high = jnp.where(core == 0, got, own)
                mine[...] = jnp.concatenate([low, high], axis=0).astype(BF)

            schedule.ready[n] = ready
        else:
            copy = swap_rows(shard, mine, part[1], r.swap_sends.at[n], r.swap_gots.at[n])
        swaps.append(copy)
        gathers.append(
            Gather(mine, fulls[layer, name], part[1], part[3], r.sends.at[n], r.gots.at[n])
        )
        if n == 3:
            small_copies = gather_small(r)
            schedule.tick()
    keep = stream_place(r, piece, rows)
    schedule.tick(2)

    @pl.when(x != core)
    def _():
        swap_x.start()

    @pl.when(x == core)
    def _():
        stay_g.start()
        r.xin[...] = r.x[...]

    for copy in small_copies:
        copy.wait()
    lay_out_small(r)
    schedule.until(len(CHUNKS["qkv"]) - 1)

    @pl.when(x != core)
    def _():
        swap_x.wait()
        r.xin[...] = r.x_got[...]

    for layer in range(LAYERS):
        forward_block(layer, first, fulls, schedule, keep, r, swap_g)
    schedule.finish()

    @pl.when(x != core)
    def _():
        swap_g.wait()

    @pl.when(x == core)
    def _():
        stay_g.wait()

    for copy in r.puts:
        copy.wait()


def forward_block(layer, first, fulls, schedule, keep, r, swap_g):
    piece, after, before = path_place()
    x_ref = r.x2 if layer else r.xin
    count = {name: len(parts) for name, parts in CHUNKS.items()}

    def until(name, part):
        schedule.until(first[layer, name] + part)

    def put(*names):
        for name in names:
            n = len(r.puts)
            copy = pltpu.make_async_copy(getattr(r, name), r.saved[layer][name], r.put_sems.at[n])
            copy.start()
            r.puts.append(copy)

    until("qkv", count["qkv"] - 1)
    wb = r.smalls[8 * layer : 8 * layer + 8].astype(BF)
    mix = r.smalls[16 + layer : 17 + layer]
    mlp = r.smalls[18 + layer : 19 + layer]
    taps = r.taps.at[layer]
    spans = [(n * 768, 768) for n in range(4)]
    loads = load_columns(fulls[layer, "qkv"], r.vbig, spans, r.load_sems.at[0])
    for copy in r.puts:
        copy.wait()
    r.puts.clear()
    put("x2" if layer else "xin")
    h = rms_scale(x_ref[...].astype(F32), mix).astype(BF)
    r.h[...] = h
    r.beta[...] = jax.nn.sigmoid(dot_t(h, wb) + r.bias[layer].astype(F32))
    for (start, size), copy in zip(spans, loads):
        copy.wait()
        value = dot(h, weight_columns(r.vbig, start, size))
        r.proj[:, start : start + size] = value
        r.edge[:, start : start + size] = value[-16:].astype(BF)
        if start:
            schedule.tick()
    halo_ref = r.halo.at[layer]
    halo = pltpu.make_async_remote_copy(
        src_ref=r.edge, dst_ref=halo_ref, send_sem=r.halo_sems.at[0, layer], recv_sem=r.halo_sems.at[1, layer],
        device_id=after, device_id_type=MESH,
    )

    @pl.when(piece < 7)
    def _():
        halo.start()

    put("h", "proj", "beta")

    @pl.when(piece == 0)
    def _():
        halo_ref[...] = jnp.zeros_like(halo_ref)

    @pl.when(piece > 0)
    def _():
        halo.wait_recv()

    r.before[...] = halo_ref[...]
    schedule.tick()
    for head in range(0, HEADS, 2):
        local_heads(
            [head, head + 1], keep, r.pos, r.beta, r.proj, halo_ref, taps, r.o, r.eff, r.tot, r.inv, r.st,
        )
        schedule.tick(2)
    last = r.last.at[layer]
    links = [
        pltpu.make_async_remote_copy(
            src_ref=r.next.at[pl.ds(2 * n, 2)], dst_ref=last.at[pl.ds(2 * n, 2)],
            send_sem=r.chain_sends.at[layer, n], recv_sem=r.chain_gots.at[layer, n],
            device_id=after, device_id_type=MESH,
        )
        for n in range(4)
    ]

    @pl.when(piece == 0)
    def _():
        last[...] = jnp.zeros_like(last)

    r.a[...] = r.tot[:, :, HEAD_DIM:]

    def pass_on():
        for n, link in enumerate(links):

            @pl.when(piece > 0)
            def _():
                link.wait_recv()

            for head in (2 * n, 2 * n + 1):
                state = last[head]
                r.sin[head] = state
                high, low = two_parts(r.tot[head, :, HEAD_DIM:])
                part = state.astype(BF)
                r.next[head] = r.tot[head, :, :HEAD_DIM] + state + (dot(high, part) + dot(low, part))

            @pl.when(piece < 7)
            def _():
                link.start()

    around(schedule, 2, piece >= 4, pass_on)
    put("before", "inv", "st", "eff", "sin", "a")
    until("out", count["out"] - 1)
    load = load_columns(fulls[layer, "out"], r.vout, [(0, D)], r.load_sems.at[0])
    gain = r.head[layer].astype(F32)
    for head in range(HEADS):
        s = slice(head * HEAD_DIM, (head + 1) * HEAD_DIM)
        o = r.o[:, s] + dot_fine(r.eff[:, s], r.sin[head])
        r.o[:, s] = o
        r.on[:, s] = rms_scale(o, gain).astype(BF)
    load[0].wait()
    r.x1[...] = x_ref[...].astype(F32) + dot(r.on[...], weight_columns(r.vout, 0, D))
    h2 = rms_scale(r.x1[...], mlp).astype(BF)
    r.h2[...] = h2
    put("o", "on", "x1", "h2")
    ff = r.hid.shape[1]
    waiting = []

    def gate_up_part(start, size, loads):
        loads[0].wait()
        gate = dot(h2, weight_columns(r.vbig, start, size))
        r.gu[:, start : start + size] = gate.astype(BF)
        loads[1].wait()
        up = dot(h2, weight_columns(r.vbig, start + ff, size))
        r.gu[:, start + ff : start + ff + size] = up.astype(BF)
        r.hid[:, start : start + size] = (gate * jax.nn.sigmoid(gate) * up).astype(BF)

    for part, (_, start, size, _) in enumerate(CHUNKS["gate_up"]):
        until("gate_up", part)
        spans = [(start, size), (start + ff, size)]
        waiting.append((start, size, load_columns(fulls[layer, "gate_up"], r.vbig, spans, r.load_sems.at[part % 2])))
        if part:
            gate_up_part(*waiting.pop(0))
    gate_up_part(*waiting.pop(0))
    put("gu", "hid")
    x2 = r.mixed if layer else r.x2
    if layer:
        x, _, core, _ = place_xy()

        @pl.when(x != core)
        def _():
            swap_g.start()

    for part, (_, start, size, _) in enumerate(CHUNKS["down"]):
        until("down", part)
        spans = [(start, size), (start + D // 2, size)]
        loads = load_columns(fulls[layer, "down"], r.vdown, spans, r.load_sems.at[0])
        for (begin, wide), copy in zip(spans, loads):
            copy.wait()
            value = dot(r.hid[...], weight_columns(r.vdown, begin, wide))
            x2[:, begin : begin + wide] = (r.x1[:, begin : begin + wide] + value).astype(x2.dtype)
    if layer:
        put("mixed")

    @pl.when(piece < 7)
    def _():
        halo.wait_send()
        for link in links:
            link.wait_send()


def saved_shapes(rows, ff2):
    count = rows // STRETCH
    return dict(
        h=((rows, D), BF), proj=((rows, 3 * D), F32), beta=((rows, HEADS), F32), before=((16, 3 * D), BF),
        o=((rows, D), F32), eff=((rows, D), BF), a=((HEADS, HEAD_DIM, HEAD_DIM), F32), inv=((HEADS, rows, rows), BF),
        st=((HEADS, count, HEAD_DIM, 2 * HEAD_DIM), BF), sin=((HEADS, HEAD_DIM, HEAD_DIM), F32), on=((rows, D), BF),
        x1=((rows, D), F32), h2=((rows, D), BF), gu=((rows, ff2), BF), hid=((rows, ff2 // 2), BF),
    )


def forward_call(x, g, packed, lengths, bias, head, shards):
    rows = x.shape[0]
    ff2 = 2 * shards["gate_up"][0].shape[2]
    names = list(shards)
    chunks = [(n, name, part) for n in range(LAYERS) for name in names for part in CHUNKS[name]]
    whole, anywhere = pl.BlockSpec(memory_space=pltpu.VMEM), pl.BlockSpec(memory_space=pl.ANY)
    ins = dict(lengths=lengths, g=g, x=x, bias=bias, head=head, packed=packed)
    sources = [value for name in names for value in shards[name]]
    saved = saved_shapes(rows, ff2)
    layers = [dict(saved, xin=((rows, D), BF)), dict(saved, x2=((rows, D), F32), mixed=((rows, D), BF))]
    wide = dict(out=D, gate_up=ff2, down=D, qkv=3 * D)
    far = [((4, 2, 2, 176 if name == "down" else 64, wide[name]), BF) for _ in range(LAYERS) for name in names]
    outs = dict(smalls=((24, D), F32), taps=((LAYERS, CONV, 3 * D), F32))
    v = pltpu.VMEM
    scratch = {key: v(*d) for layer in layers for key, d in layer.items()}
    scratch.update(
        other_down=v((LAYERS, 88, 512), BF), vbig=v((4, 2, 2, 64, ff2), BF), vout=v((4, 2, 2, 64, D), BF),
        vdown=v((4, 2, 2, 176, D), BF), edge=v((16, 3 * D), BF), halo=v((LAYERS, 16, 3 * D), BF),
        tot=v((HEADS, HEAD_DIM, 2 * HEAD_DIM), F32), next=v((HEADS, HEAD_DIM, HEAD_DIM), F32),
        last=v((LAYERS, HEADS, HEAD_DIM, HEAD_DIM), F32), pos=v((rows, 1), jnp.int32),
        sends=dma(len(chunks), 9), gots=dma(len(chunks), 9), swap_sends=dma(len(chunks)), swap_gots=dma(len(chunks)),
        load_sems=dma(2, 4), halo_sems=dma(2, LAYERS), chain_sends=dma(LAYERS, 4), chain_gots=dma(LAYERS, 4),
        put_sems=dma(len(layers[1])), move_sems=dma(5), x_got=v((rows, D), BF), packs=v((32, 48, 128), BF), small_sends=dma(31), small_gots=dma(31),
    )
    mine = [v((part[0], part[2]), BF) for _, _, part in chunks]

    def run(*refs):
        refs = list(refs)

        def take(count):
            taken = refs[:count]
            del refs[:count]
            return taken

        r = dict(zip(ins, take(len(ins))))
        given = {name: take(len(shards[name])) for name in names}
        r.update(zip(outs, take(len(outs))))
        kept = [dict(zip(d, take(len(d)))) for d in layers]
        fulls = {(n, name): take(1)[0] for n in range(LAYERS) for name in names}
        r["g_moved"] = take(1)[0]
        r.update(zip(scratch, take(len(scratch))))
        forward_kernel(chunks, given, fulls, refs, SimpleNamespace(saved=kept, puts=[], **r))

    shapes = list(outs.values()) + [d for layer in layers for d in layer.values()] + far + [((rows, D), BF)]
    result = list(
        pl.pallas_call(
            run,
            in_specs=[pl.BlockSpec(memory_space=pltpu.SMEM), anywhere] + [whole] * (len(ins) - 2 + len(sources)),
            out_specs=[whole] * len(outs) + [anywhere] * (len(shapes) - len(outs)),
            out_shape=[jax.ShapeDtypeStruct(*d) for d in shapes],
            scratch_shapes=list(scratch.values()) + mine,
            compiler_params=pltpu.CompilerParams(
                collective_id=1, has_side_effects=True, vmem_limit_bytes=VMEM_BYTES
            ),
            name="forward",
        )(*ins.values(), *sources)
    )
    small = [result.pop(0) for _ in outs]
    kept = [{key: result.pop(0) for key in d} for d in layers]
    for n in range(LAYERS):
        kept[n].update({"w_" + name: result.pop(0) for name in names})
    mixed = kept[1].pop("mixed")
    kept[1]["x"] = kept[1].pop("x2")
    kept[0]["x"] = kept[0].pop("xin")
    return kept, small, mixed, result.pop(0)


Room = namedtuple(
    "Room", ("sent", "landing", "sums", "one_a", "one_b", "two_a", "two_b", "three", "final", "own")
)


class Scatter:
    def __init__(self, left, right, outs, rows, begin, size, cut, room, sends, gots):
        self.left, self.right, self.outs = left, right, outs
        self.rows, self.begin, self.size, self.cut = rows, begin, size, cut
        self.half = right.shape[1] // 2
        self.room, self.sends, self.gots = Room(*room), sends, gots
        self.stage = 0
        self.stages = [self.start, self.square, self.side, self.line, self.total, self.end]

    def step(self):
        self.stages[self.stage]()
        self.stage += 1
        return self.stage == len(self.stages)

    def copy(self, n, src, dst, peer):
        return pltpu.make_async_remote_copy(
            src_ref=src, dst_ref=dst, send_sem=self.sends.at[n], recv_sem=self.gots.at[n],
            device_id=peer, device_id_type=MESH,
        )

    def products(self, core, store):
        left = self.left[...]
        for start, size in blocks(self.size, 384 if self.rows == 64 else 128):
            spot = pl.multiple_of(core * self.half + self.begin + start, 128)
            store(start, size, t_dot(left, self.right[:, pl.ds(spot, size)]).reshape(4, 2, 2, self.rows, size))

    def parts(self):
        return [n for n, size in enumerate((self.cut, self.size - self.cut)) if size]

    def span(self, n):
        return (0, self.cut) if n == 0 else (self.cut, self.size - self.cut)

    def to_core(self):
        x, y, core, z = place_xy()
        cols = pl.ds(0, self.size)
        sent, landing = (ref.at[:, :, :, :, cols] for ref in (self.room.sent, self.room.landing))
        return self.copy(0, sent, landing, device(x, y, 1 - core, z))

    def ones(self):
        x, y, core, z = place_xy()
        made = []
        for n in self.parts():
            start, size = self.span(n)
            if n == 0:
                source, peer = self.room.sums.at[:, :, 1 - y, :, pl.ds(start, size)], device(x, 1 - y, core, z)
            else:
                source, peer = self.room.sums.at[:, 1 - x, :, :, pl.ds(start, size)], device(1 - x, y, core, z)
            target = (self.room.one_a, self.room.one_b)[n].at[:, :, :, pl.ds(0, size)]
            made.append(self.copy(1 + n, source, target, peer))
        return made

    def twos(self):
        x, y, core, z = place_xy()
        made = []
        for n in self.parts():
            start, size = self.span(n)
            if n == 0:
                source, peer = self.room.sums.at[:, 1 - x, y, :, pl.ds(start, size)], device(1 - x, y, core, z)
            else:
                source, peer = self.room.sums.at[:, x, 1 - y, :, pl.ds(start, size)], device(x, 1 - y, core, z)
            target = (self.room.two_a, self.room.two_b)[n].at[:, :, pl.ds(0, size)]
            made.append(self.copy(3 + n, source, target, peer))
        return made

    def threes(self):
        x, y, core, z = place_xy()
        cols = pl.ds(0, self.size)
        return [
            self.copy(
                4 + k, self.room.sums.at[(z + k) % 4, x, y, :, cols], self.room.three.at[k - 1, :, cols],
                device(x, y, core, (z + k) % 4),
            )
            for k in range(1, 4)
        ]

    def place(self, ref, core):
        if len(self.outs) == 2:
            return ref.at[:, pl.ds(self.begin, self.size)]
        return ref.at[:, pl.ds(pl.multiple_of(core * self.half + self.begin, 128), self.size)]

    def sides(self):
        core = place_xy()[2]
        if len(self.outs) == 2:
            return [(core == side, ref) for side, ref in enumerate(self.outs)]
        return [(None, self.outs[0])]

    def finals(self, ref):
        x, y, core, z = place_xy()
        cols = pl.ds(0, self.size)
        return (
            pltpu.make_async_copy(self.room.own.at[:, cols], self.place(ref, core), self.sends.at[9]),
            self.copy(8, self.room.final.at[:, cols], self.place(ref, core), device(x, y, 1 - core, z)),
        )

    def start(self):
        def store(start, size, value):
            self.room.sent[:, :, :, :, start : start + size] = value.astype(BF)

        self.products(1 - place_xy()[2], store)
        self.to_core().start()

    def square(self):
        self.to_core().wait()
        room = self.room

        def store(start, width, value):
            got = room.landing[:, :, :, :, start : start + width].astype(F32)
            room.sums[:, :, :, :, start : start + width] = (value + got).astype(BF)

        self.products(place_xy()[2], store)
        for copy in self.ones():
            copy.start()

    def side(self):
        x, y, core, z = place_xy()
        room, sums = self.room, self.room.sums
        for copy in self.ones():
            copy.wait_recv()
        for n in self.parts():
            start, size = self.span(n)
            end = start + size
            for far in range(2):
                if n == 0:
                    part = sums[:, far, pl.ds(y, 1), :, start:end][:, 0].astype(F32)
                    part = part + room.one_a[:, far, :, :size].astype(F32)
                    sums[:, far, pl.ds(y, 1), :, start:end] = part.astype(BF)[:, None]
                else:
                    part = sums[:, pl.ds(x, 1), far, :, start:end][:, 0].astype(F32)
                    part = part + room.one_b[:, far, :, :size].astype(F32)
                    sums[:, pl.ds(x, 1), far, :, start:end] = part.astype(BF)[:, None]
        for copy in self.twos():
            copy.start()

    def line(self):
        x, y, core, z = place_xy()
        room, sums = self.room, self.room.sums
        for copy in self.twos():
            copy.wait_recv()
        for n in self.parts():
            start, size = self.span(n)
            got = (room.two_a, room.two_b)[n]
            for k in range(4):
                spot = (k, pl.ds(x, 1), pl.ds(y, 1), slice(None), slice(start, start + size))
                part = sums[spot][0, 0].astype(F32) + got[k, :, :size].astype(F32)
                sums[spot] = part.astype(BF)[None, None]
        for copy in self.threes():
            copy.start()

    def total(self):
        x, y, core, z = place_xy()
        room, size = self.room, self.size
        for copy in self.threes():
            copy.wait()
        for copy in self.ones() + self.twos():
            copy.wait_send()
        own = room.sums[pl.ds(z, 1), pl.ds(x, 1), pl.ds(y, 1), :, :size][0, 0, 0].astype(F32)
        for k in range(3):
            own = own + room.three[k, :, :size].astype(F32)
        half = self.rows // 2
        low, high = own[:half], own[half:]
        room.own[:, :size] = jnp.where(core == 0, low, high)
        room.final[:, :size] = jnp.where(core == 0, high, low)
        for condition, ref in self.sides():

            def go(ref=ref):
                for copy in self.finals(ref):
                    copy.start()

            go() if condition is None else pl.when(condition)(go)

    def end(self):
        x, y, core, z = place_xy()
        for condition, ref in self.sides():

            def stay(ref=ref):
                local, away = self.finals(ref)
                local.wait()
                away.wait_send()

            def come(ref=ref):
                target = self.place(ref, 1 - core)
                self.copy(8, self.room.final.at[:, pl.ds(0, self.size)], target, device(x, y, 1 - core, z)).wait_recv()

            if condition is None:
                stay()
                come()
            else:
                pl.when(condition)(stay)
                pl.when(jnp.logical_not(condition))(come)


class SumAll:
    def __init__(self, values, out, low, got, sends, gots):
        self.values, self.out, self.low, self.got = values, out, low, got
        self.sends, self.gots = sends, gots
        self.stage = 0

    def flying(self, stage):
        x, y, core, z = place_xy()
        peers = [device(x, y, 1 - core, z), device(1 - x, y, core, z), device(x, 1 - y, core, z)]
        moves = [(stage, peers[stage])] if stage < 3 else [(2 + k, device(x, y, core, (z + k) % 4)) for k in range(1, 4)]
        return [
            pltpu.make_async_remote_copy(
                src_ref=self.low.at[stage], dst_ref=self.got.at[n], send_sem=self.sends.at[n], recv_sem=self.gots.at[n],
                device_id=peer, device_id_type=MESH,
            )
            for n, peer in moves
        ]

    def step(self):
        z = place_xy()[3]
        if self.stage:
            for copy in self.flying(self.stage - 1):
                copy.wait()
        if self.stage == 0:
            total = self.values[...]
        elif self.stage < 4:
            total = self.low[self.stage - 1].astype(F32) + self.got[self.stage - 1].astype(F32)
        else:
            total = None
            for place in range(4):
                part = self.low[3].astype(F32)
                for k in range(1, 4):
                    part = jnp.where((z + 4 - k) % 4 == place, self.got[2 + k].astype(F32), part)
                total = part if total is None else total + part
            self.out[...] = total
            return True
        self.low[self.stage] = total.astype(self.low.dtype)
        for copy in self.flying(self.stage):
            copy.start()
        self.stage += 1
        return False


class Pipeline:
    def __init__(self):
        self.active, self.queue = [], []

    def add(self, *jobs):
        self.queue += jobs

    def tick(self, times=1):
        for _ in range(times):
            self.one_tick()

    def one_tick(self):
        left = []
        for entry in self.active:
            job = entry[0]
            entry[1] += 1
            due = not isinstance(job, Scatter) or entry[1] == LAGS[job.stage]
            if not (due and job.step()):
                left.append(entry)
        self.active = left
        if self.queue:
            job = self.queue.pop(0)
            job.step()
            self.active.append([job, 0])

    def drain(self):
        while self.active or self.queue:
            self.tick()

    def settle(self, jobs):
        while min(job.stage for job in jobs) < 2:
            self.tick()

    def save(self):
        return [list(entry) + [entry[0].stage] for entry in self.active], list(self.queue)

    def restore(self, state):
        self.active = [entry[:2] for entry in state[0]]
        for job, _, stage in state[0]:
            job.stage = stage
        self.queue = list(state[1])
        for job in self.queue:
            job.stage = 0


class Backward:
    def __init__(self, r):
        self.r = r
        self.pipe = Pipeline()
        self.counts = [0, 0]
        self.loads = 0

    def jobs(self, left, right, outs, parts):
        r = self.r
        made = []
        for rows_chip, begin, size, cut in parts:
            wide = rows_chip == 64
            rooms, depths = (r.wide, WIDE) if wide else (r.narrow, NARROW)
            n = self.counts[wide]
            m = sum(self.counts)
            self.counts[wide] += 1
            buffers = [buffer.at[n % depth] for buffer, depth in zip(rooms, depths)]
            if not wide:
                buffers[1], buffers[4], buffers[6] = buffers[2], buffers[3], buffers[5]
            made.append(Scatter(left, right, outs, rows_chip, begin, size, cut, buffers, r.sends.at[m], r.gots.at[m]))
        self.pipe.add(*made)
        return made

    def fetch(self, source, target):
        copy = pltpu.make_async_copy(source, target, self.r.load_sems.at[self.loads])
        copy.start()
        self.loads += 1
        return copy


def backward_kernel(r):
    piece, after, before = path_place()
    x, y, core, z = place_xy()
    signal_all(near_peers() + [after, before, partner()])
    keep = stream_place(r, piece, r.g.shape[0])
    mixed = pltpu.make_async_remote_copy(
        src_ref=r.mixed, dst_ref=r.mixed_out, send_sem=r.move_sems.at[0], recv_sem=r.move_sems.at[1],
        device_id=partner(), device_id_type=MESH,
    )
    stays = pltpu.make_async_copy(r.mixed, r.mixed_out, r.move_sems.at[2])

    @pl.when(x != core)
    def _():
        mixed.start()

    @pl.when(x == core)
    def _():
        stays.start()

    r.g_out[...] = r.g[...].astype(F32)
    shared = Backward(r)
    old = []
    for layer in reversed(range(LAYERS)):
        old = backward_block(layer, shared, keep, old, r)
    moved = pltpu.make_async_remote_copy(
        src_ref=r.g_low, dst_ref=r.g_got, send_sem=r.move_sems.at[3], recv_sem=r.move_sems.at[4],
        device_id=partner(), device_id_type=MESH,
    )

    @pl.when(x != core)
    def _():
        r.g_low[...] = r.g_out[...].astype(BF)
        moved.start()

    shared.pipe.drain()

    @pl.when(x == core)
    def _():
        stays.wait()

    @pl.when(x != core)
    def _():
        mixed.wait()
        moved.wait()
        r.g_out[...] = r.g_got[...].astype(F32)


def backward_block(layer, shared, keep, old, r):
    piece, after, before = path_place()
    saved, pipe, fetch = SimpleNamespace(**r.saved[layer]), shared.pipe, shared.fetch
    rows = r.g.shape[0]
    wb = r.smalls[8 * layer : 8 * layer + 8].astype(BF)
    mix = r.smalls[16 + layer : 17 + layer]
    mlp = r.smalls[18 + layer : 19 + layer]
    taps = r.taps.at[layer]
    values, ds, halo_ref = r.values.at[layer], r.ds.at[layer], r.halo.at[layer]
    grads = {key: [ref.at[layer] for ref in refs] for key, refs in r.grads.items()}
    hid = fetch(saved.hid, r.v_hid)
    down = [fetch(saved.w_down.at[pl.ds(0, 2)], r.vdown)]
    gu = fetch(saved.gu, r.v_gu)
    big = [fetch(saved.w_gate_up.at[n], r.vbig.at[n]) for n in range(2)]
    r.dy2[...] = r.g_out[...].astype(BF)
    made = shared.jobs(r.v_hid, r.dy2, grads["down"], CHUNKS["down"])
    hid.wait()
    pipe.tick()
    h2, x1, o, eff, on = (
        fetch(a, b)
        for a, b in ((saved.h2, r.v_h2), (saved.x1, r.v_x), (saved.o, r.v_o), (saved.eff, r.v_eff), (saved.on, r.v_on))
    )

    def fetch_rows(source, n):
        return fetch(source.at[n], r.vbig.at[n % 2, :, :, :, pl.ds(0, source.shape[4])])

    ff = r.v_hid.shape[1]
    gu.wait()
    for n in range(2):
        down[n].wait()
        dhid_all = dot_t(r.dy2[...], r.vdown[...].reshape(ff // 2, D))
        if n == 0:
            down.append(fetch(saved.w_down.at[pl.ds(2, 2)], r.vdown))
        for begin, size in blocks(ff // 2, 384):
            start = n * (ff // 2) + begin
            dhid = dhid_all[:, begin : begin + size]
            gate = r.v_gu[:, start : start + size].astype(F32)
            up = r.v_gu[:, ff + start : ff + start + size].astype(F32)
            sig = jax.nn.sigmoid(gate)
            act = gate * sig
            r.v_gu[:, start : start + size] = (dhid * up * (sig + act * (1.0 - sig))).astype(BF)
            r.v_gu[:, ff + start : ff + start + size] = (dhid * act).astype(BF)
        pipe.tick()
    h2.wait()
    made += shared.jobs(r.v_h2, r.v_gu, grads["gate_up"], CHUNKS["gate_up"])
    for n in range(4):
        big[n].wait()
        r.acc[:, n * 256 : (n + 1) * 256] = dot_t(r.v_gu[...], r.vbig[n % 2].reshape(256, 2 * ff))
        big.append(fetch_rows(saved.w_gate_up if n < 2 else saved.w_out, (n + 2) % 4))
        if n % 2:
            pipe.tick()
    x1.wait()
    back, part = rms_back(r.v_x[...], mlp, r.acc[...])
    values[9:10] = jnp.sum(part, axis=0, keepdims=True)
    r.dx1[...] = r.g_out[...] + back
    r.dy1[...] = r.dx1[...].astype(BF)
    later = [
        fetch(a, b)
        for a, b in (
            (saved.sin, r.v_sin), (saved.a, r.v_a), (saved.beta, r.v_beta), (saved.before, r.v_before),
            (saved.proj, r.v_proj), (saved.inv, r.v_inv), (saved.st, r.v_st),
            (saved.x, r.v_x if layer else r.g_low),
        )
    ]
    on.wait()
    made += shared.jobs(r.v_on, r.dy1, grads["out"], CHUNKS["out"])
    for n in range(4):
        big[4 + n].wait()
        r.acc[:, n * 256 : (n + 1) * 256] = dot_t(r.dy1[...], r.vbig[n % 2, :, :, :, :D].reshape(256, D))
        big.append(fetch_rows(saved.w_out if n < 2 else saved.w_qkv, (n + 2) % 4))
    pipe.tick()
    o.wait()
    eff.wait()
    gain = r.head[layer].astype(F32)
    dgain = jnp.zeros((1, HEAD_DIM), F32)
    for head in range(HEADS):
        s = slice(head * HEAD_DIM, (head + 1) * HEAD_DIM)
        back, part = rms_back(r.v_o[:, s], gain, r.acc[:, s])
        dgain = dgain + jnp.sum(part, axis=0, keepdims=True)
        low = back.astype(BF)
        r.do[:, s] = low
        r.ds0[head] = t_dot(r.v_eff[:, s], low)
    values[16:32] = jnp.zeros((16, D), F32)
    tiny = r.tiny.at[layer]
    tiny[...] = jnp.zeros_like(tiny)
    tiny[0:1, HEAD_DIM : 2 * HEAD_DIM] = dgain
    for copy in later:
        copy.wait()
    pipe.tick()
    links = [
        pltpu.make_async_remote_copy(
            src_ref=r.next.at[pl.ds(2 * n, 2)], dst_ref=ds.at[pl.ds(2 * n, 2)],
            send_sem=r.chain_sends.at[layer, n], recv_sem=r.chain_gots.at[layer, n],
            device_id=before, device_id_type=MESH,
        )
        for n in range(4)
    ]

    @pl.when(piece == 7)
    def _():
        ds[...] = jnp.zeros_like(ds)

    def pass_on():
        for n, link in enumerate(links):

            @pl.when(piece < 7)
            def _():
                link.wait_recv()

            for head in (2 * n, 2 * n + 1):
                high, low = two_parts(r.v_a[head])
                part = ds[head]
                r.next[head] = (r.ds0[head] + part.astype(F32) + (t_dot(high, part) + t_dot(low, part))).astype(BF)

            @pl.when(piece > 0)
            def _():
                link.start()

    around(pipe, 2, piece < 4, pass_on)
    if old:
        pipe.settle(old)
    own = fetch(saved.h, r.v_h)
    r.dlogit[...] = jnp.zeros_like(r.dlogit)
    for head in range(0, HEADS, 2):
        back_heads(
            [head, head + 1], keep, r.pos, r.v_beta, r.v_proj, r.v_before, taps, r.v_inv, r.v_st,
            r.v_sin, ds, r.do, r.dproj, r.tail, r.edge, r.dtaps, r.dlogit,
        )
        pipe.tick(2)
    halo = pltpu.make_async_remote_copy(
        src_ref=r.edge, dst_ref=halo_ref, send_sem=r.halo_sems.at[0, layer], recv_sem=r.halo_sems.at[1, layer],
        device_id=before, device_id_type=MESH,
    )

    @pl.when(piece > 0)
    def _():
        halo.start()

    dlogit = r.dlogit[...]
    low = dlogit.astype(BF)
    own.wait()
    values[0:8] = t_dot(low, r.v_h[...])
    tiny[0:1, 0:HEADS] = jnp.sum(dlogit, axis=0, keepdims=True)
    for tap in range(CONV):
        for third in range(3):
            row = 10 + tap * 3 + third
            values[row : row + 1] = r.dtaps[tap : tap + 1, third * D : (third + 1) * D]

    @pl.when(piece == 7)
    def _():
        halo_ref[...] = jnp.zeros_like(halo_ref)

    @pl.when(piece < 7)
    def _():
        halo.wait_recv()

    r.dproj[rows - 16 :] = (r.tail[...] + halo_ref[...].astype(F32)).astype(BF)
    mine = shared.jobs(r.v_h, r.dproj, grads["qkv"], CHUNKS["qkv"])
    pipe.tick()
    for n in range(4):
        big[8 + n].wait()
        r.acc[:, n * 256 : (n + 1) * 256] = dot_t(
            r.dproj[...], r.vbig[n % 2, :, :, :, : 3 * D].reshape(256, 3 * D)
        ) + dot(low, wb[:, n * 256 : (n + 1) * 256])
        if n < 2:
            big.append(fetch_rows(saved.w_qkv, n + 2))
        if n % 2:
            pipe.tick()
    x_in = r.v_x[...] if layer else r.g_low[...].astype(F32)
    back, part = rms_back(x_in, mix, r.acc[...])
    values[8:9] = jnp.sum(part, axis=0, keepdims=True)
    r.g_out[...] = r.dx1[...] + back
    pipe.add(
        SumAll(
            values, r.small.at[layer], r.small_low.at[layer], r.small_got.at[layer],
            r.small_sends.at[layer], r.small_gots.at[layer],
        ),
        SumAll(
            tiny, r.tiny_out.at[layer], r.tiny_low.at[layer], r.tiny_got.at[layer],
            r.tiny_sends.at[layer], r.tiny_gots.at[layer],
        ),
    )
    pipe.settle(made)

    @pl.when(piece > 0)
    def _():
        halo.wait_send()
        for link in links:
            link.wait_send()

    return mine


WIDE = (2, 4, 6, 4, 4, 4, 4, 4, 1, 1)
NARROW = (2, 1, 4, 4, 1, 4, 1, 4, 1, 1)


def rooms(depths, rows, size):
    half = (size // 128 + 1) // 2 * 128
    dims = (
        (4, 2, 2, rows, size), (4, 2, 2, rows, size), (4, 2, 2, rows, size), (4, 2, rows, half), (4, 2, rows, half),
        (4, rows, half), (4, rows, half), (3, rows, size), (rows // 2, size),
        (rows // 2, size),
    )
    return [pltpu.VMEM((depth,) + d, F32 if n >= 8 else BF) for n, (depth, d) in enumerate(zip(depths, dims))]


def backward_call(g, saved, small, mixed, lengths, head):
    rows = g.shape[0]
    count = rows // STRETCH
    ff2 = saved[0]["gu"].shape[1]
    whole, anywhere = pl.BlockSpec(memory_space=pltpu.VMEM), pl.BlockSpec(memory_space=pl.ANY)
    vmem = dict(head=head, g=g, smalls=small[0], taps=small[1])
    keys = [key for key in saved[0]]
    hbm = [layer[key] for layer in saved for key in keys]
    outs = dict(small=((LAYERS, 32, D), F32), tiny_out=((LAYERS, 8, 256), F32), g_out=((rows, D), F32))
    far = [
        ((rows, D), BF), ((LAYERS, 32, 3 * D), F32), ((LAYERS, 32, D), F32), ((LAYERS, 32, ff2 // 2), F32),
        ((LAYERS, 32, ff2 // 2), F32), ((LAYERS, 88, D), F32),
    ]
    v = pltpu.VMEM
    scratch = dict(
        v_gu=v((rows, ff2), BF), v_x=v((rows, D), F32), v_hid=v((rows, ff2 // 2), BF), v_h2=v((rows, D), BF),
        v_o=v((rows, D), F32), v_eff=v((rows, D), BF), v_on=v((rows, D), BF), v_proj=v((rows, 3 * D), F32),
        v_inv=v((HEADS, rows, rows), BF), v_st=v((HEADS, count, HEAD_DIM, 2 * HEAD_DIM), BF),
        v_sin=v((HEADS, HEAD_DIM, HEAD_DIM), F32), v_a=v((HEADS, HEAD_DIM, HEAD_DIM), F32), v_h=v((rows, D), BF),
        v_beta=v((rows, HEADS), F32), v_before=v((16, 3 * D), BF),
        acc=v((rows, D), F32), dy2=v((rows, D), BF), dy1=v((rows, D), BF), dx1=v((rows, D), F32), do=v((rows, D), BF),
        ds=v((LAYERS, HEADS, HEAD_DIM, HEAD_DIM), BF), next=v((HEADS, HEAD_DIM, HEAD_DIM), BF),
        ds0=v((HEADS, HEAD_DIM, HEAD_DIM), F32), tail=v((16, 3 * D), F32), edge=v((16, 3 * D), BF),
        halo=v((LAYERS, 16, 3 * D), BF), dtaps=v((CONV, 3 * D), F32), dlogit=v((rows, HEADS), F32),
        values=v((LAYERS, 32, D), F32), small_low=v((LAYERS, 4, 32, D), BF), small_got=v((LAYERS, 6, 32, D), BF),
        tiny=v((LAYERS, 8, 256), F32), tiny_low=v((LAYERS, 4, 8, 256), F32), tiny_got=v((LAYERS, 6, 8, 256), F32),
        tiny_sends=dma(LAYERS, 6), tiny_gots=dma(LAYERS, 6),
        vdown=v((2, 2, 2, 176, D), BF), vbig=v((2, 2, 2, 64, ff2), BF), dproj=v((rows, 3 * D), BF),
        g_low=v((rows, D), BF), g_got=v((rows, D), BF), pos=v((rows, 1), jnp.int32),
        sends=dma(36, 10), gots=dma(36, 10), small_sends=dma(LAYERS, 6), small_gots=dma(LAYERS, 6), load_sems=dma(80),
        halo_sems=dma(2, LAYERS), chain_sends=dma(LAYERS, 4), chain_gots=dma(LAYERS, 4), move_sems=dma(5),
    )
    wide, narrow = rooms(WIDE, 64, 384), rooms(NARROW, 176, 128)

    def run(*refs):
        refs = list(refs)

        def take(count):
            taken = refs[:count]
            del refs[:count]
            return taken

        r = dict(lengths=take(1)[0], **dict(zip(vmem, take(len(vmem)))))
        kept = [dict(zip(keys, take(len(keys)))) for _ in saved]
        r["mixed"] = take(1)[0]
        r.update(zip(outs, take(len(outs))))
        r["mixed_out"], qkv, out, gate, up, down = take(len(far))
        r.update(zip(scratch, take(len(scratch))))
        r["wide"], r["narrow"] = take(len(wide)), take(len(narrow))
        r["grads"] = dict(qkv=[qkv], out=[out], gate_up=[gate, up], down=[down])
        backward_kernel(SimpleNamespace(saved=kept, **r))

    return pl.pallas_call(
        run,
        in_specs=[pl.BlockSpec(memory_space=pltpu.SMEM)] + [whole] * len(vmem) + [anywhere] * (len(hbm) + 1),
        out_specs=[whole] * len(outs) + [anywhere] * len(far),
        out_shape=[jax.ShapeDtypeStruct(*d) for d in list(outs.values()) + far],
        scratch_shapes=list(scratch.values()) + wide + narrow,
        compiler_params=pltpu.CompilerParams(
            collective_id=2, has_side_effects=True, vmem_limit_bytes=BACK_BYTES
        ),
        name="backward",
    )(lengths, *vmem.values(), *hbm, mixed)


def shape(dims, dtype):
    return jax.ShapeDtypeStruct(dims, dtype)


def forward(x, w, bias, head_gain, pos, keep):
    rows = x.shape[0]
    metas = {name: w[name][0] for name in ("qkv", "out", "gate_up", "down")}
    width, ff2 = metas["qkv"][2], metas["gate_up"][2]
    h, proj, beta, edge = weight_call(
        qkv_kernel, [metas["qkv"]], [w["qkv"][1]], (x, w["mix"][None], w["beta"], bias),
        [shape((rows, D), BF), shape((rows, width), F32), shape((rows, HEADS), F32), shape((16, width), BF)],
        [], "norm_qkv", 2 * rows * D * width,
    )
    before = shift(edge, 1)
    o, eff, tot, inv, st = local_call(keep, pos, beta, proj, before, w["conv"])
    sin = chain(tot[:, :, :HEAD_DIM], tot[:, :, HEAD_DIM:], 1)
    o, on, x1, h2 = weight_call(
        out_kernel, [metas["out"]], [w["out"][1]], (o, eff, sin, head_gain, x, w["mlp"][None]),
        [shape((rows, D), F32), shape((rows, D), BF), shape((rows, D), F32), shape((rows, D), BF)],
        [], "head_out", 2 * rows * D * D,
    )
    gu, hid, x2 = weight_call(
        mlp_kernel, [metas["gate_up"], metas["down"]], [w["gate_up"][1], w["down"][1]], (h2, x1),
        [shape((rows, ff2), F32), shape((rows, ff2 // 2), BF), shape((rows, D), F32)],
        [], "mlp", 3 * rows * D * ff2,
    )
    kept = dict(
        x=x, h=h, proj=proj, before=before, beta=beta, o=o, eff=eff, a=tot[:, :, HEAD_DIM:],
        inv=inv, st=st, sin=sin, head_gain=head_gain, on=on, x1=x1, h2=h2, gu=gu, hid=hid, w=w,
    )
    return x2, kept


def backward(g, kept, pos, keep):
    w = kept["w"]
    rows = g.shape[0]
    metas = {name: w[name][0] for name in ("qkv", "out", "gate_up", "down")}
    width, ff2 = metas["qkv"][2], metas["gate_up"][2]
    d_down = scatter(kept["hid"], g.astype(BF))
    dgu, dx1, dy1, d_mlp, do, ds0, d_head = weight_call(
        mlp_back_kernel,
        [metas["down"], metas["gate_up"], metas["out"]],
        [w["down"][1], w["gate_up"][1], w["out"][1]],
        (g, kept["gu"], kept["x1"], w["mlp"][None], kept["o"], kept["eff"], kept["head_gain"]),
        [
            shape((rows, ff2), BF), shape((rows, D), F32), shape((rows, D), BF), shape((1, D), F32),
            shape((rows, D), BF), shape((HEADS, HEAD_DIM, HEAD_DIM), F32), shape((1, HEAD_DIM), F32),
        ],
        [pltpu.VMEM((rows, D), BF), pltpu.VMEM((rows, ff2 // 2), F32), pltpu.VMEM((rows, D), F32)],
        "mlp_back", 3 * rows * D * ff2,
    )
    d_gate_up = scatter(kept["h2"], dgu)
    d_out = scatter(kept["on"], dy1)
    ds = chain(ds0, jnp.swapaxes(kept["a"], 1, 2), -1)
    dproj, tail, dbefore, dtaps, dlogit = back_call(
        keep, pos, kept["beta"], kept["proj"], kept["before"], w["conv"],
        kept["inv"], kept["st"], kept["sin"], ds, do,
    )
    returned = shift(dbefore, -1)
    dproj, g, d_mix, d_beta, d_bias = weight_call(
        qkv_back_kernel, [metas["qkv"]], [w["qkv"][1]],
        (dproj, tail, returned, dlogit, w["beta"], kept["x"], w["mix"][None], dx1, kept["h"]),
        [
            shape((rows, width), BF), shape((rows, D), F32), shape((1, D), F32), shape((D, HEADS), F32),
            shape((1, HEADS), F32),
        ],
        [], "qkv_back", 2 * rows * D * width,
    )
    d_qkv = scatter(kept["h"], dproj)
    large = (d_qkv, d_out, d_gate_up, d_down)
    small = (dtaps, d_beta, d_bias[0], d_head[0], d_mix[0], d_mlp[0])
    return g, large, small


def fast_body(
    tokens, qkv_weight, conv_weight, beta_weight, beta_bias, head_gain, out_weight, mixer_gain, mlp_gain,
    gate_weight, up_weight, down_weight, lengths, cotangent,
):
    pairs = []
    for seq in range(8):
        for batch in range(4):
            z, x, y, core = seq // 2, seq % 2, batch // 2, batch % 2
            pairs.append((seq * 4 + batch, (z * 2 + core) * 4 + y * 2 + x))
    lengths = lax.ppermute(lengths, BOTH, pairs)
    conv = jnp.pad(conv_weight.reshape(LAYERS * CONV, -1), ((0, 8), (0, 32)))
    columns_of = jnp.concatenate([beta_weight[0], beta_weight[1], mixer_gain.T, mlp_gain.T], axis=1)
    packed = jnp.concatenate([conv, jnp.pad(columns_of, ((0, 0), (0, 128 - columns_of.shape[1])))], axis=0)
    bias, head = beta_bias[:, None], head_gain[:, None]
    shards = dict(qkv=(qkv_weight,), out=(out_weight,), gate_up=(gate_weight, up_weight), down=(down_weight,))
    saved, small, mixed, cotangent = forward_call(tokens[0], cotangent[0], packed, lengths, bias, head, shards)
    tiny, least, g, mixed, *large = backward_call(cotangent, saved, small, mixed, lengths, head)
    place = lax.axis_index("seq") * lax.axis_size("batch") + lax.axis_index("batch")

    def own(values, axis):
        return lax.dynamic_slice_in_dim(values, place * (values.shape[axis] // 32), values.shape[axis] // 32, axis)

    beta = jnp.swapaxes(own(tiny[:, 0:8], 2), 1, 2)
    return (
        mixed[None], g[None], large[0], own(tiny[:, 10:22].reshape(LAYERS, CONV, -1), 2),
        beta, least[:, 0, :HEADS], least[:, 0, HEAD_DIM : 2 * HEAD_DIM], large[1], own(tiny[:, 8], 1),
        own(tiny[:, 9], 1), large[2], large[3], large[4],
    )


def general_body(
    tokens, qkv_weight, conv_weight, beta_weight, beta_bias, head_gain, out_weight, mixer_gain, mlp_gain,
    gate_weight, up_weight, down_weight, lengths, cotangent,
):
    rows = tokens.shape[1]
    tokens, cotangent = tokens[0], cotangent[0]
    index = lax.axis_index("seq") * rows + jnp.arange(rows, dtype=jnp.int32)
    seq_lengths = lengths[0]
    starts = jnp.cumsum(seq_lengths) - seq_lengths
    begin = jnp.max(jnp.where(starts[None, :] <= index[:, None], starts[None, :], 0), axis=1)
    positions = (index - begin).astype(jnp.int32)
    keep = (positions[::STRETCH] != 0).astype(F32)
    pos = positions[:, None]
    x = tokens.astype(F32)
    saved = []
    weights = gather_weights(
        qkv_weight, conv_weight, beta_weight, out_weight, mixer_gain, mlp_gain, gate_weight, up_weight, down_weight
    )
    for n in range(LAYERS):
        x, kept = forward(x, weights[n], beta_bias[n].astype(F32)[None], head_gain[n][None], pos, keep)
        saved.append(kept)
    mixed = x.astype(BF)
    g = cotangent.astype(F32)
    large = [None] * LAYERS
    small = [None] * LAYERS
    place = lax.axis_index("seq") * lax.axis_size("batch") + lax.axis_index("batch")
    for n in reversed(range(LAYERS)):
        g, large[n], parts = backward(g, saved[n], pos, keep)
        sizes = [p.size for p in parts]
        flat = lax.psum(jnp.concatenate([p.reshape(-1) for p in parts]), BOTH)
        pieces = []
        start = 0
        for p, size in zip(parts, sizes):
            pieces.append(flat[start : start + size].reshape(p.shape))
            start += size
        small[n] = pieces

    def own(values, axis):
        size = values.shape[axis] // (lax.axis_size("seq") * lax.axis_size("batch"))
        return lax.dynamic_slice_in_dim(values, place * size, size, axis)

    big = [jnp.stack([layer[m] for layer in large]) for m in range(4)]
    ff = big[2].shape[2] // 2
    big[2:3] = [big[2][..., :ff], big[2][..., ff:]]
    tiny = [jnp.stack([small[n][m] for n in range(LAYERS)]) for m in range(6)]
    return (
        mixed[None], g[None], big[0], own(tiny[0], 2), own(tiny[1], 1), tiny[2], tiny[3], big[1],
        own(tiny[4], 1), own(tiny[5], 1), big[2], big[3], big[4],
    )


def solution(mesh):
    rows = P(None, BOTH, None)
    vector = P(None, BOTH)
    cols = P(None, None, BOTH)
    stream = P("batch", "seq", None)
    return jax.shard_map(
        fast_body if (mesh.shape["seq"], mesh.shape["batch"]) == (8, 4) else general_body,
        mesh=mesh,
        in_specs=(
            stream, rows, cols, rows, P(), P(), rows, vector, vector, rows, rows, rows, P("batch", None), stream,
        ),
        out_specs=(stream, stream, rows, cols, rows, P(), P(), rows, vector, vector, rows, rows, rows),
        check_vma=False,
    )
```
